32 devices in a mesh: dp: 8 (over z, y), tensor: 4 (over x, core).
Axes of the slice: x: 2, y: 2, z: 4, core: 2. Of those that a mesh axis runs over, the one named last changes fastest.
Arguments:
- layer_input: bfloat16 [4096, 2048], P(('dp', 'tensor')), may hold values from -6 to 6
- doc_lengths: int32 [8, 8], P('dp'), may hold values from 1 to 505, as said below
- w_query: bfloat16 [2048, 2048], P(None, 'tensor'), may hold values from -0.125 to 0.125
- w_key: bfloat16 [2048, 512], P(None, 'tensor'), may hold values from -0.125 to 0.125
- w_value: bfloat16 [2048, 512], P(None, 'tensor'), may hold values from -0.125 to 0.125
- w_out: bfloat16 [2048, 2048], P('tensor'), may hold values from -0.5 to 0.5
- w_gate: bfloat16 [2048, 8192], P(None, 'tensor'), may hold values from -0.125 to 0.125
- w_up: bfloat16 [2048, 8192], P(None, 'tensor'), may hold values from -0.125 to 0.125
- w_down: bfloat16 [8192, 2048], P('tensor'), may hold values from -0.0625 to 0.0625
- gain_attn: float32 [2048], replicated, may hold values from 0.1 to 1.9
- gain_ffn: float32 [2048], replicated, may hold values from 0.1 to 1.9
- gain_query: float32 [64], replicated, may hold values from 0.1 to 1.9
- gain_key: float32 [64], replicated, may hold values from 0.1 to 1.9
- out_grad: bfloat16 [4096, 2048], P(('dp', 'tensor')), may hold values from -6 to 6
Outputs:
- layer_out: bfloat16 [4096, 2048], P(('dp', 'tensor'))
- input_grad: bfloat16 [4096, 2048], P(('dp', 'tensor'))
- grad_query: float32 [2048, 2048], P('dp', 'tensor')
- grad_key: float32 [2048, 512], P('dp', 'tensor')
- grad_value: float32 [2048, 512], P('dp', 'tensor')
- grad_out: float32 [2048, 2048], P('tensor', 'dp')
- grad_gate: float32 [2048, 8192], P('dp', 'tensor')
- grad_up: float32 [2048, 8192], P('dp', 'tensor')
- grad_down: float32 [8192, 2048], P('tensor', 'dp')
- grad_gain_attn: float32 [2048], replicated
- grad_gain_ffn: float32 [2048], replicated
- grad_gain_query: float32 [64], replicated
- grad_gain_key: float32 [64], replicated
The draws below stay inside these ranges and needn't reach their ends.
Inputs may be any that keep to these rules, and one draw needn't show every extreme that they name: `doc_lengths`: each row's 8 lengths sum to 512. One document of each row, at a place that varies, is longer than 384; each other one has 1 to 16 tokens. In one row all other documents have 1 token.
All inputs are finite; a program needn't handle non-finite values.
Results may differ from the reference program's by a relative error of at most 0.025.
Values may be sent and summed in bfloat16 or wider, within the bound.
A program may use at most 192 MiB of HBM per device.

```python
import jax
import jax.numpy as jnp
from jax import lax

D = 2048
HEADS = 32
KV = 8
HEAD_DIM = 64
FF = 8192
TOK_DEV = 128
DOCS = 8
ROWS = 8
LENGTH = 512
TOKENS = 4096


def draw_doc_lengths(key, part):
    key = jax.random.fold_in(key, 11)
    short_key, place_key, row_key = jax.random.split(key, 3)
    short_docs = jax.random.randint(short_key, (ROWS, DOCS), 1, TOK_DEV // DOCS + 1, dtype=jnp.int32)
    unit_row = jax.random.randint(row_key, (), 0, ROWS, dtype=jnp.int32)
    is_unit_row = jnp.arange(ROWS, dtype=jnp.int32)[:, None] == unit_row
    short_docs = jnp.where(is_unit_row, 1, short_docs).astype(jnp.int32)
    long_place = jax.random.randint(place_key, (ROWS, 1), 0, DOCS, dtype=jnp.int32)
    is_long = jnp.arange(DOCS, dtype=jnp.int32)[None, :] == long_place
    others = jnp.sum(jnp.where(is_long, 0, short_docs), axis=1, keepdims=True).astype(jnp.int32)
    return jnp.where(is_long, LENGTH - others, short_docs).astype(jnp.int32)


def levels(own_key, extent, pieces, least, largest):
    def one(axis_at, blocks):
        steps = jax.random.uniform(jax.random.fold_in(jax.random.fold_in(own_key, 6), axis_at), (blocks,), jnp.float32, least / len(pieces), largest / len(pieces))
        return jnp.repeat(jnp.exp(steps), extent[axis_at] // blocks).reshape((-1,) + (1,) * (len(extent) - axis_at - 1))

    gain = one(*pieces[0])
    for cut in pieces[1:]:
        gain = gain * one(*cut)
    return gain


def normal_values(key, extent, deviation, most, pieces=(), held_as=jnp.bfloat16):
    values = deviation * jax.random.normal(key, extent, jnp.float32)
    if pieces:
        values = values * levels(key, extent, pieces, -0.22, 0.18)
    return jnp.clip(values, -most, most).astype(held_as)


def setup_inputs(seed: int = 0) -> dict:
    arg_keys = jax.random.split(jax.random.key(seed), 15)
    return {
        "layer_input": normal_values(arg_keys[0], (TOKENS, D), 1.0, 6.0, ((0, 32),)),
        "doc_lengths": draw_doc_lengths(jax.random.fold_in(arg_keys[14], 71), 0),
        "w_query": normal_values(arg_keys[2], (D, HEADS * HEAD_DIM), D ** -0.5, 0.125, ((1, 4),)),
        "w_key": normal_values(arg_keys[3], (D, KV * HEAD_DIM), D ** -0.5, 0.125, ((1, 4),)),
        "w_value": normal_values(arg_keys[4], (D, KV * HEAD_DIM), D ** -0.5, 0.125, ((1, 4),)),
        "w_out": normal_values(arg_keys[5], (HEADS * HEAD_DIM, D), (HEADS * HEAD_DIM // 16) ** -0.5, 0.5, ((0, 4),)),
        "w_gate": normal_values(arg_keys[6], (D, FF), D ** -0.5, 0.125, ((1, 4),)),
        "w_up": normal_values(arg_keys[7], (D, FF), D ** -0.5, 0.125, ((1, 4),)),
        "w_down": normal_values(arg_keys[8], (FF, D), FF ** -0.5, 0.0625, ((0, 4),)),
        "gain_attn": jnp.clip(1.0 + 0.18 * jax.random.normal(arg_keys[9], (D,), jnp.float32), 0.1, 1.9),
        "gain_ffn": jnp.clip(1.0 + 0.18 * jax.random.normal(arg_keys[10], (D,), jnp.float32), 0.1, 1.9),
        "gain_query": jnp.clip(1.0 + 0.18 * jax.random.normal(arg_keys[11], (HEAD_DIM,), jnp.float32), 0.1, 1.9),
        "gain_key": jnp.clip(1.0 + 0.18 * jax.random.normal(arg_keys[12], (HEAD_DIM,), jnp.float32), 0.1, 1.9),
        "out_grad": normal_values(arg_keys[13], (TOKENS, D), 1.0, 6.0, ((0, 32),)),
    }


EPSILON = 1e-06
ROPE_BASE = 10000.0
MASKED = -1e+30
HIGHEST = lax.Precision.HIGHEST

@jax.custom_vjp
def low(v):
    return lax.optimization_barrier(v.astype(jnp.bfloat16)).astype(jnp.float32)

@jax.custom_vjp
def low_back(v):
    return v

def low_keep(v):
    return (low(v), None)

def low_pass(kept, grad):
    return (grad,)

def back_keep(v):
    return (v, None)

def back_low(kept, grad):
    return (low(grad),)
low.defvjp(low_keep, low_pass)
low_back.defvjp(back_keep, back_low)

def norm_gain(row_block, gain_vec):
    factor = lax.rsqrt(lax.optimization_barrier(jnp.mean(row_block * row_block, axis=-1, keepdims=True)) + EPSILON)
    return row_block * factor * gain_vec

def rotate(vector, cosine, sine_table):
    half_width = vector.shape[-1] // 2
    first = vector[..., :half_width]
    second = vector[..., half_width:]
    return jnp.concatenate([first * cosine - second * sine_table, second * cosine + first * sine_table], axis=-1)

def head_prep(raw_proj, gain_vec, cosine, sine_table):
    head_width = gain_vec.shape[0]
    per_head = raw_proj.reshape(raw_proj.shape[0], raw_proj.shape[1] // head_width, head_width)
    return rotate(norm_gain(per_head, gain_vec), cosine[:, None, :], sine_table[:, None, :])

def doc_layout(lengths, length):
    doc_ends = jnp.cumsum(lengths.astype(jnp.int32)).astype(jnp.int32)
    places = jnp.arange(length, dtype=jnp.int32)
    passed_end = (places[:, None] >= doc_ends[None, :]).astype(jnp.int32)
    doc_ids = lax.optimization_barrier(jnp.sum(passed_end, axis=1)).astype(jnp.int32)
    starts = lax.optimization_barrier(jnp.sum(passed_end * lengths.astype(jnp.int32)[None, :], axis=1)).astype(jnp.int32)
    return (doc_ids, places, places - starts)

def rope_tables(offsets, head_width):
    frequency = ROPE_BASE ** (-jnp.arange(0, head_width, 2, dtype=jnp.float32) / head_width)
    angles = offsets.astype(jnp.float32)[:, None] * frequency[None, :]
    return (jnp.cos(angles), jnp.sin(angles))

def matmul_high(left_mat, right_mat):
    return jnp.dot(left_mat, right_mat, precision=HIGHEST)

def row_forward(row_input, lengths, params):
    w_query, w_key, w_value, w_out, w_gate, w_up, w_down, gain_attn, gain_ffn, gain_query, gain_key = params
    length = row_input.shape[0]
    doc_ids, places, offsets = doc_layout(lengths, length)
    cosine, sine_table = rope_tables(offsets, HEAD_DIM)
    attn_in = low(norm_gain(row_input, gain_attn))
    query_raw = low_back(matmul_high(attn_in, w_query))
    key_raw = low_back(low(matmul_high(attn_in, w_key)))
    value_raw = low_back(low(matmul_high(attn_in, w_value)))
    queries = low(head_prep(query_raw, gain_query, cosine, sine_table))
    key_rot = low(head_prep(key_raw, gain_key, cosine, sine_table))
    key_heads = jnp.repeat(key_rot, HEADS // KV, axis=1)
    value_heads = jnp.repeat(value_raw.reshape(length, KV, HEAD_DIM), HEADS // KV, axis=1)
    scores = low_back(jnp.einsum('qhd,khd->hqk', queries, key_heads, precision=HIGHEST) * HEAD_DIM ** (-0.5))
    allowed = (doc_ids[:, None] == doc_ids[None, :]) & (places[None, :] <= places[:, None])
    scores = jnp.where(allowed[None], scores, MASKED)
    weights = low(jax.nn.softmax(scores, axis=-1))
    attn_mixed = jnp.einsum('hqk,khd->qhd', weights, value_heads, precision=HIGHEST)
    attn_mixed = low_back(low(attn_mixed.reshape(length, HEADS * HEAD_DIM)))
    residual = row_input + low_back(matmul_high(attn_mixed, w_out))
    ffn_in = low(norm_gain(residual, gain_ffn))
    gate_proj = low_back(matmul_high(ffn_in, w_gate))
    up_proj = low_back(matmul_high(ffn_in, w_up))
    hidden = low(jax.nn.silu(gate_proj) * up_proj)
    return residual + low_back(matmul_high(hidden, w_down))

def reference(layer_input, doc_lengths, w_query, w_key, w_value, w_out, w_gate, w_up, w_down, gain_attn, gain_ffn, gain_query, gain_key, out_grad):
    params = tuple((weight_arg.astype(jnp.float32) for weight_arg in (w_query, w_key, w_value, w_out, w_gate, w_up, w_down, gain_attn, gain_ffn, gain_query, gain_key)))
    rows_in = layer_input.astype(jnp.float32).reshape(ROWS, LENGTH, D)

    def forward(rows_in, params):

        def row_step(row_pair):
            return row_forward(row_pair[0], row_pair[1], params)
        return lax.map(jax.checkpoint(row_step), (rows_in, doc_lengths))
    result, pull_back = jax.vjp(forward, rows_in, params)
    input_cot, param_cot = pull_back(out_grad.astype(jnp.float32).reshape(ROWS, LENGTH, D))
    return (result.reshape(TOKENS, D).astype(jnp.bfloat16), input_cot.reshape(TOKENS, D).astype(jnp.bfloat16), param_cot[0], param_cot[1], param_cot[2], param_cot[3], param_cot[4], param_cot[5], param_cot[6], param_cot[7], param_cot[8], param_cot[9], param_cot[10])
```

```python
import jax
import jax.numpy as jnp
from jax import lax
from jax.experimental import pallas as pl
from jax.experimental.pallas import tpu as pltpu
from jax.sharding import PartitionSpec as P

HEADS = 32
KV = 8


EPSILON = 1e-06
ROPE_BASE = 10000.0
MASKED = -1e30


def norm_gain(row_block, gain_vec):
    factor = lax.rsqrt(jnp.mean(row_block * row_block, axis=-1, keepdims=True) + EPSILON)
    return row_block * factor * gain_vec


def rotate(vector, cosine, sine_table):
    half_width = vector.shape[-1] // 2
    first = vector[..., :half_width]
    second = vector[..., half_width:]
    return jnp.concatenate(
        [first * cosine - second * sine_table, second * cosine + first * sine_table], axis=-1
    )


def head_prep(raw_proj, gain_vec, cosine, sine_table):
    head_width = gain_vec.shape[0]
    per_head = raw_proj.reshape(raw_proj.shape[0], raw_proj.shape[1] // head_width, head_width)
    return rotate(norm_gain(per_head, gain_vec), cosine[:, None, :], sine_table[:, None, :])


def doc_layout(lengths, length):
    doc_ends = jnp.cumsum(lengths)
    places = jnp.arange(length, dtype=jnp.int32)
    passed_end = (places[:, None] >= doc_ends[None, :]).astype(jnp.int32)
    doc_ids = jnp.sum(passed_end, axis=1)
    starts = jnp.sum(passed_end * lengths[None, :], axis=1)
    return (doc_ids, places, places - starts)


def rope_tables(offsets, head_width):
    frequency = ROPE_BASE ** (-jnp.arange(0, head_width, 2, dtype=jnp.float32) / head_width)
    angles = offsets.astype(jnp.float32)[:, None] * frequency[None, :]
    return (jnp.cos(angles), jnp.sin(angles))


def swiglu(gate_proj, up_proj):
    return jax.nn.silu(gate_proj) * up_proj


def matmul_nt(left_mat, right_mat):
    return lax.dot_general(
        left_mat, right_mat, (((1,), (1,)), ((), ())), preferred_element_type=jnp.float32
    )


def matmul_tn(left_mat, right_mat):
    return lax.dot_general(
        left_mat, right_mat, (((0,), (0,)), ((), ())), preferred_element_type=jnp.float32
    )


def per_device(
    layer_input,
    doc_lengths,
    w_query,
    w_key,
    w_value,
    w_out,
    w_gate,
    w_up,
    w_down,
    gain_attn,
    gain_ffn,
    gain_query,
    gain_key,
    out_grad,
):
    tok_rows = layer_input.shape[0]
    head_width = gain_query.shape[0]
    tensor_count = lax.axis_size("tensor")
    length = tok_rows * tensor_count
    per_dev = w_query.shape[1] // head_width
    groups_dev = w_key.shape[1] // head_width
    input_f32 = layer_input.astype(jnp.float32)
    doc_ids, places, offsets = doc_layout(doc_lengths[0], length)
    cosine, sine_table = rope_tables(offsets, head_width)
    attn_in = lax.all_gather(
        norm_gain(input_f32, gain_attn).astype(jnp.bfloat16), "tensor", axis=0, tiled=True
    )
    query_raw = jnp.dot(attn_in, w_query, preferred_element_type=jnp.float32)
    key_raw = jnp.dot(attn_in, w_key, preferred_element_type=jnp.float32).astype(jnp.bfloat16)
    value_raw = jnp.dot(attn_in, w_value, preferred_element_type=jnp.float32).astype(jnp.bfloat16)
    key_f32 = key_raw.astype(jnp.float32)
    queries = head_prep(query_raw, gain_query, cosine, sine_table).astype(jnp.bfloat16)
    key_rot = head_prep(key_f32, gain_key, cosine, sine_table).astype(jnp.bfloat16)
    local_heads = jnp.arange(per_dev, dtype=jnp.int32)
    group_pick = (
        local_heads[:, None] // (HEADS // KV) == jnp.arange(groups_dev, dtype=jnp.int32)[None, :]
    ).astype(jnp.float32)
    pick_low = group_pick.astype(jnp.bfloat16)
    key_heads = jnp.einsum(
        "lgd,hg->lhd", key_rot, pick_low, preferred_element_type=jnp.float32
    ).astype(jnp.bfloat16)
    value_heads = jnp.einsum(
        "lgd,hg->lhd",
        value_raw.reshape(length, groups_dev, head_width),
        pick_low,
        preferred_element_type=jnp.float32,
    ).astype(jnp.bfloat16)
    block_rows = min(512, length)
    block_count = length // block_rows
    score_scale = head_width ** (-0.5)

    def block_scores(block_num):
        row_begin = block_num * block_rows
        query_block = lax.dynamic_slice_in_dim(queries, row_begin, block_rows, 0)
        ids_block = lax.dynamic_slice_in_dim(doc_ids, row_begin, block_rows, 0)
        places_block = lax.dynamic_slice_in_dim(places, row_begin, block_rows, 0)
        scores = (
            jnp.einsum("qhd,khd->hqk", query_block, key_heads, preferred_element_type=jnp.float32)
            * score_scale
        )
        allowed = (ids_block[:, None] == doc_ids[None, :]) & (
            places[None, :] <= places_block[:, None]
        )
        return (query_block, jnp.where(allowed[None], scores, MASKED))

    def forward_block(block_num):
        query_block, scores = block_scores(block_num)
        row_top = jnp.max(scores, axis=-1, keepdims=True)
        exponent = jnp.exp(scores - row_top)
        row_total = jnp.sum(exponent, axis=-1, keepdims=True)
        probabilities = (exponent / row_total).astype(jnp.bfloat16)
        mixed_block = jnp.einsum(
            "hqk,khd->qhd", probabilities, value_heads, preferred_element_type=jnp.float32
        )
        return (mixed_block, row_top + jnp.log(row_total))

    mixed_all, log_totals = lax.map(forward_block, jnp.arange(block_count, dtype=jnp.int32))
    attn_mixed = mixed_all.reshape(length, per_dev * head_width).astype(jnp.bfloat16)
    residual = input_f32 + lax.psum_scatter(
        jnp.dot(attn_mixed, w_out, preferred_element_type=jnp.float32).astype(jnp.bfloat16),
        "tensor",
        scatter_dimension=0,
        tiled=True,
    ).astype(jnp.float32)
    ffn_in = lax.all_gather(
        norm_gain(residual, gain_ffn).astype(jnp.bfloat16), "tensor", axis=0, tiled=True
    )
    gate_proj = jnp.dot(ffn_in, w_gate, preferred_element_type=jnp.float32)
    up_proj = jnp.dot(ffn_in, w_up, preferred_element_type=jnp.float32)
    hidden = swiglu(gate_proj, up_proj).astype(jnp.bfloat16)
    layer_out = (
        residual
        + lax.psum_scatter(
            jnp.dot(hidden, w_down, preferred_element_type=jnp.float32).astype(jnp.bfloat16),
            "tensor",
            scatter_dimension=0,
            tiled=True,
        ).astype(jnp.float32)
    ).astype(jnp.bfloat16)
    grad_rows = lax.all_gather(out_grad, "tensor", axis=0, tiled=True)
    hidden_grad = matmul_nt(grad_rows, w_down)
    grad_down = matmul_tn(hidden, grad_rows)
    unused_value, swiglu_back = jax.vjp(swiglu, gate_proj, up_proj)
    gate_grad, up_grad = swiglu_back(hidden_grad)
    gate_grad = gate_grad.astype(jnp.bfloat16)
    up_grad = up_grad.astype(jnp.bfloat16)
    grad_gate = matmul_tn(ffn_in, gate_grad)
    grad_up = matmul_tn(ffn_in, up_grad)
    ffn_in_grad = lax.psum_scatter(
        (matmul_nt(gate_grad, w_gate) + matmul_nt(up_grad, w_up)).astype(jnp.bfloat16),
        "tensor",
        scatter_dimension=0,
        tiled=True,
    ).astype(jnp.float32)
    unused_norm, ffn_norm_back = jax.vjp(norm_gain, residual, gain_ffn)
    residual_grad, gain_ffn_grad = ffn_norm_back(ffn_in_grad)
    residual_grad = residual_grad + out_grad.astype(jnp.float32)
    res_low = lax.all_gather(residual_grad.astype(jnp.bfloat16), "tensor", axis=0, tiled=True)
    mixed_grad = matmul_nt(res_low, w_out).astype(jnp.bfloat16).reshape(length, per_dev, head_width)
    grad_out = matmul_tn(attn_mixed, res_low)

    def backward_block(running, block_num):
        key_acc, value_acc = running
        query_block, scores = block_scores(block_num)
        probabilities = jnp.exp(scores - log_totals[block_num])
        grad_block = lax.dynamic_slice_in_dim(mixed_grad, block_num * block_rows, block_rows, 0)
        prob_grad = jnp.einsum(
            "qhd,khd->hqk", grad_block, value_heads, preferred_element_type=jnp.float32
        )
        value_acc = value_acc + jnp.einsum(
            "hqk,qhd->khd",
            probabilities.astype(jnp.bfloat16),
            grad_block,
            preferred_element_type=jnp.float32,
        )
        centre = jnp.sum(probabilities * prob_grad, axis=-1, keepdims=True)
        score_grad = (probabilities * (prob_grad - centre)).astype(jnp.bfloat16)
        query_part = (
            jnp.einsum("hqk,khd->qhd", score_grad, key_heads, preferred_element_type=jnp.float32)
            * score_scale
        )
        key_acc = (
            key_acc
            + jnp.einsum(
                "hqk,qhd->khd", score_grad, query_block, preferred_element_type=jnp.float32
            )
            * score_scale
        )
        return ((key_acc, value_acc), query_part)

    zeros_init = jnp.zeros((length, per_dev, head_width), jnp.float32)
    (key_acc, value_acc), query_parts = lax.scan(
        backward_block, (zeros_init, zeros_init), jnp.arange(block_count, dtype=jnp.int32)
    )
    query_rot_grad = query_parts.reshape(length, per_dev, head_width)
    unused_query, query_back = jax.vjp(
        lambda raw_proj, gain_vec: head_prep(raw_proj, gain_vec, cosine, sine_table),
        query_raw,
        gain_query,
    )
    query_raw_grad, gain_query_grad = query_back(query_rot_grad)
    query_low = query_raw_grad.astype(jnp.bfloat16)
    key_group_grad = jnp.einsum("lhd,hg->lgd", key_acc, group_pick, precision=lax.Precision.HIGHEST)
    value_group_grad = jnp.einsum(
        "lhd,hg->lgd", value_acc, group_pick, precision=lax.Precision.HIGHEST
    )
    unused_key, key_back = jax.vjp(
        lambda raw_proj, gain_vec: head_prep(raw_proj, gain_vec, cosine, sine_table),
        key_f32,
        gain_key,
    )
    key_raw_grad, gain_key_grad = key_back(key_group_grad)
    key_low = key_raw_grad.astype(jnp.bfloat16)
    value_low = value_group_grad.reshape(length, groups_dev * head_width).astype(jnp.bfloat16)
    grad_query = matmul_tn(attn_in, query_low)
    grad_key = matmul_tn(attn_in, key_low)
    grad_value = matmul_tn(attn_in, value_low)
    attn_in_grad = lax.psum_scatter(
        (
            matmul_nt(query_low, w_query)
            + matmul_nt(key_low, w_key)
            + matmul_nt(value_low, w_value)
        ).astype(jnp.bfloat16),
        "tensor",
        scatter_dimension=0,
        tiled=True,
    ).astype(jnp.float32)
    unused_attn, attn_norm_back = jax.vjp(norm_gain, input_f32, gain_attn)
    input_part, gain_attn_grad = attn_norm_back(attn_in_grad)
    input_grad = (input_part + residual_grad).astype(jnp.bfloat16)
    reduced = (
        lax.psum_scatter(
            grad_query.astype(jnp.bfloat16), "dp", scatter_dimension=0, tiled=True
        ).astype(jnp.float32),
        lax.psum_scatter(
            grad_key.astype(jnp.bfloat16), "dp", scatter_dimension=0, tiled=True
        ).astype(jnp.float32),
        lax.psum_scatter(
            grad_value.astype(jnp.bfloat16), "dp", scatter_dimension=0, tiled=True
        ).astype(jnp.float32),
        lax.psum_scatter(
            grad_out.astype(jnp.bfloat16), "dp", scatter_dimension=1, tiled=True
        ).astype(jnp.float32),
        lax.psum_scatter(
            grad_gate.astype(jnp.bfloat16), "dp", scatter_dimension=0, tiled=True
        ).astype(jnp.float32),
        lax.psum_scatter(
            grad_up.astype(jnp.bfloat16), "dp", scatter_dimension=0, tiled=True
        ).astype(jnp.float32),
        lax.psum_scatter(
            grad_down.astype(jnp.bfloat16), "dp", scatter_dimension=1, tiled=True
        ).astype(jnp.float32),
    )
    gain_sums = lax.psum(
        (gain_attn_grad, gain_ffn_grad, gain_query_grad, gain_key_grad), ("dp", "tensor")
    )
    return (
        layer_out,
        input_grad,
        reduced[0],
        reduced[1],
        reduced[2],
        reduced[3],
        reduced[4],
        reduced[5],
        reduced[6],
        gain_sums[0],
        gain_sums[1],
        gain_sums[2],
        gain_sums[3],
    )


def dp_shape():
    total = lax.axis_size("dp")
    z_count = 4 if total % 4 == 0 else total
    return (z_count, total // z_count)


def dp_place():
    z_count, y_count = dp_shape()
    me = lax.axis_index("dp")
    return (me // y_count, me % y_count)


def own_slices(array, dim, index):
    z_count, y_count = dp_shape()
    shape = array.shape
    width = shape[dim] // (z_count * y_count)
    split = array.reshape(shape[:dim] + (z_count, y_count, width) + shape[dim + 1 :])
    part = lax.dynamic_index_in_dim(split, index, dim + 1, keepdims=False)
    return part.reshape(shape[:dim] + (z_count * width,) + shape[dim + 1 :])


def y_shift(array, distance):
    z_count, y_count = dp_shape()
    pairs = [
        (z * y_count + y, z * y_count + (y + distance) % y_count)
        for z in range(z_count)
        for y in range(y_count)
    ]
    return lax.ppermute(array, "dp", pairs)


def pair_product(left, right, dim):
    z_count, y_count = dp_shape()
    y_me = dp_place()[1]
    shared, full = (left, right) if dim == 0 else (right, left)
    total = None
    for distance in range(y_count):
        target = (y_me + distance) % y_count
        own = own_slices(shared, 1, target)
        rest = full
        if distance:
            own, rest = y_shift(own, distance), y_shift(full, distance)
        term = matmul_tn(own, rest) if dim == 0 else matmul_tn(rest, own)
        total = term if total is None else total + term
    return total.astype(jnp.bfloat16)


def pair_sum(left, right, dim):
    z_count, y_count = dp_shape()
    y_me = dp_place()[1]
    product = matmul_tn(left, right)
    total = own_slices(product, dim, y_me)
    for distance in range(1, y_count):
        part = own_slices(product, dim, (y_me + distance) % y_count).astype(jnp.bfloat16)
        total = total + y_shift(part, distance).astype(jnp.float32)
    return total.astype(jnp.bfloat16)


def line_reduce(partial, dim):
    z_count, y_count = dp_shape()
    z_me = dp_place()[0]
    shape = partial.shape
    blocks = partial.reshape(
        shape[:dim] + (z_count, shape[dim] // z_count) + shape[dim + 1 :]
    )

    def block(index):
        return lax.dynamic_index_in_dim(
            blocks, jnp.clip(index, 0, z_count - 1), dim, keepdims=False
        )

    def chain(step_of, place, block_of):
        arrived = None
        for step in range(z_count - 1):
            send = block(block_of(z_count - 1 - step + place(z_me)))
            if arrived is not None:
                send = (send.astype(jnp.float32) + arrived.astype(jnp.float32)).astype(
                    jnp.bfloat16
                )
            pairs = [
                (z * y_count + y, (z + step_of) * y_count + y)
                for z in range(z_count)
                for y in range(y_count)
                if place(z) <= step
            ]
            arrived = lax.ppermute(send, "dp", pairs)
        return arrived

    from_low = chain(1, lambda z: z, lambda index: index)
    from_high = chain(-1, lambda z: z_count - 1 - z, lambda index: z_count - 1 - index)
    return (
        block(z_me).astype(jnp.float32)
        + from_low.astype(jnp.float32)
        + from_high.astype(jnp.float32)
    )


def attention_forward(attn_in, doc_lengths, w_query, w_key, w_value, gain_query, gain_key):
    head_width = gain_query.shape[0]
    length = attn_in.shape[0]
    per_dev = w_query.shape[1] // head_width
    groups_dev = w_key.shape[1] // head_width
    doc_ids, places, offsets = doc_layout(doc_lengths[0], length)
    cosine, sine_table = rope_tables(offsets, head_width)
    query_raw = jnp.dot(attn_in, w_query, preferred_element_type=jnp.float32)
    key_raw = jnp.dot(attn_in, w_key, preferred_element_type=jnp.float32).astype(jnp.bfloat16)
    value_raw = jnp.dot(attn_in, w_value, preferred_element_type=jnp.float32).astype(jnp.bfloat16)
    key_f32 = key_raw.astype(jnp.float32)
    queries = head_prep(query_raw, gain_query, cosine, sine_table).astype(jnp.bfloat16)
    key_rot = head_prep(key_f32, gain_key, cosine, sine_table).astype(jnp.bfloat16)
    local_heads = jnp.arange(per_dev, dtype=jnp.int32)
    group_pick = (
        local_heads[:, None] // (HEADS // KV) == jnp.arange(groups_dev, dtype=jnp.int32)[None, :]
    ).astype(jnp.float32)
    pick_low = group_pick.astype(jnp.bfloat16)
    key_heads = jnp.einsum(
        "lgd,hg->lhd", key_rot, pick_low, preferred_element_type=jnp.float32
    ).astype(jnp.bfloat16)
    value_heads = jnp.einsum(
        "lgd,hg->lhd",
        value_raw.reshape(length, groups_dev, head_width),
        pick_low,
        preferred_element_type=jnp.float32,
    ).astype(jnp.bfloat16)
    block_rows = min(512, length)
    block_count = length // block_rows
    score_scale = head_width ** (-0.5)

    def block_scores(block_num):
        row_begin = block_num * block_rows
        query_block = lax.dynamic_slice_in_dim(queries, row_begin, block_rows, 0)
        ids_block = lax.dynamic_slice_in_dim(doc_ids, row_begin, block_rows, 0)
        places_block = lax.dynamic_slice_in_dim(places, row_begin, block_rows, 0)
        scores = (
            jnp.einsum("qhd,khd->hqk", query_block, key_heads, preferred_element_type=jnp.float32)
            * score_scale
        )
        allowed = (ids_block[:, None] == doc_ids[None, :]) & (
            places[None, :] <= places_block[:, None]
        )
        return (query_block, jnp.where(allowed[None], scores, MASKED))

    def forward_block(block_num):
        query_block, scores = block_scores(block_num)
        row_top = jnp.max(scores, axis=-1, keepdims=True)
        exponent = jnp.exp(scores - row_top)
        row_total = jnp.sum(exponent, axis=-1, keepdims=True)
        probabilities = (exponent / row_total).astype(jnp.bfloat16)
        mixed_block = jnp.einsum(
            "hqk,khd->qhd", probabilities, value_heads, preferred_element_type=jnp.float32
        )
        return (mixed_block, row_top + jnp.log(row_total))

    mixed_all, log_totals = lax.map(forward_block, jnp.arange(block_count, dtype=jnp.int32))
    attn_mixed = mixed_all.reshape(length, per_dev * head_width).astype(jnp.bfloat16)
    saved = (
        block_scores,
        log_totals,
        (key_heads, value_heads, queries),
        (query_raw, key_f32, cosine, sine_table, group_pick),
    )
    return (attn_mixed, saved)


def attention_backward(mixed_grad, saved, gain_query, gain_key):
    block_scores, log_totals, heads, rest = saved
    key_heads, value_heads, queries = heads
    query_raw, key_f32, cosine, sine_table, group_pick = rest
    length, per_dev, head_width = queries.shape
    groups_dev = group_pick.shape[1]
    block_rows = min(512, length)
    block_count = length // block_rows
    score_scale = head_width ** (-0.5)
    mixed_grad = mixed_grad.reshape(length, per_dev, head_width)

    def backward_block(running, block_num):
        key_acc, value_acc = running
        query_block, scores = block_scores(block_num)
        probabilities = jnp.exp(scores - log_totals[block_num])
        grad_block = lax.dynamic_slice_in_dim(mixed_grad, block_num * block_rows, block_rows, 0)
        prob_grad = jnp.einsum(
            "qhd,khd->hqk", grad_block, value_heads, preferred_element_type=jnp.float32
        )
        value_acc = value_acc + jnp.einsum(
            "hqk,qhd->khd",
            probabilities.astype(jnp.bfloat16),
            grad_block,
            preferred_element_type=jnp.float32,
        )
        centre = jnp.sum(probabilities * prob_grad, axis=-1, keepdims=True)
        score_grad = (probabilities * (prob_grad - centre)).astype(jnp.bfloat16)
        query_part = (
            jnp.einsum("hqk,khd->qhd", score_grad, key_heads, preferred_element_type=jnp.float32)
            * score_scale
        )
        key_acc = (
            key_acc
            + jnp.einsum(
                "hqk,qhd->khd", score_grad, query_block, preferred_element_type=jnp.float32
            )
            * score_scale
        )
        return ((key_acc, value_acc), query_part)

    zeros_init = jnp.zeros((length, per_dev, head_width), jnp.float32)
    (key_acc, value_acc), query_parts = lax.scan(
        backward_block, (zeros_init, zeros_init), jnp.arange(block_count, dtype=jnp.int32)
    )
    query_rot_grad = query_parts.reshape(length, per_dev, head_width)
    unused_query, query_back = jax.vjp(
        lambda raw_proj, gain_vec: head_prep(raw_proj, gain_vec, cosine, sine_table),
        query_raw,
        gain_query,
    )
    query_raw_grad, gain_query_grad = query_back(query_rot_grad)
    query_low = query_raw_grad.astype(jnp.bfloat16)
    key_group_grad = jnp.einsum("lhd,hg->lgd", key_acc, group_pick, precision=lax.Precision.HIGHEST)
    value_group_grad = jnp.einsum(
        "lhd,hg->lgd", value_acc, group_pick, precision=lax.Precision.HIGHEST
    )
    unused_key, key_back = jax.vjp(
        lambda raw_proj, gain_vec: head_prep(raw_proj, gain_vec, cosine, sine_table),
        key_f32,
        gain_key,
    )
    key_raw_grad, gain_key_grad = key_back(key_group_grad)
    key_low = key_raw_grad.astype(jnp.bfloat16)
    value_low = value_group_grad.reshape(length, groups_dev * head_width).astype(jnp.bfloat16)
    return (query_low, key_low, value_low, gain_query_grad, gain_key_grad)


MESH_ID = pl.DeviceIdType.MESH
ORDERS = (("x", "y", "z"), ("y", "z", "x"), ("z", "x", "y"))
LINKS = ("x", "y", "z", "core")
F32 = jnp.float32
BF16 = jnp.bfloat16


class Place:
    def __init__(self):
        row, column = lax.axis_index("dp"), lax.axis_index("tensor")
        self.far = row // 4
        self.at = {
            "z": (row // 2) % 2,
            "y": row % 2,
            "x": column // 2,
            "core": column % 2,
        }

    def flipped(self, names):
        return {
            name: 1 - value if name in names else value for name, value in self.at.items()
        }

    def device(self, name):
        at = self.flipped((name,))
        return {
            "dp": self.far * 4 + at["z"] * 2 + at["y"],
            "tensor": at["x"] * 2 + at["core"],
        }

    def column(self, names=()):
        at = self.flipped(names)
        return at["x"] * 2 + at["core"]

    def quarter(self):
        return self.at["z"] * 2 + self.at["y"]


def enter(place, names):
    barrier = pltpu.get_barrier_semaphore()
    for name in names:
        pl.semaphore_signal(
            barrier, inc=1, device_id=place.device(name), device_id_type=MESH_ID
        )
    pl.semaphore_wait(barrier, len(names))


class Sender:
    def __init__(self, place, send_sems, recv_sems):
        self.place, self.send_sems, self.recv_sems, self.used = place, send_sems, recv_sems, 0

    def copy(self, source, target, name):
        slot = self.used
        self.used += 1
        return pltpu.make_async_remote_copy(
            src_ref=source,
            dst_ref=target,
            send_sem=self.send_sems.at[slot],
            recv_sem=self.recv_sems.at[slot],
            device_id=self.place.device(name),
            device_id_type=MESH_ID,
        )


def part_rows(tokens):
    unit = tokens // 16
    first = -(-unit // 3)
    second = -(-(unit - first) // 2)
    return (first * 16, second * 16, (unit - first - second) * 16)


def part_starts(tokens):
    rows = part_rows(tokens)
    return (0, rows[0], rows[0] + rows[1])


def spot(tokens, part, half, core, index):
    rows, start = part_rows(tokens)[part], part_starts(tokens)[part]
    return half * 8 * tokens + 8 * start + core * 4 * rows + index * rows


def gather16(tokens, buffer, own, sender):
    links, cores = [], []
    for part, order in enumerate(ORDERS):
        rows, start = part_rows(tokens)[part], part_starts(tokens)[part]
        base = spot(tokens, part, 0, 0, 0)
        mine = own.at[pl.ds(start, rows)] if own is not None else buffer.at[pl.ds(base, rows)]
        pairs = (
            (mine, spot(tokens, part, 0, 0, 1), rows),
            (buffer.at[pl.ds(base, 2 * rows)], spot(tokens, part, 0, 0, 2), 2 * rows),
            (buffer.at[pl.ds(base, 4 * rows)], spot(tokens, part, 1, 0, 0), 4 * rows),
        )
        links.append(
            [
                sender.copy(source, buffer.at[pl.ds(target, count)], order[step])
                for step, (source, target, count) in enumerate(pairs)
            ]
        )
        moves = (
            (mine, 0, 0, rows),
            (None, 0, 1, rows),
            (None, 0, 2, 2 * rows),
            (None, 1, 0, 4 * rows),
        )
        cores.append(
            [
                sender.copy(
                    buffer.at[pl.ds(spot(tokens, part, half, 0, index), count)]
                    if source is None
                    else source,
                    buffer.at[pl.ds(spot(tokens, part, half, 1, index), count)],
                    "core",
                )
                for source, half, index, count in moves
            ]
        )
    return links, cores


def gather4(tokens, buffer, own, sender, place):
    mine = pl.ds(pl.multiple_of(place.column() * tokens, tokens), tokens)
    theirs = pl.ds(pl.multiple_of(place.column(("x",)) * tokens, tokens), tokens)
    return (
        sender.copy(own, buffer.at[mine], "x"),
        sender.copy(own, buffer.at[mine], "core"),
        sender.copy(buffer.at[theirs], buffer.at[theirs], "core"),
    )


def normed(values, gain):
    factor = lax.rsqrt(jnp.mean(values * values, axis=-1, keepdims=True) + EPSILON)
    return values * factor * gain


def norm_back(values, gain, grad):
    factor = lax.rsqrt(jnp.mean(values * values, axis=-1, keepdims=True) + EPSILON)
    unit = values * factor
    scaled = gain * grad
    back = factor * (scaled - unit * jnp.mean(scaled * unit, axis=-1, keepdims=True))
    return back, jnp.sum(grad * unit, axis=0, keepdims=True)


def start_kernel(
    input_ref, gain_ref, grad_ref, attn_ref, grad_all, own, send_sems, recv_sems, local_sems
):
    tokens = input_ref.shape[0]
    place = Place()
    enter(place, LINKS)
    sender = Sender(place, send_sems, recv_sems)
    links, cores = gather16(tokens, grad_all, grad_ref, sender)
    own[...] = normed(input_ref[...].astype(F32), gain_ref[...]).astype(BF16)
    row_copies = gather4(tokens, attn_ref, own, sender, place)
    row_copies[0].start()
    row_copies[1].start()
    keep = []
    for part in range(3):
        links[part][0].start()
        cores[part][0].start()
        rows, start = part_rows(tokens)[part], part_starts(tokens)[part]
        keep.append(
            pltpu.make_async_copy(
                grad_ref.at[pl.ds(start, rows)],
                grad_all.at[pl.ds(spot(tokens, part, 0, 0, 0), rows)],
                local_sems.at[part],
            )
        )
        keep[-1].start()
    mine = pl.ds(pl.multiple_of(place.column() * tokens, tokens), tokens)
    own_copy = pltpu.make_async_copy(own, attn_ref.at[mine], local_sems.at[3])
    own_copy.start()
    for copy in keep:
        copy.wait()
    for step in range(3):
        for part in range(3):
            links[part][step].wait_recv()
            if step < 2:
                links[part][step + 1].start()
            cores[part][step + 1].start()
        if step == 0:
            row_copies[0].wait_recv()
            row_copies[2].start()
    own_copy.wait()
    row_copies[1].wait_recv()
    row_copies[2].wait_recv()
    for copy in row_copies:
        copy.wait_send()
    for part in range(3):
        for copy in links[part]:
            copy.wait_send()
        for copy in cores[part]:
            copy.wait()


def scatter4(partial, from_core, from_x, tokens, sender, place):
    copies = []
    for names in (("x", "core"), ("core",)):
        shard = pl.ds(pl.multiple_of(place.column(names) * tokens, tokens), tokens)
        copies.append(
            sender.copy(partial.at[shard], from_core.at[len(copies)], "core")
        )
    return copies


def sum4(partial, from_core, outgoing, from_x, tokens, sender, place):
    copies = scatter4(partial, from_core, from_x, tokens, sender, place)
    for copy in copies:
        copy.start()
    far = pl.ds(pl.multiple_of(place.column(("x",)) * tokens, tokens), tokens)
    mine = pl.ds(pl.multiple_of(place.column() * tokens, tokens), tokens)
    copies[0].wait_recv()
    outgoing[...] = (partial[far, :].astype(F32) + from_core[0].astype(F32)).astype(BF16)
    along = sender.copy(outgoing, from_x, "x")
    along.start()
    copies[1].wait_recv()
    near = partial[mine, :].astype(F32) + from_core[1].astype(F32)
    along.wait_recv()
    total = near + from_x[...].astype(F32)
    for copy in copies:
        copy.wait_send()
    along.wait_send()
    return total


def silu_parts(gate, up, hidden_grad):
    s = 1.0 / (1.0 + jnp.exp(-gate))
    silu = gate * s
    hidden = silu * up
    gate_grad = hidden_grad * up * s * (1.0 + gate * (1.0 - s))
    return hidden, gate_grad, hidden_grad * silu


def ffn_kernel(
    partial_ref,
    input_ref,
    gain_ref,
    grad_all,
    gate_w,
    up_w,
    down_w,
    residual_ref,
    ffn_all,
    hidden_ref,
    pair_ref,
    rows_ref,
    from_core,
    outgoing,
    from_x,
    ffn_buf,
    grad_buf,
    gate_v,
    up_v,
    down_v,
    send_sems,
    recv_sems,
    local_sems,
):
    tokens = input_ref.shape[0]
    units = gate_v.shape[1]
    place = Place()
    columns = pl.ds(pl.multiple_of(place.quarter() * units, units), units)
    loads = [
        pltpu.make_async_copy(gate_w.at[:, columns], gate_v, local_sems.at[0]),
        pltpu.make_async_copy(up_w.at[:, columns], up_v, local_sems.at[1]),
        pltpu.make_async_copy(down_w.at[columns, :], down_v, local_sems.at[2]),
        pltpu.make_async_copy(grad_all, grad_buf, local_sems.at[3]),
    ]
    enter(place, LINKS)
    for copy in loads:
        copy.start()
    sender = Sender(place, send_sems, recv_sems)
    residual = input_ref[...].astype(F32) + sum4(
        partial_ref, from_core, outgoing, from_x, tokens, sender, place
    )
    residual_ref[...] = residual
    own = normed(residual, gain_ref[...]).astype(BF16)
    for part in range(3):
        rows, start = part_rows(tokens)[part], part_starts(tokens)[part]
        ffn_buf[pl.ds(spot(tokens, part, 0, 0, 0), rows), :] = own[start : start + rows]
    links, cores = gather16(tokens, ffn_buf, None, sender)
    for part in range(3):
        links[part][0].start()
        cores[part][0].start()
    for copy in loads:
        copy.wait()
    for step in range(2):
        for part in range(3):
            links[part][step].wait_recv()
            links[part][step + 1].start()
            cores[part][step + 1].start()
    for part in range(3):
        for copy in cores[part][:3]:
            copy.wait_recv()

    block = 2 * tokens

    def compute(index):
        rows = pl.ds(pl.multiple_of(index * block, block), block)
        values = ffn_buf[rows, :]
        gate = jnp.dot(values, gate_v[...], preferred_element_type=F32)
        up = jnp.dot(values, up_v[...], preferred_element_type=F32)
        hidden_grad = matmul_nt(grad_buf[rows, :], down_v[...])
        hidden, gate_grad, up_grad = silu_parts(gate, up, hidden_grad)
        hidden_ref[rows, :] = hidden.astype(BF16)
        pair_ref[rows, :units] = gate_grad.astype(BF16)
        pair_ref[rows, units:] = up_grad.astype(BF16)

    half = 8 * tokens
    first = pltpu.make_async_copy(
        ffn_buf.at[pl.ds(0, half)], ffn_all.at[pl.ds(0, half)], local_sems.at[4]
    )
    second = pltpu.make_async_copy(
        ffn_buf.at[pl.ds(half, half)], ffn_all.at[pl.ds(half, half)], local_sems.at[5]
    )
    first.start()
    pl.loop(0, 4)(compute)
    for part in range(3):
        links[part][2].wait_recv()
        cores[part][3].start()
    for part in range(3):
        cores[part][3].wait_recv()
    second.start()
    pl.loop(4, 8)(compute)
    for part, order in enumerate(ORDERS):
        rows, start = part_rows(tokens)[part], part_starts(tokens)[part]
        for half_bit in range(2):
            for core in range(2):
                for index in range(4):
                    bits = (index % 2, index // 2, half_bit)
                    flips = tuple(name for name, bit in zip(order, bits) if bit)
                    row = ("z" in flips) * 2 + ("y" in flips)
                    names = tuple(n for n in flips if n == "x") + (("core",) if core else ())
                    target = row * 4 * tokens + place.column(names) * tokens + start
                    rows_ref[pl.ds(pl.multiple_of(target, 16), rows), :] = hidden_ref[
                        pl.ds(spot(tokens, part, half_bit, core, index), rows), :
                    ]
    first.wait()
    second.wait()
    for part in range(3):
        for copy in links[part] + cores[part]:
            copy.wait_send()


def back_kernel(
    pair_ref,
    gate_w,
    up_w,
    residual_ref,
    gain_ref,
    grad_ref,
    back_ref,
    gain_back_ref,
    low_all,
    weights,
    products,
    from_core,
    third,
    second,
    first,
    own,
    send_sems,
    recv_sems,
    local_sems,
):
    tokens = residual_ref.shape[0]
    units = pair_ref.shape[1] // 2
    place = Place()
    columns = pl.ds(pl.multiple_of(place.quarter() * units, units), units)
    loads = [
        pltpu.make_async_copy(
            gate_w.at[:, columns], weights.at[:, pl.ds(0, units)], local_sems.at[0]
        ),
        pltpu.make_async_copy(
            up_w.at[:, columns], weights.at[:, pl.ds(units, units)], local_sems.at[1]
        ),
    ]
    enter(place, LINKS)
    for copy in loads:
        copy.start()
    sender = Sender(place, send_sems, recv_sems)
    part_list = [
        (part, part_rows(tokens)[part], part_starts(tokens)[part]) for part in range(3)
    ]

    def place_of(part, half, core, index, count):
        return pl.ds(spot(tokens, part, half, core, index), count)

    to_core = [
        [
            sender.copy(
                products.at[place_of(part, half, 1, 0, 4 * rows)],
                from_core.at[pl.ds(half * 4 * tokens + 4 * start, 4 * rows)],
                "core",
            )
            for part, rows, start in part_list
        ]
        for half in range(2)
    ]
    far = [
        sender.copy(
            products.at[place_of(part, 1, 0, 0, 4 * rows)],
            third.at[pl.ds(4 * start, 4 * rows)],
            ORDERS[part][2],
        )
        for part, rows, start in part_list
    ]
    middle = [
        sender.copy(
            products.at[place_of(part, 0, 0, 2, 2 * rows)],
            second.at[pl.ds(2 * start, 2 * rows)],
            ORDERS[part][1],
        )
        for part, rows, start in part_list
    ]
    close = [
        sender.copy(
            products.at[place_of(part, 0, 0, 1, rows)],
            first.at[pl.ds(start, rows)],
            ORDERS[part][0],
        )
        for part, rows, start in part_list
    ]
    for copy in loads:
        copy.wait()
    block = 2 * tokens

    def compute(index):
        rows = pl.ds(pl.multiple_of(index * block, block), block)
        products[rows, :] = matmul_nt(pair_ref[rows, :], weights[...]).astype(BF16)

    def add_in(rows, arrived):
        products[rows, :] = (
            products[rows, :].astype(F32) + arrived.astype(F32)
        ).astype(BF16)

    pl.loop(4, 8)(compute)
    for copy in to_core[1]:
        copy.start()
    pl.loop(0, 2)(compute)
    for part, rows, start in part_list:
        to_core[1][part].wait_recv()
        add_in(
            place_of(part, 1, 0, 0, 4 * rows),
            from_core[pl.ds(4 * tokens + 4 * start, 4 * rows), :],
        )
        far[part].start()
    pl.loop(2, 4)(compute)
    for copy in to_core[0]:
        copy.start()
    for part, rows, start in part_list:
        to_core[0][part].wait_recv()
        add_in(
            place_of(part, 0, 0, 0, 4 * rows), from_core[pl.ds(4 * start, 4 * rows), :]
        )
    for part, rows, start in part_list:
        far[part].wait_recv()
        add_in(
            place_of(part, 0, 0, 2, 2 * rows),
            third[pl.ds(4 * start + 2 * rows, 2 * rows), :],
        )
        middle[part].start()
        add_in(place_of(part, 0, 0, 0, 2 * rows), third[pl.ds(4 * start, 2 * rows), :])
    for part, rows, start in part_list:
        middle[part].wait_recv()
        add_in(place_of(part, 0, 0, 1, rows), second[pl.ds(2 * start + rows, rows), :])
        close[part].start()
        add_in(place_of(part, 0, 0, 0, rows), second[pl.ds(2 * start, rows), :])
    gain_total = jnp.zeros(gain_ref.shape, F32)
    for part, rows, start in part_list:
        close[part].wait_recv()
        mine = pl.ds(start, rows)
        ffn_in_grad = products[place_of(part, 0, 0, 0, rows), :].astype(F32) + first[
            mine, :
        ].astype(F32)
        back, gain_part = norm_back(residual_ref[mine, :], gain_ref[...], ffn_in_grad)
        back = back + grad_ref[mine, :].astype(F32)
        back_ref[mine, :] = back
        own[mine, :] = back.astype(BF16)
        gain_total = gain_total + gain_part
    gain_back_ref[...] = gain_total
    row_copies = gather4(tokens, low_all, own, sender, place)
    row_copies[0].start()
    row_copies[1].start()
    mine = pl.ds(pl.multiple_of(place.column() * tokens, tokens), tokens)
    own_copy = pltpu.make_async_copy(own, low_all.at[mine], local_sems.at[2])
    own_copy.start()
    for copy in to_core[0] + to_core[1] + far + middle + close:
        copy.wait_send()
    row_copies[0].wait_recv()
    row_copies[2].start()
    own_copy.wait()
    row_copies[1].wait_recv()
    row_copies[2].wait_recv()
    for copy in row_copies:
        copy.wait_send()


def end_kernel(
    partial_ref,
    input_ref,
    gain_ref,
    back_ref,
    grad_ref,
    gain_back_ref,
    from_core,
    outgoing,
    from_x,
    send_sems,
    recv_sems,
):
    tokens = input_ref.shape[0]
    place = Place()
    enter(place, ("x", "core"))
    sender = Sender(place, send_sems, recv_sems)
    total = sum4(partial_ref, from_core, outgoing, from_x, tokens, sender, place)
    back, gain_part = norm_back(input_ref[...].astype(F32), gain_ref[...], total)
    grad_ref[...] = (back + back_ref[...]).astype(BF16)
    gain_back_ref[...] = gain_part


IN_VMEM = pl.BlockSpec(memory_space=pltpu.VMEM)
ANYWHERE = pl.BlockSpec(memory_space=pl.ANY)
MIB = 1 << 20


def shape_of(shape, dtype):
    return jax.ShapeDtypeStruct(shape, dtype)


def call(kernel, number, ins, outs, out_specs, scratch, limit, operands, flops, moved):
    return pl.pallas_call(
        kernel,
        out_shape=outs,
        in_specs=ins,
        out_specs=out_specs,
        scratch_shapes=scratch,
        cost_estimate=pl.CostEstimate(
            flops=flops, bytes_accessed=moved, transcendentals=0
        ),
        compiler_params=pltpu.CompilerParams(
            collective_id=number, has_side_effects=True, vmem_limit_bytes=limit
        ),
    )(*operands)


def copies(count):
    return [pltpu.SemaphoreType.DMA((count,)), pltpu.SemaphoreType.DMA((count,))]


def start_step(layer_input, gain_attn, out_grad):
    tokens, width = layer_input.shape
    return call(
        start_kernel,
        0,
        [IN_VMEM, IN_VMEM, ANYWHERE],
        [shape_of((4 * tokens, width), BF16), shape_of((16 * tokens, width), BF16)],
        [ANYWHERE, ANYWHERE],
        [pltpu.VMEM((tokens, width), BF16)] + copies(24) + [pltpu.SemaphoreType.DMA((4,))],
        32 * MIB,
        (layer_input, gain_attn[None, :], out_grad),
        10**6,
        100 * 10**6,
    )


def ffn_step(partial, layer_input, gain_ffn, grad_all, w_gate, w_up, w_down):
    tokens, width = layer_input.shape
    units = w_gate.shape[1] // 4
    everyone = 16 * tokens
    return call(
        ffn_kernel,
        1,
        [IN_VMEM, IN_VMEM, IN_VMEM, ANYWHERE, ANYWHERE, ANYWHERE, ANYWHERE],
        [
            shape_of((tokens, width), F32),
            shape_of((everyone, width), BF16),
            shape_of((everyone, units), BF16),
            shape_of((everyone, 2 * units), BF16),
            shape_of((everyone, units), BF16),
        ],
        [IN_VMEM, ANYWHERE, IN_VMEM, IN_VMEM, IN_VMEM],
        [
            pltpu.VMEM((2, tokens, width), BF16),
            pltpu.VMEM((tokens, width), BF16),
            pltpu.VMEM((tokens, width), BF16),
            pltpu.VMEM((everyone, width), BF16),
            pltpu.VMEM((everyone, width), BF16),
            pltpu.VMEM((width, units), BF16),
            pltpu.VMEM((width, units), BF16),
            pltpu.VMEM((units, width), BF16),
        ]
        + copies(24)
        + [pltpu.SemaphoreType.DMA((6,))],
        56 * MIB,
        (partial, layer_input, gain_ffn[None, :], grad_all, w_gate, w_up, w_down),
        6 * everyone * width * units,
        150 * 10**6,
    )


def back_step(pair, w_gate, w_up, residual, gain_ffn, out_grad):
    tokens, width = residual.shape
    units = pair.shape[1] // 2
    everyone = 16 * tokens
    return call(
        back_kernel,
        2,
        [IN_VMEM, ANYWHERE, ANYWHERE, IN_VMEM, IN_VMEM, IN_VMEM],
        [
            shape_of((tokens, width), F32),
            shape_of((1, width), F32),
            shape_of((4 * tokens, width), BF16),
        ],
        [IN_VMEM, IN_VMEM, ANYWHERE],
        [
            pltpu.VMEM((width, 2 * units), BF16),
            pltpu.VMEM((everyone, width), BF16),
            pltpu.VMEM((everyone // 2, width), BF16),
            pltpu.VMEM((everyone // 4, width), BF16),
            pltpu.VMEM((everyone // 8, width), BF16),
            pltpu.VMEM((everyone // 16, width), BF16),
            pltpu.VMEM((tokens, width), BF16),
        ]
        + copies(18)
        + [pltpu.SemaphoreType.DMA((3,))],
        56 * MIB,
        (pair, w_gate, w_up, residual, gain_ffn[None, :], out_grad),
        4 * everyone * width * units,
        150 * 10**6,
    )


def end_step(partial, layer_input, gain_attn, back):
    tokens, width = layer_input.shape
    return call(
        end_kernel,
        3,
        [IN_VMEM] * 4,
        [shape_of((tokens, width), BF16), shape_of((1, width), F32)],
        [IN_VMEM] * 2,
        [
            pltpu.VMEM((2, tokens, width), BF16),
            pltpu.VMEM((tokens, width), BF16),
            pltpu.VMEM((tokens, width), BF16),
        ]
        + copies(3),
        32 * MIB,
        (partial, layer_input, gain_attn[None, :], back),
        10**6,
        50 * 10**6,
    )


def across(array, offset):
    return lax.ppermute(array, "dp", [(row, row ^ offset) for row in range(8)])


def spread(total, own_quarter, dim):
    mine = lax.dynamic_index_in_dim(total, own_quarter, 0, keepdims=False)
    low = total.astype(BF16)
    blocks = [mine] + [
        across(
            lax.dynamic_index_in_dim(low, own_quarter ^ offset, 0, keepdims=False), offset
        ).astype(F32)
        for offset in range(1, 4)
    ]
    width = mine.shape[dim]
    shape = list(mine.shape)
    shape[dim] = 4 * width
    result = jnp.zeros(shape, F32)
    for offset, block in enumerate(blocks):
        result = lax.dynamic_update_slice_in_dim(
            result, block, (own_quarter ^ offset) * width, dim
        )
    return result


def per_device_sixteen(
    layer_input,
    doc_lengths,
    w_query,
    w_key,
    w_value,
    w_out,
    w_gate,
    w_up,
    w_down,
    gain_attn,
    gain_ffn,
    gain_query,
    gain_key,
    out_grad,
):
    row = lax.axis_index("dp")
    half, quarter = row // 4, row % 4
    length = layer_input.shape[0] * 4
    attn_in, grad_all = start_step(layer_input, gain_attn, out_grad)
    attn_mixed, saved = attention_forward(
        attn_in, doc_lengths, w_query, w_key, w_value, gain_query, gain_key
    )
    partial = jnp.dot(attn_mixed, w_out, preferred_element_type=F32).astype(BF16)
    residual, ffn_all, hidden, pair, hidden_rows = ffn_step(
        partial, layer_input, gain_ffn, grad_all, w_gate, w_up, w_down
    )
    width = ffn_all.shape[1]
    units = hidden.shape[1]

    def half_of(array, which):
        return lax.dynamic_slice_in_dim(array, which * (width // 2), width // 2, 1)

    down_sent = matmul_tn(hidden, half_of(grad_all, 1 - half)).astype(BF16)
    pair_sent = matmul_tn(half_of(ffn_all, 1 - half), pair).astype(BF16)
    down_came = across(down_sent, 4)
    pair_came = across(pair_sent, 4)
    pair, down_sent, pair_sent = lax.optimization_barrier((pair, down_sent, pair_sent))
    residual_grad, gain_ffn_part, res_low = back_step(
        pair, w_gate, w_up, residual, gain_ffn, out_grad
    )
    rows = hidden_rows.reshape(4, length, units)
    arrived = jnp.stack([rows[0]] + [across(rows[offset], offset) for offset in range(1, 4)])
    row_hidden = jnp.concatenate(
        [
            lax.dynamic_index_in_dim(arrived, quarter ^ place, 0, keepdims=False)
            for place in range(4)
        ],
        axis=1,
    )
    layer_out = (
        residual
        + lax.psum_scatter(
            jnp.dot(row_hidden, w_down, preferred_element_type=F32).astype(BF16),
            "tensor",
            scatter_dimension=0,
            tiled=True,
        ).astype(F32)
    ).astype(BF16)
    mixed_grad = matmul_nt(res_low, w_out).astype(BF16)
    grad_out = line_reduce(pair_sum(attn_mixed, res_low, 1), 1)
    query_low, key_low, value_low, gain_query_part, gain_key_part = attention_backward(
        mixed_grad, saved, gain_query, gain_key
    )
    partial_in = (
        matmul_nt(query_low, w_query) + matmul_nt(key_low, w_key) + matmul_nt(value_low, w_value)
    ).astype(BF16)
    input_grad, gain_attn_part = end_step(partial_in, layer_input, gain_attn, residual_grad)
    query_cols, key_cols = query_low.shape[1], key_low.shape[1]
    grad_qkv = line_reduce(
        pair_sum(attn_in, jnp.concatenate([query_low, key_low, value_low], axis=1), 0), 0
    )
    down_total = matmul_tn(hidden, half_of(grad_all, half)) + down_came.astype(F32)
    pair_total = matmul_tn(half_of(ffn_all, half), pair) + pair_came.astype(F32)
    block = width // 8
    grad_down = spread(down_total.reshape(units, 4, block).transpose(1, 0, 2), quarter, 0)
    pair_blocks = spread_pair(pair_total.reshape(4, block, 2, units), quarter)
    gain_sums = lax.psum(
        (gain_attn_part[0], gain_ffn_part[0], gain_query_part, gain_key_part),
        ("dp", "tensor"),
    )
    return (
        layer_out,
        input_grad,
        grad_qkv[:, :query_cols],
        grad_qkv[:, query_cols : query_cols + key_cols],
        grad_qkv[:, query_cols + key_cols :],
        grad_out,
        pair_blocks[0],
        pair_blocks[1],
        grad_down,
        gain_sums[0],
        gain_sums[1],
        gain_sums[2],
        gain_sums[3],
    )


def spread_pair(total, own_quarter):
    mine = lax.dynamic_index_in_dim(total, own_quarter, 0, keepdims=False)
    low = total.astype(BF16)
    blocks = [mine] + [
        across(
            lax.dynamic_index_in_dim(low, own_quarter ^ offset, 0, keepdims=False), offset
        ).astype(F32)
        for offset in range(1, 4)
    ]
    block, units = mine.shape[0], mine.shape[2]
    results = []
    for which in range(2):
        result = jnp.zeros((block, 4 * units), F32)
        for offset, values in enumerate(blocks):
            result = lax.dynamic_update_slice_in_dim(
                result, values[:, which], (own_quarter ^ offset) * units, 1
            )
        results.append(result)
    return results


def solution(mesh):
    in_specs = (
        P(("dp", "tensor"), None),
        P("dp", None),
        P(None, "tensor"),
        P(None, "tensor"),
        P(None, "tensor"),
        P("tensor", None),
        P(None, "tensor"),
        P(None, "tensor"),
        P("tensor", None),
        P(),
        P(),
        P(),
        P(),
        P(("dp", "tensor"), None),
    )
    out_specs = (
        P(("dp", "tensor"), None),
        P(("dp", "tensor"), None),
        P("dp", "tensor"),
        P("dp", "tensor"),
        P("dp", "tensor"),
        P("tensor", "dp"),
        P("dp", "tensor"),
        P("dp", "tensor"),
        P("tensor", "dp"),
        P(),
        P(),
        P(),
        P(),
    )
    sixteen = mesh.shape["dp"] == 8 and mesh.shape["tensor"] == 4
    return jax.shard_map(
        per_device_sixteen if sixteen else per_device, mesh=mesh, in_specs=in_specs, out_specs=out_specs, check_vma=False
    )
```

```python
import jax
import jax.numpy as jnp
import numpy as np
from jax import lax
from jax.experimental import pallas as pl
from jax.experimental.pallas import tpu as pltpu
from jax.sharding import PartitionSpec as P

HEADS = 32
KV = 8


EPSILON = 1e-06
ROPE_BASE = 10000.0
MASKED = -1e30


def norm_gain(row_block, gain_vec):
    factor = lax.rsqrt(jnp.mean(row_block * row_block, axis=-1, keepdims=True) + EPSILON)
    return row_block * factor * gain_vec


def rotate(vector, cosine, sine_table):
    half_width = vector.shape[-1] // 2
    first = vector[..., :half_width]
    second = vector[..., half_width:]
    return jnp.concatenate(
        [first * cosine - second * sine_table, second * cosine + first * sine_table], axis=-1
    )


def head_prep(raw_proj, gain_vec, cosine, sine_table):
    head_width = gain_vec.shape[0]
    per_head = raw_proj.reshape(raw_proj.shape[0], raw_proj.shape[1] // head_width, head_width)
    return rotate(norm_gain(per_head, gain_vec), cosine[:, None, :], sine_table[:, None, :])


def doc_layout(lengths, length):
    doc_ends = jnp.cumsum(lengths)
    places = jnp.arange(length, dtype=jnp.int32)
    passed_end = (places[:, None] >= doc_ends[None, :]).astype(jnp.int32)
    doc_ids = jnp.sum(passed_end, axis=1)
    starts = jnp.sum(passed_end * lengths[None, :], axis=1)
    return (doc_ids, places, places - starts)


def rope_tables(offsets, head_width):
    frequency = ROPE_BASE ** (-jnp.arange(0, head_width, 2, dtype=jnp.float32) / head_width)
    angles = offsets.astype(jnp.float32)[:, None] * frequency[None, :]
    return (jnp.cos(angles), jnp.sin(angles))


def swiglu(gate_proj, up_proj):
    return jax.nn.silu(gate_proj) * up_proj


def matmul_nt(left_mat, right_mat):
    return lax.dot_general(
        left_mat, right_mat, (((1,), (1,)), ((), ())), preferred_element_type=jnp.float32
    )


def matmul_tn(left_mat, right_mat):
    return lax.dot_general(
        left_mat, right_mat, (((0,), (0,)), ((), ())), preferred_element_type=jnp.float32
    )


def per_device(
    layer_input,
    doc_lengths,
    w_query,
    w_key,
    w_value,
    w_out,
    w_gate,
    w_up,
    w_down,
    gain_attn,
    gain_ffn,
    gain_query,
    gain_key,
    out_grad,
):
    tok_rows = layer_input.shape[0]
    head_width = gain_query.shape[0]
    tensor_count = lax.axis_size("tensor")
    length = tok_rows * tensor_count
    per_dev = w_query.shape[1] // head_width
    groups_dev = w_key.shape[1] // head_width
    input_f32 = layer_input.astype(jnp.float32)
    doc_ids, places, offsets = doc_layout(doc_lengths[0], length)
    cosine, sine_table = rope_tables(offsets, head_width)
    attn_in = lax.all_gather(
        norm_gain(input_f32, gain_attn).astype(jnp.bfloat16), "tensor", axis=0, tiled=True
    )
    query_raw = jnp.dot(attn_in, w_query, preferred_element_type=jnp.float32)
    key_raw = jnp.dot(attn_in, w_key, preferred_element_type=jnp.float32).astype(jnp.bfloat16)
    value_raw = jnp.dot(attn_in, w_value, preferred_element_type=jnp.float32).astype(jnp.bfloat16)
    key_f32 = key_raw.astype(jnp.float32)
    queries = head_prep(query_raw, gain_query, cosine, sine_table).astype(jnp.bfloat16)
    key_rot = head_prep(key_f32, gain_key, cosine, sine_table).astype(jnp.bfloat16)
    local_heads = jnp.arange(per_dev, dtype=jnp.int32)
    group_pick = (
        local_heads[:, None] // (HEADS // KV) == jnp.arange(groups_dev, dtype=jnp.int32)[None, :]
    ).astype(jnp.float32)
    pick_low = group_pick.astype(jnp.bfloat16)
    key_heads = jnp.einsum(
        "lgd,hg->lhd", key_rot, pick_low, preferred_element_type=jnp.float32
    ).astype(jnp.bfloat16)
    value_heads = jnp.einsum(
        "lgd,hg->lhd",
        value_raw.reshape(length, groups_dev, head_width),
        pick_low,
        preferred_element_type=jnp.float32,
    ).astype(jnp.bfloat16)
    block_rows = min(512, length)
    block_count = length // block_rows
    score_scale = head_width ** (-0.5)

    def block_scores(block_num):
        row_begin = block_num * block_rows
        query_block = lax.dynamic_slice_in_dim(queries, row_begin, block_rows, 0)
        ids_block = lax.dynamic_slice_in_dim(doc_ids, row_begin, block_rows, 0)
        places_block = lax.dynamic_slice_in_dim(places, row_begin, block_rows, 0)
        scores = (
            jnp.einsum("qhd,khd->hqk", query_block, key_heads, preferred_element_type=jnp.float32)
            * score_scale
        )
        allowed = (ids_block[:, None] == doc_ids[None, :]) & (
            places[None, :] <= places_block[:, None]
        )
        return (query_block, jnp.where(allowed[None], scores, MASKED))

    def forward_block(block_num):
        query_block, scores = block_scores(block_num)
        row_top = jnp.max(scores, axis=-1, keepdims=True)
        exponent = jnp.exp(scores - row_top)
        row_total = jnp.sum(exponent, axis=-1, keepdims=True)
        probabilities = (exponent / row_total).astype(jnp.bfloat16)
        mixed_block = jnp.einsum(
            "hqk,khd->qhd", probabilities, value_heads, preferred_element_type=jnp.float32
        )
        return (mixed_block, row_top + jnp.log(row_total))

    mixed_all, log_totals = lax.map(forward_block, jnp.arange(block_count, dtype=jnp.int32))
    attn_mixed = mixed_all.reshape(length, per_dev * head_width).astype(jnp.bfloat16)
    residual = input_f32 + lax.psum_scatter(
        jnp.dot(attn_mixed, w_out, preferred_element_type=jnp.float32).astype(jnp.bfloat16),
        "tensor",
        scatter_dimension=0,
        tiled=True,
    ).astype(jnp.float32)
    ffn_in = lax.all_gather(
        norm_gain(residual, gain_ffn).astype(jnp.bfloat16), "tensor", axis=0, tiled=True
    )
    gate_proj = jnp.dot(ffn_in, w_gate, preferred_element_type=jnp.float32)
    up_proj = jnp.dot(ffn_in, w_up, preferred_element_type=jnp.float32)
    hidden = swiglu(gate_proj, up_proj).astype(jnp.bfloat16)
    layer_out = (
        residual
        + lax.psum_scatter(
            jnp.dot(hidden, w_down, preferred_element_type=jnp.float32).astype(jnp.bfloat16),
            "tensor",
            scatter_dimension=0,
            tiled=True,
        ).astype(jnp.float32)
    ).astype(jnp.bfloat16)
    grad_rows = lax.all_gather(out_grad, "tensor", axis=0, tiled=True)
    hidden_grad = matmul_nt(grad_rows, w_down)
    grad_down = matmul_tn(hidden, grad_rows)
    unused_value, swiglu_back = jax.vjp(swiglu, gate_proj, up_proj)
    gate_grad, up_grad = swiglu_back(hidden_grad)
    gate_grad = gate_grad.astype(jnp.bfloat16)
    up_grad = up_grad.astype(jnp.bfloat16)
    grad_gate = matmul_tn(ffn_in, gate_grad)
    grad_up = matmul_tn(ffn_in, up_grad)
    ffn_in_grad = lax.psum_scatter(
        (matmul_nt(gate_grad, w_gate) + matmul_nt(up_grad, w_up)).astype(jnp.bfloat16),
        "tensor",
        scatter_dimension=0,
        tiled=True,
    ).astype(jnp.float32)
    unused_norm, ffn_norm_back = jax.vjp(norm_gain, residual, gain_ffn)
    residual_grad, gain_ffn_grad = ffn_norm_back(ffn_in_grad)
    residual_grad = residual_grad + out_grad.astype(jnp.float32)
    res_low = lax.all_gather(residual_grad.astype(jnp.bfloat16), "tensor", axis=0, tiled=True)
    mixed_grad = matmul_nt(res_low, w_out).astype(jnp.bfloat16).reshape(length, per_dev, head_width)
    grad_out = matmul_tn(attn_mixed, res_low)

    def backward_block(running, block_num):
        key_acc, value_acc = running
        query_block, scores = block_scores(block_num)
        probabilities = jnp.exp(scores - log_totals[block_num])
        grad_block = lax.dynamic_slice_in_dim(mixed_grad, block_num * block_rows, block_rows, 0)
        prob_grad = jnp.einsum(
            "qhd,khd->hqk", grad_block, value_heads, preferred_element_type=jnp.float32
        )
        value_acc = value_acc + jnp.einsum(
            "hqk,qhd->khd",
            probabilities.astype(jnp.bfloat16),
            grad_block,
            preferred_element_type=jnp.float32,
        )
        centre = jnp.sum(probabilities * prob_grad, axis=-1, keepdims=True)
        score_grad = (probabilities * (prob_grad - centre)).astype(jnp.bfloat16)
        query_part = (
            jnp.einsum("hqk,khd->qhd", score_grad, key_heads, preferred_element_type=jnp.float32)
            * score_scale
        )
        key_acc = (
            key_acc
            + jnp.einsum(
                "hqk,qhd->khd", score_grad, query_block, preferred_element_type=jnp.float32
            )
            * score_scale
        )
        return ((key_acc, value_acc), query_part)

    zeros_init = jnp.zeros((length, per_dev, head_width), jnp.float32)
    (key_acc, value_acc), query_parts = lax.scan(
        backward_block, (zeros_init, zeros_init), jnp.arange(block_count, dtype=jnp.int32)
    )
    query_rot_grad = query_parts.reshape(length, per_dev, head_width)
    unused_query, query_back = jax.vjp(
        lambda raw_proj, gain_vec: head_prep(raw_proj, gain_vec, cosine, sine_table),
        query_raw,
        gain_query,
    )
    query_raw_grad, gain_query_grad = query_back(query_rot_grad)
    query_low = query_raw_grad.astype(jnp.bfloat16)
    key_group_grad = jnp.einsum("lhd,hg->lgd", key_acc, group_pick, precision=lax.Precision.HIGHEST)
    value_group_grad = jnp.einsum(
        "lhd,hg->lgd", value_acc, group_pick, precision=lax.Precision.HIGHEST
    )
    unused_key, key_back = jax.vjp(
        lambda raw_proj, gain_vec: head_prep(raw_proj, gain_vec, cosine, sine_table),
        key_f32,
        gain_key,
    )
    key_raw_grad, gain_key_grad = key_back(key_group_grad)
    key_low = key_raw_grad.astype(jnp.bfloat16)
    value_low = value_group_grad.reshape(length, groups_dev * head_width).astype(jnp.bfloat16)
    grad_query = matmul_tn(attn_in, query_low)
    grad_key = matmul_tn(attn_in, key_low)
    grad_value = matmul_tn(attn_in, value_low)
    attn_in_grad = lax.psum_scatter(
        (
            matmul_nt(query_low, w_query)
            + matmul_nt(key_low, w_key)
            + matmul_nt(value_low, w_value)
        ).astype(jnp.bfloat16),
        "tensor",
        scatter_dimension=0,
        tiled=True,
    ).astype(jnp.float32)
    unused_attn, attn_norm_back = jax.vjp(norm_gain, input_f32, gain_attn)
    input_part, gain_attn_grad = attn_norm_back(attn_in_grad)
    input_grad = (input_part + residual_grad).astype(jnp.bfloat16)
    reduced = (
        lax.psum_scatter(
            grad_query.astype(jnp.bfloat16), "dp", scatter_dimension=0, tiled=True
        ).astype(jnp.float32),
        lax.psum_scatter(
            grad_key.astype(jnp.bfloat16), "dp", scatter_dimension=0, tiled=True
        ).astype(jnp.float32),
        lax.psum_scatter(
            grad_value.astype(jnp.bfloat16), "dp", scatter_dimension=0, tiled=True
        ).astype(jnp.float32),
        lax.psum_scatter(
            grad_out.astype(jnp.bfloat16), "dp", scatter_dimension=1, tiled=True
        ).astype(jnp.float32),
        lax.psum_scatter(
            grad_gate.astype(jnp.bfloat16), "dp", scatter_dimension=0, tiled=True
        ).astype(jnp.float32),
        lax.psum_scatter(
            grad_up.astype(jnp.bfloat16), "dp", scatter_dimension=0, tiled=True
        ).astype(jnp.float32),
        lax.psum_scatter(
            grad_down.astype(jnp.bfloat16), "dp", scatter_dimension=1, tiled=True
        ).astype(jnp.float32),
    )
    gain_sums = lax.psum(
        (gain_attn_grad, gain_ffn_grad, gain_query_grad, gain_key_grad), ("dp", "tensor")
    )
    return (
        layer_out,
        input_grad,
        reduced[0],
        reduced[1],
        reduced[2],
        reduced[3],
        reduced[4],
        reduced[5],
        reduced[6],
        gain_sums[0],
        gain_sums[1],
        gain_sums[2],
        gain_sums[3],
    )


MESH_ID = pl.DeviceIdType.MESH
ORDERS = (("x", "y", "z"), ("y", "z", "x"), ("z", "x", "y"))
LINKS = ("x", "y", "z", "core")
GRAD_PATHS = (("x", "y", "z"), ("x", "z", "y"), ("x", "y", "z"))
HEAD_WIDTH = 64
QUARTERS = (("y", "z"), ("y",), ("z",), ())
F32 = jnp.float32
BF16 = jnp.bfloat16


class Place:
    def __init__(self):
        row, column = lax.axis_index("dp"), lax.axis_index("tensor")
        self.far = row // 4
        self.at = {
            "z": (row // 2) % 2,
            "y": row % 2,
            "x": column // 2,
            "core": column % 2,
        }

    def flipped(self, names):
        return {
            name: 1 - value if name in names else value for name, value in self.at.items()
        }

    def device(self, names):
        names = (names,) if isinstance(names, str) else names
        at = self.flipped(names)
        far = 1 - self.far if "far" in names else self.far
        return {
            "dp": far * 4 + at["z"] * 2 + at["y"],
            "tensor": at["x"] * 2 + at["core"],
        }

    def column(self, names=()):
        at = self.flipped(names)
        return at["x"] * 2 + at["core"]

    def quarter(self, names=()):
        at = self.flipped(names)
        return at["z"] * 2 + at["y"]


def enter(place, names):
    barrier = pltpu.get_barrier_semaphore()
    for name in names:
        pl.semaphore_signal(
            barrier, inc=1, device_id=place.device(name), device_id_type=MESH_ID
        )
    pl.semaphore_wait(barrier, len(names))


class Sender:
    def __init__(self, place, send_sems, recv_sems):
        self.place, self.send_sems, self.recv_sems, self.used = place, send_sems, recv_sems, 0

    def copy(self, source, target, name):
        slot = self.used
        self.used += 1
        return pltpu.make_async_remote_copy(
            src_ref=source,
            dst_ref=target,
            send_sem=self.send_sems.at[slot],
            recv_sem=self.recv_sems.at[slot],
            device_id=self.place.device(name),
            device_id_type=MESH_ID,
        )


def part_rows(tokens):
    unit = tokens // 16
    first = -(-unit // 3)
    second = -(-(unit - first) // 2)
    return (first * 16, second * 16, (unit - first - second) * 16)


def part_starts(tokens):
    rows = part_rows(tokens)
    return (0, rows[0], rows[0] + rows[1])


def spot(tokens, part, half, core, index):
    rows, start = part_rows(tokens)[part], part_starts(tokens)[part]
    return half * 8 * tokens + 8 * start + core * 4 * rows + index * rows


def gather4(tokens, buffer, own, sender, place):
    mine = pl.ds(pl.multiple_of(place.column() * tokens, tokens), tokens)
    theirs = pl.ds(pl.multiple_of(place.column(("x",)) * tokens, tokens), tokens)
    return (
        sender.copy(own, buffer.at[mine], "x"),
        sender.copy(own, buffer.at[mine], "core"),
        sender.copy(buffer.at[theirs], buffer.at[theirs], "core"),
    )


def normed(values, gain):
    factor = lax.rsqrt(jnp.mean(values * values, axis=-1, keepdims=True) + EPSILON)
    return values * factor * gain


def norm_back(values, gain, grad):
    factor = lax.rsqrt(jnp.mean(values * values, axis=-1, keepdims=True) + EPSILON)
    unit = values * factor
    scaled = gain * grad
    back = factor * (scaled - unit * jnp.mean(scaled * unit, axis=-1, keepdims=True))
    return back, jnp.sum(grad * unit, axis=0, keepdims=True)


def scatter4(partial, from_core, from_x, tokens, sender, place):
    copies = []
    for names in (("x", "core"), ("core",)):
        shard = pl.ds(pl.multiple_of(place.column(names) * tokens, tokens), tokens)
        copies.append(
            sender.copy(partial.at[shard], from_core.at[len(copies)], "core")
        )
    return copies


def sum4(partial, from_core, outgoing, from_x, tokens, sender, place):
    copies = scatter4(partial, from_core, from_x, tokens, sender, place)
    for copy in copies:
        copy.start()
    far = pl.ds(pl.multiple_of(place.column(("x",)) * tokens, tokens), tokens)
    mine = pl.ds(pl.multiple_of(place.column() * tokens, tokens), tokens)
    copies[0].wait_recv()
    outgoing[...] = (partial[far, :].astype(F32) + from_core[0].astype(F32)).astype(BF16)
    along = sender.copy(outgoing, from_x, "x")
    along.start()
    copies[1].wait_recv()
    near = partial[mine, :].astype(F32) + from_core[1].astype(F32)
    along.wait_recv()
    total = near + from_x[...].astype(F32)
    for copy in copies:
        copy.wait_send()
    along.wait_send()
    return total


def silu_parts(gate, up, hidden_grad):
    s = 1.0 / (1.0 + jnp.exp(-gate))
    silu = gate * s
    hidden = silu * up
    gate_grad = hidden_grad * up * s * (1.0 + gate * (1.0 - s))
    return hidden, gate_grad, hidden_grad * silu


def back_kernel(
    pair_ref,
    gate_w,
    up_w,
    residual_ref,
    gain_ref,
    grad_ref,
    hidden_ref,
    ffn_all,
    grad_all,
    back_ref,
    gain_back_ref,
    low_all,
    down_came,
    pair_sent,
    weights,
    down_sent,
    ffn_half,
    grad_half,
    products,
    from_core,
    third,
    second,
    first,
    own,
    send_sems,
    recv_sems,
    local_sems,
):
    tokens = residual_ref.shape[0]
    units = pair_ref.shape[1] // 2
    place = Place()
    columns = pl.ds(pl.multiple_of(place.quarter() * units, units), units)
    loads = [
        pltpu.make_async_copy(
            gate_w.at[:, columns], weights.at[:, pl.ds(0, units)], local_sems.at[0]
        ),
        pltpu.make_async_copy(
            up_w.at[:, columns], weights.at[:, pl.ds(units, units)], local_sems.at[1]
        ),
    ]
    width = residual_ref.shape[1]
    block_width = width // 8
    other = pl.ds(pl.multiple_of((1 - place.far) * (width // 2), width // 2), width // 2)
    halves = [
        pltpu.make_async_copy(grad_all.at[:, other], grad_half, local_sems.at[3]),
        pltpu.make_async_copy(ffn_all.at[:, other], ffn_half, local_sems.at[4]),
    ]
    enter(place, LINKS + ("far",))
    for copy in loads + halves:
        copy.start()
    sender = Sender(place, send_sems, recv_sems)
    part_list = [
        (part, part_rows(tokens)[part], part_starts(tokens)[part]) for part in range(3)
    ]

    def place_of(part, half, core, index, count):
        return pl.ds(spot(tokens, part, half, core, index), count)

    to_core = [
        [
            sender.copy(
                products.at[place_of(part, half, 1, 0, 4 * rows)],
                from_core.at[pl.ds(half * 4 * tokens + 4 * start, 4 * rows)],
                "core",
            )
            for part, rows, start in part_list
        ]
        for half in range(2)
    ]
    far = [
        sender.copy(
            products.at[place_of(part, 1, 0, 0, 4 * rows)],
            third.at[pl.ds(4 * start, 4 * rows)],
            ORDERS[part][2],
        )
        for part, rows, start in part_list
    ]
    middle = [
        sender.copy(
            products.at[place_of(part, 0, 0, 2, 2 * rows)],
            second.at[pl.ds(2 * start, 2 * rows)],
            ORDERS[part][1],
        )
        for part, rows, start in part_list
    ]
    close = [
        sender.copy(
            products.at[place_of(part, 0, 0, 1, rows)],
            first.at[pl.ds(start, rows)],
            ORDERS[part][0],
        )
        for part, rows, start in part_list
    ]
    bulk = [
        sender.copy(
            down_sent.at[turn], down_came.at[pl.ds(turn * units, units)], "far"
        )
        for turn in range(4)
    ]

    def columns_of(names):
        start = place.quarter(names) * block_width
        return pl.ds(pl.multiple_of(start, block_width), block_width)

    for copy in loads:
        copy.wait()
    block = 2 * tokens

    def compute(index):
        rows = pl.ds(pl.multiple_of(index * block, block), block)
        products[rows, :] = matmul_nt(pair_ref[rows, :], weights[...]).astype(BF16)

    def add_in(rows, arrived):
        products[rows, :] = (
            products[rows, :].astype(F32) + arrived.astype(F32)
        ).astype(BF16)

    pl.loop(4, 8)(compute)
    for copy in to_core[1]:
        copy.start()
    pl.loop(0, 2)(compute)
    for part, rows, start in part_list:
        to_core[1][part].wait_recv()
        add_in(
            place_of(part, 1, 0, 0, 4 * rows),
            from_core[pl.ds(4 * tokens + 4 * start, 4 * rows), :],
        )
        far[part].start()
    pl.loop(2, 4)(compute)
    for copy in to_core[0]:
        copy.start()
    halves[0].wait()
    for turn, names in enumerate(QUARTERS):
        down_sent[turn] = matmul_tn(
            hidden_ref[...], grad_half[:, columns_of(names)]
        ).astype(BF16)
        if turn < 2:
            bulk[turn].start()
    for part, rows, start in part_list:
        to_core[0][part].wait_recv()
        add_in(
            place_of(part, 0, 0, 0, 4 * rows), from_core[pl.ds(4 * start, 4 * rows), :]
        )
    halves[1].wait()
    for turn, names in enumerate(QUARTERS):
        pair_sent[turn] = matmul_tn(
            ffn_half[:, columns_of(names)], pair_ref[...]
        ).astype(BF16)
    for part, rows, start in part_list:
        far[part].wait_recv()
        add_in(
            place_of(part, 0, 0, 2, 2 * rows),
            third[pl.ds(4 * start + 2 * rows, 2 * rows), :],
        )
        middle[part].start()
        add_in(place_of(part, 0, 0, 0, 2 * rows), third[pl.ds(4 * start, 2 * rows), :])
    bulk[2].start()
    for part, rows, start in part_list:
        middle[part].wait_recv()
        add_in(place_of(part, 0, 0, 1, rows), second[pl.ds(2 * start + rows, rows), :])
        close[part].start()
        add_in(place_of(part, 0, 0, 0, rows), second[pl.ds(2 * start, rows), :])
    bulk[3].start()
    gain_total = jnp.zeros(gain_ref.shape, F32)
    for part, rows, start in part_list:
        close[part].wait_recv()
        mine = pl.ds(start, rows)
        ffn_in_grad = products[place_of(part, 0, 0, 0, rows), :].astype(F32) + first[
            mine, :
        ].astype(F32)
        back, gain_part = norm_back(residual_ref[mine, :], gain_ref[...], ffn_in_grad)
        back = back + grad_ref[mine, :].astype(F32)
        back_ref[mine, :] = back
        own[mine, :] = back.astype(BF16)
        gain_total = gain_total + gain_part
    gain_back_ref[...] = gain_total
    row_copies = gather4(tokens, low_all, own, sender, place)
    row_copies[0].start()
    row_copies[1].start()
    mine = pl.ds(pl.multiple_of(place.column() * tokens, tokens), tokens)
    own_copy = pltpu.make_async_copy(own, low_all.at[mine], local_sems.at[2])
    own_copy.start()
    row_copies[0].wait_recv()
    row_copies[2].start()
    own_copy.wait()
    row_copies[1].wait_recv()
    row_copies[2].wait_recv()
    for copy in to_core[0] + to_core[1] + far + middle + close + list(row_copies):
        copy.wait_send()
    for copy in bulk:
        copy.wait()


def runs16(order, path, step):
    place_of = {
        name: position for position, name in enumerate(order)
    }
    known = [set(chosen) for chosen in subsets(path[:step])]
    moves = []
    for flips in known:
        spots = []
        for names in (flips, flips | {path[step]}):
            bits = [int(name in names) for name in order]
            spots.append((bits[2], bits[0] + 2 * bits[1]))
        moves.append(spots)
    moves.sort()
    runs = []
    for (half, index), (to_half, to_index) in moves:
        if runs:
            last = runs[-1]
            if (
                last[0] == half
                and last[2] == to_half
                and last[1] + last[4] == index
                and last[3] + last[4] == to_index
            ):
                last[4] += 1
                continue
        runs.append([half, index, to_half, to_index, 1])
    return runs


def subsets(names):
    result = [()]
    for name in names:
        result = result + [chosen + (name,) for chosen in result]
    return result


def gather16(tokens, buffer, own, sender, paths):
    links, cores = [], []
    for part, order in enumerate(ORDERS):
        rows, start = part_rows(tokens)[part], part_starts(tokens)[part]

        def region(half, index, count, core=0):
            return buffer.at[pl.ds(spot(tokens, part, half, core, index), count * rows)]

        mine = region(0, 0, 1) if own is None else own.at[pl.ds(start, rows)]
        part_links = []
        part_cores = [[sender.copy(mine, region(0, 0, 1, 1), "core")]]
        for step in range(3):
            step_links, step_cores = [], []
            for half, index, to_half, to_index, count in runs16(order, paths[part], step):
                source = mine if step == 0 else region(half, index, count)
                step_links.append(
                    sender.copy(source, region(to_half, to_index, count), paths[part][step])
                )
                step_cores.append(
                    sender.copy(
                        region(to_half, to_index, count),
                        region(to_half, to_index, count, 1),
                        "core",
                    )
                )
            part_links.append(step_links)
            part_cores.append(step_cores)
        links.append(part_links)
        cores.append(part_cores)
    return links, cores


def gather_begin(links, cores):
    for part in range(3):
        for copy in links[part][0] + cores[part][0]:
            copy.start()


def gather_go(links, cores, step):
    for part in range(3):
        for copy in links[part][step]:
            copy.wait_recv()
        if step < 2:
            for copy in links[part][step + 1]:
                copy.start()
        for copy in cores[part][step + 1]:
            copy.start()


def gather_sent(links, cores):
    for part in range(3):
        for copies in links[part] + cores[part]:
            for copy in copies:
                copy.wait_send()


def document_tables(lengths_ref, frequency, length):
    down = lax.broadcasted_iota(jnp.int32, (length, 128), 0)
    across_lanes = lax.broadcasted_iota(jnp.int32, (8, length), 1)
    ids_down = jnp.zeros((length, 128), jnp.int32)
    starts = jnp.zeros((length, 128), jnp.int32)
    ids_across = jnp.zeros((8, length), jnp.int32)
    end = jnp.int32(0)
    for document in range(lengths_ref.shape[1]):
        count = lengths_ref[0, document]
        end = end + count
        passed = down >= end
        ids_down = ids_down + jnp.where(passed, 1, 0)
        starts = starts + jnp.where(passed, count, 0)
        ids_across = ids_across + jnp.where(across_lanes >= end, 1, 0)
    angles = (down - starts).astype(F32) * frequency
    return ids_down[:, :1], ids_across[:1, :], angles


def document_bias(ids_down, ids_across, length):
    allowed = (ids_down == ids_across) & (
        lax.broadcasted_iota(jnp.int32, (length, length), 1)
        <= lax.broadcasted_iota(jnp.int32, (length, length), 0)
    )
    return jnp.where(allowed, 0.0, MASKED)


def head_forward(raw, gain, cosine, sine, head_width):
    factor = lax.rsqrt(head_means(raw * raw, head_width) + EPSILON)
    values = raw * factor * gain
    width = raw.shape[1]
    return values * widen(cosine, width) + swap_halves(values, head_width) * widen(sine, width)


def forward_kernel(
    lengths_ref,
    input_ref,
    gain_attn,
    gain_ffn,
    gain_query,
    gain_key,
    frequency,
    out_grad,
    query_w,
    key_w,
    value_w,
    out_w,
    gate_w,
    up_w,
    down_w,
    attn_all,
    mixed_ref,
    query_ref,
    key_ref,
    value_ref,
    query_raw,
    key_raw,
    totals_ref,
    cosine_ref,
    sine_ref,
    residual_ref,
    ffn_all,
    grad_all,
    hidden_ref,
    pair_ref,
    rows_ref,
    own,
    attn_in,
    qkv_w,
    out_v,
    bias,
    partial,
    from_core,
    outgoing,
    from_x,
    ffn_buf,
    grad_buf,
    gate_v,
    up_v,
    down_v,
    send_sems,
    recv_sems,
    local_sems,
):
    tokens, width = input_ref.shape
    length = 4 * tokens
    units = gate_v.shape[1]
    heads_width, key_width = query_ref.shape[1], key_ref.shape[1]
    place = Place()
    columns = pl.ds(pl.multiple_of(place.quarter() * units, units), units)
    local_used = [0]

    def load(source, target):
        copy = pltpu.make_async_copy(source, target, local_sems.at[local_used[0]])
        local_used[0] += 1
        copy.start()
        return copy

    enter(place, LINKS)
    sender = Sender(place, send_sems, recv_sems)
    own[...] = normed(input_ref[...].astype(F32), gain_attn[...]).astype(BF16)
    row_copies = gather4(tokens, attn_in, own, sender, place)
    row_copies[0].start()
    row_copies[1].start()
    grad_links, grad_cores = gather16(tokens, grad_buf, out_grad, sender, GRAD_PATHS)
    gather_begin(grad_links, grad_cores)
    first_loads = [
        load(query_w, qkv_w.at[:, pl.ds(0, heads_width)]),
        load(key_w, qkv_w.at[:, pl.ds(heads_width, key_width)]),
        load(value_w, qkv_w.at[:, pl.ds(heads_width + key_width, key_width)]),
        load(out_w, out_v),
    ]
    mine = pl.ds(pl.multiple_of(place.column() * tokens, tokens), tokens)
    attn_in[mine, :] = own[...]
    grad_loads = []
    for part in range(3):
        rows, start = part_rows(tokens)[part], part_starts(tokens)[part]
        grad_loads.append(
            load(
                out_grad.at[pl.ds(start, rows)],
                grad_buf.at[pl.ds(spot(tokens, part, 0, 0, 0), rows)],
            )
        )
    later_loads = [
        load(gate_w.at[:, columns], gate_v),
        load(up_w.at[:, columns], up_v),
        load(down_w.at[columns, :], down_v),
    ]
    ids_down, ids_across, angles = document_tables(lengths_ref, frequency[...], length)
    lane = lax.broadcasted_iota(jnp.int32, (length, 128), 1)
    cosine_ref[...] = jnp.cos(angles)
    sine = jnp.sin(angles)
    sine_ref[...] = jnp.where(lane % HEAD_WIDTH < HEAD_WIDTH // 2, -sine, sine)
    bias[...] = document_bias(ids_down, ids_across, length)
    for copy in first_loads + grad_loads:
        copy.wait()
    row_copies[0].wait_recv()
    row_copies[2].start()
    row_copies[1].wait_recv()
    row_copies[2].wait_recv()
    attn_store = load(attn_in, attn_all)
    gather_go(grad_links, grad_cores, 0)

    raw = jnp.dot(attn_in[...], qkv_w[...], preferred_element_type=F32)
    query_raw[...] = raw[:, :heads_width]
    key_raw[...] = raw[:, heads_width : heads_width + key_width].astype(BF16).astype(F32)
    value_ref[...] = raw[:, heads_width + key_width :].astype(BF16)
    query_ref[...] = head_forward(
        query_raw[...], gain_query[...], cosine_ref[...], sine_ref[...], HEAD_WIDTH
    ).astype(BF16)
    key_ref[...] = head_forward(
        key_raw[...], gain_key[...], cosine_ref[...], sine_ref[...], HEAD_WIDTH
    ).astype(BF16)
    scale = HEAD_WIDTH ** (-0.5)
    group_heads = HEADS // KV
    mixed_parts = []
    head_total = heads_width // HEAD_WIDTH
    for head in range(head_total):
        group = head // group_heads
        group_lanes = slice(group * HEAD_WIDTH, (group + 1) * HEAD_WIDTH)
        scores = (
            matmul_nt(
                query_ref[:, head * HEAD_WIDTH : (head + 1) * HEAD_WIDTH],
                key_ref[:, group_lanes],
            )
            * scale
            + bias[...]
        )
        top = jnp.max(scores, axis=-1, keepdims=True)
        exponent = jnp.exp(scores - top)
        total = jnp.sum(exponent, axis=-1, keepdims=True)
        probs = (exponent * (1.0 / total)).astype(BF16)
        mixed_parts.append(
            jnp.dot(probs, value_ref[:, group_lanes], preferred_element_type=F32)
        )
        totals_ref[:, head : head + 1] = top + jnp.log(total)
        if head % 2 == 1:
            mixed_ref[:, (head - 1) * HEAD_WIDTH : (head + 1) * HEAD_WIDTH] = (
                jnp.concatenate(mixed_parts, axis=1).astype(BF16)
            )
            mixed_parts = []
        if head == head_total // 2 - 1:
            gather_go(grad_links, grad_cores, 1)
    partial[...] = jnp.dot(mixed_ref[...], out_v[...], preferred_element_type=F32).astype(BF16)

    residual = input_ref[...].astype(F32) + sum4(
        partial, from_core, outgoing, from_x, tokens, sender, place
    )
    residual_ref[...] = residual
    for copy in row_copies:
        copy.wait_send()
    own[...] = normed(residual, gain_ffn[...]).astype(BF16)
    for part in range(3):
        rows, start = part_rows(tokens)[part], part_starts(tokens)[part]
        ffn_buf[pl.ds(spot(tokens, part, 0, 0, 0), rows), :] = own[pl.ds(start, rows), :]
    links, cores = gather16(tokens, ffn_buf, None, sender, ORDERS)
    gather_begin(links, cores)
    gather_go(grad_links, grad_cores, 2)
    gather_go(links, cores, 0)
    for copy in later_loads:
        copy.wait()
    for part in range(3):
        for step_copies in grad_cores[part]:
            for copy in step_copies:
                copy.wait_recv()
    grad_store = load(grad_buf, grad_all)
    gather_go(links, cores, 1)
    for part in range(3):
        for step_copies in cores[part][:3]:
            for copy in step_copies:
                copy.wait_recv()

    block = 2 * tokens

    def compute(index):
        rows = pl.ds(pl.multiple_of(index * block, block), block)
        values = ffn_buf[rows, :]
        gate = jnp.dot(values, gate_v[...], preferred_element_type=F32)
        up = jnp.dot(values, up_v[...], preferred_element_type=F32)
        hidden_grad = matmul_nt(grad_buf[rows, :], down_v[...])
        hidden, gate_grad, up_grad = silu_parts(gate, up, hidden_grad)
        hidden_ref[rows, :] = hidden.astype(BF16)
        pair_ref[rows, :units] = gate_grad.astype(BF16)
        pair_ref[rows, units:] = up_grad.astype(BF16)

    half = 8 * tokens
    first = load(ffn_buf.at[pl.ds(0, half)], ffn_all.at[pl.ds(0, half)])
    pl.loop(0, 4)(compute)
    gather_go(links, cores, 2)
    for part in range(3):
        for copy in cores[part][3]:
            copy.wait_recv()
    second = load(ffn_buf.at[pl.ds(half, half)], ffn_all.at[pl.ds(half, half)])
    pl.loop(4, 8)(compute)
    for part, order in enumerate(ORDERS):
        rows, start = part_rows(tokens)[part], part_starts(tokens)[part]
        for half_bit in range(2):
            for core in range(2):
                for index in range(4):
                    bits = (index % 2, index // 2, half_bit)
                    flips = tuple(name for name, bit in zip(order, bits) if bit)
                    row = ("z" in flips) * 2 + ("y" in flips)
                    names = tuple(n for n in flips if n == "x") + (("core",) if core else ())
                    target = row * 4 * tokens + place.column(names) * tokens + start
                    rows_ref[pl.ds(pl.multiple_of(target, 16), rows), :] = hidden_ref[
                        pl.ds(spot(tokens, part, half_bit, core, index), rows), :
                    ]
    for copy in (attn_store, grad_store, first, second):
        copy.wait()
    gather_sent(grad_links, grad_cores)
    gather_sent(links, cores)


GAIN_LINKS = ("core", "x", "y", "z", "far")


def swap_halves(values, head_width):
    width = values.shape[1]
    half = head_width // 2
    lane = lax.broadcasted_iota(jnp.int32, values.shape, 1)
    return jnp.where(
        lane % head_width < half,
        pltpu.roll(values, width - half, 1),
        pltpu.roll(values, half, 1),
    )


def head_means(values, head_width):
    width = values.shape[1]
    rows = lax.broadcasted_iota(jnp.int32, (width, width), 0) // head_width
    columns = lax.broadcasted_iota(jnp.int32, (width, width), 1) // head_width
    blocks = jnp.where(rows == columns, 1.0 / head_width, 0.0).astype(BF16)
    upper = values.astype(BF16)
    lower = (values - upper.astype(F32)).astype(BF16)
    return jnp.dot(upper, blocks, preferred_element_type=F32) + jnp.dot(
        lower, blocks, preferred_element_type=F32
    )


def widen(table, width):
    return jnp.concatenate([table] * (width // table.shape[1]), axis=1)


def head_back(grad, raw, gain, cosine, sine, head_width):
    width = grad.shape[1]
    back = grad * widen(cosine, width) - swap_halves(grad, head_width) * widen(sine, width)
    factor = lax.rsqrt(head_means(raw * raw, head_width) + EPSILON)
    unit = raw * factor
    scaled = gain * back
    result = factor * (scaled - unit * head_means(scaled * unit, head_width))
    return result, jnp.sum(back * unit, axis=0, keepdims=True)


def fold_heads(row, head_width):
    total = row[:, :128]
    for start in range(128, row.shape[1], 128):
        total = total + row[:, start : start + 128]
    return total + pltpu.roll(total, head_width, 1)


GAIN_LINKS = ("core", "x", "y", "z", "far")


def finish_kernel(
    low_all,
    out_w,
    query_w,
    key_w,
    value_w,
    down_w,
    attn_all,
    pair_all,
    hidden_all,
    ffn_all,
    grad_all,
    rows_all,
    pair_sent,
    down_came,
    mixed_ref,
    query_ref,
    key_ref,
    value_ref,
    query_raw,
    key_raw,
    totals_ref,
    cosine_ref,
    sine_ref,
    lengths_ref,
    gain_query,
    gain_key,
    gain_attn,
    input_ref,
    back_ref,
    ffn_gain_ref,
    residual_ref,
    layer_ref,
    input_grad_ref,
    qkv_out,
    out_out,
    gate_out,
    up_out,
    down_out,
    gains_ref,
    low,
    out_v,
    qkv_w,
    attn_in,
    pair,
    hidden,
    columns_v,
    down_arrived,
    bias,
    mixed_grad,
    qkv_low,
    qkv_peer,
    attn_peer,
    out_sent,
    out_came,
    out_near_came,
    out_far_came,
    qkv_near,
    qkv_near_came,
    qkv_far,
    qkv_far_came,
    pair_came,
    pair_block,
    pair_blocks_came,
    down_block,
    down_blocks_came,
    rows_came,
    from_core,
    outgoing,
    from_x,
    sums,
    came,
    send_sems,
    recv_sems,
    local_sems,
):
    tokens, width = input_ref.shape
    length = 4 * tokens
    units = hidden.shape[1]
    heads_width = query_ref.shape[1]
    key_width = key_ref.shape[1]
    head_width = HEAD_WIDTH
    group_heads = HEADS // KV
    groups = key_width // head_width
    block = width // 8
    place = Place()
    y, z, far = place.at["y"], place.at["z"], place.far
    sender = Sender(place, send_sems, recv_sems)
    local_used = [0]

    def load(source, target):
        copy = pltpu.make_async_copy(source, target, local_sems.at[local_used[0]])
        local_used[0] += 1
        copy.start()
        return copy

    def lanes(start, count):
        return pl.ds(pl.multiple_of(start, count), count)

    def quarter_lanes(names):
        return lanes(place.quarter(names) * block, block)

    def own_half(source):
        return source.at[:, lanes(far * (width // 2), width // 2)]

    enter(place, GAIN_LINKS + (("y", "z"),))
    low_load = load(low_all, low)
    out_load = load(out_w, out_v)
    attn_load = load(attn_all, attn_in)
    hidden_load = load(hidden_all, hidden)
    grad_load = load(own_half(grad_all), columns_v)
    down_load = load(down_came, down_arrived)
    pair_load = load(pair_all, pair)
    qkv_loads = [
        load(query_w, qkv_w.at[:, pl.ds(0, heads_width)]),
        load(key_w, qkv_w.at[:, pl.ds(heads_width, key_width)]),
        load(value_w, qkv_w.at[:, pl.ds(heads_width + key_width, key_width)]),
    ]
    bulk = [sender.copy(pair_sent.at[turn], pair_came.at[turn], "far") for turn in range(4)]
    bulk[0].start()
    bulk[1].start()
    row_copies = [
        sender.copy(
            rows_all.at[pl.ds(offset * length, length)], rows_came.at[offset - 1], names
        )
        for offset, names in ((1, ("y",)), (2, ("z",)), (3, ("y", "z")))
    ]
    attn_copies = [
        sender.copy(
            attn_all.at[:, lanes((index * 2 + 1 - y) * block, block)],
            attn_peer.at[:, pl.ds(index * block, block)],
            "y",
        )
        for index in range(4)
    ]
    for copy in attn_copies + row_copies:
        copy.start()
    bulk[2].start()
    bulk[3].start()

    low_load.wait()
    out_load.wait()
    mixed_grad[...] = matmul_nt(low[...], out_v[...]).astype(BF16)
    for index in range(4):
        out_sent[index] = matmul_tn(
            mixed_ref[...], low[:, lanes((index * 2 + 1 - y) * block, block)]
        ).astype(BF16)
    out_copy = sender.copy(out_sent, out_came, "y")
    out_copy.start()
    ids_down, ids_across, unused_angles = document_tables(
        lengths_ref, jnp.ones((1, 128), F32), length
    )
    bias[...] = document_bias(ids_down, ids_across, length)

    scale = head_width ** (-0.5)
    key_parts, value_parts, query_gain = [], [], None
    peer_copies = []
    down_copies = []

    def spread_down():
        hidden_load.wait()
        grad_load.wait()
        down_load.wait()
        for turn, names in enumerate(QUARTERS):
            total = matmul_tn(hidden[...], columns_v[:, quarter_lanes(names)]) + down_arrived[
                pl.ds(turn * units, units), :
            ].astype(F32)
            if names:
                down_block[turn] = total.astype(BF16)
                copy = sender.copy(down_block.at[turn], down_blocks_came.at[turn], names)
                copy.start()
                down_copies.append(copy)
            else:
                down_out[pl.ds(pl.multiple_of(place.quarter() * units, units), units), :] = total

    for group in range(groups):
        group_lanes = slice(group * head_width, (group + 1) * head_width)
        key, value = key_ref[:, group_lanes], value_ref[:, group_lanes]
        key_grad = jnp.zeros((length, head_width), F32)
        value_grad = jnp.zeros((length, head_width), F32)
        query_parts = []
        for head in range(group * group_heads, (group + 1) * group_heads):
            head_lanes = slice(head * head_width, (head + 1) * head_width)
            query, grad = query_ref[:, head_lanes], mixed_grad[:, head_lanes]
            scores = matmul_nt(query, key) * scale + bias[...]
            probs = jnp.exp(scores - totals_ref[:, head : head + 1])
            prob_grad = matmul_nt(grad, value)
            value_grad = value_grad + matmul_tn(probs.astype(BF16), grad)
            centre = jnp.sum(probs * prob_grad, axis=-1, keepdims=True)
            score_grad = (probs * (prob_grad - centre)).astype(BF16)
            query_parts.append(jnp.dot(score_grad, key, preferred_element_type=F32) * scale)
            key_grad = key_grad + matmul_tn(score_grad, query) * scale
        key_parts.append(key_grad)
        value_parts.append(value_grad)
        wide = slice(group * group_heads * head_width, (group + 1) * group_heads * head_width)
        query_grad, gain_part = head_back(
            jnp.concatenate(query_parts, axis=1),
            query_raw[:, wide],
            gain_query[:, wide],
            cosine_ref[...],
            sine_ref[...],
            head_width,
        )
        gain_part = fold_heads(gain_part, head_width)
        query_gain = gain_part if query_gain is None else query_gain + gain_part
        qkv_low[:, wide] = query_grad.astype(BF16)
        peer_copies.append(sender.copy(qkv_low.at[:, wide], qkv_peer.at[:, wide], "y"))
        peer_copies[-1].start()
        if group == 0:
            spread_down()
    own_load = load(own_half(ffn_all), columns_v)
    key_back, key_gain = head_back(
        jnp.concatenate(key_parts, axis=1),
        key_raw[...],
        gain_key[...],
        cosine_ref[...],
        sine_ref[...],
        head_width,
    )
    key_gain = fold_heads(key_gain, head_width)
    qkv_low[:, heads_width : heads_width + key_width] = key_back.astype(BF16)
    qkv_low[:, heads_width + key_width :] = jnp.concatenate(value_parts, axis=1).astype(BF16)
    tail = slice(heads_width, heads_width + 2 * key_width)
    peer_copies.append(sender.copy(qkv_low.at[:, tail], qkv_peer.at[:, tail], "y"))
    peer_copies[-1].start()

    partial = out_v
    for copy in qkv_loads:
        copy.wait()

    def part_of(index):
        columns = lanes(index * 512, 512)
        partial[:, columns] = matmul_nt(qkv_low[...], qkv_w[columns, :]).astype(BF16)

    pl.loop(0, width // 512)(part_of)

    out_copy.wait()
    out_near, out_far = out_sent, out_sent.at[2]

    def out_total(index):
        return matmul_tn(
            mixed_ref[...], low[:, lanes((index * 2 + y) * block, block)]
        ) + out_came[index].astype(F32)

    near_copies = []
    for turn, half in enumerate((1 - far, far)):
        out_near[turn] = out_total(half * 2 + 1 - z).astype(BF16)
        copy = sender.copy(out_near.at[turn], out_near_came.at[turn], "z")
        copy.start()
        near_copies.append(copy)

    attn_grad = sum4(partial, from_core.at[0], outgoing.at[0], from_x.at[0], tokens, sender, place)
    back, attn_gain = norm_back(input_ref[...].astype(F32), gain_attn[...], attn_grad)
    input_grad_ref[...] = (back + back_ref[...]).astype(BF16)
    sums[0, :, :width] = attn_gain
    sums[0, :, width : 2 * width] = ffn_gain_ref[...]
    lane = lax.broadcasted_iota(jnp.int32, (1, 128), 1)
    sums[0, :, 2 * width :] = jnp.where(lane < head_width, query_gain, key_gain)

    attn_load.wait()
    for copy in attn_copies + peer_copies:
        copy.wait_recv()

    def qkv_total(index):
        return matmul_tn(
            attn_in[:, lanes((index * 2 + y) * block, block)], qkv_low[...]
        ) + matmul_tn(attn_peer[:, lanes(index * block, block)], qkv_peer[...])

    for turn, half in enumerate((1 - far, far)):
        qkv_near[turn] = qkv_total(half * 2 + 1 - z).astype(BF16)
        copy = sender.copy(qkv_near.at[turn], qkv_near_came.at[turn], "z")
        copy.start()
        near_copies.append(copy)
    near_copies[0].wait_recv()
    out_far[...] = (out_total((1 - far) * 2 + z) + out_near_came[0].astype(F32)).astype(BF16)
    out_far_copy = sender.copy(out_far, out_far_came, "far")
    out_far_copy.start()
    near_copies[2].wait_recv()
    qkv_far[...] = (qkv_total((1 - far) * 2 + z) + qkv_near_came[0].astype(F32)).astype(BF16)
    qkv_far_copy = sender.copy(qkv_far, qkv_far_came, "far")
    qkv_far_copy.start()
    near_copies[1].wait_recv()
    out_out[...] = out_total(far * 2 + z) + out_near_came[1].astype(F32)
    near_copies[3].wait_recv()
    qkv_out[...] = qkv_total(far * 2 + z) + qkv_near_came[1].astype(F32)

    own_load.wait()
    pair_load.wait()
    pair_copies = []

    def spread_pair(turn):
        names = QUARTERS[turn]
        bulk[turn].wait_recv()
        total = matmul_tn(columns_v[:, quarter_lanes(names)], pair[...]) + pair_came[
            turn
        ].astype(F32)
        if names:
            pair_block[turn] = total.astype(BF16)
            copy = sender.copy(pair_block.at[turn], pair_blocks_came.at[turn], names)
            copy.start()
            pair_copies.append(copy)
        else:
            mine = lanes(place.quarter() * units, units)
            gate_out[:, mine] = total[:, :units]
            up_out[:, mine] = total[:, units:]

    spread_pair(0)

    for copy in row_copies:
        copy.wait_recv()
    partial = low
    offsets = ((), ("y",), ("z",), ("y", "z"))
    own_rows = load(rows_all.at[pl.ds(0, length)], rows_came.at[3])
    own_rows.wait()
    for chunk in range(width // 512):
        columns = pl.ds(chunk * 512, 512)
        loads = [
            load(
                down_w.at[
                    pl.ds(pl.multiple_of(place.quarter(names) * units, units), units), columns
                ],
                qkv_w.at[pl.ds(offset * units, units), pl.ds(0, 512)],
            )
            for offset, names in enumerate(offsets)
        ]
        total = None
        for offset in range(4):
            loads[offset].wait()
            term = jnp.dot(
                rows_came[(offset + 3) % 4],
                qkv_w[pl.ds(offset * units, units), pl.ds(0, 512)],
                preferred_element_type=F32,
            )
            total = term if total is None else total + term
        partial[:, columns] = total.astype(BF16)
    spread_pair(1)
    layer_ref[...] = (
        residual_ref[...]
        + sum4(partial, from_core.at[1], outgoing.at[1], from_x.at[1], tokens, sender, place)
    ).astype(BF16)
    for turn, copy in enumerate(down_copies):
        copy.wait_recv()
        start = pl.multiple_of(place.quarter(QUARTERS[turn]) * units, units)
        down_out[pl.ds(start, units), :] = down_blocks_came[turn].astype(F32)
    spread_pair(2)
    spread_pair(3)
    for turn, copy in enumerate(pair_copies):
        copy.wait_recv()
        columns = lanes(place.quarter(QUARTERS[turn]) * units, units)
        gate_out[:, columns] = pair_blocks_came[turn, :, :units].astype(F32)
        up_out[:, columns] = pair_blocks_came[turn, :, units:].astype(F32)
    for step, name in enumerate(GAIN_LINKS):
        copy = sender.copy(sums.at[step], came.at[step], name)
        copy.start()
        copy.wait()
        sums[step + 1] = sums[step] + came[step]
    gains_ref[...] = sums[len(GAIN_LINKS)]
    out_far_copy.wait_recv()
    out_out[...] += out_far_came[...].astype(F32)
    qkv_far_copy.wait_recv()
    qkv_out[...] += qkv_far_came[...].astype(F32)
    for copy in (
        bulk
        + row_copies
        + attn_copies
        + peer_copies
        + near_copies
        + down_copies
        + pair_copies
        + [out_far_copy, qkv_far_copy]
    ):
        copy.wait_send()


IN_VMEM = pl.BlockSpec(memory_space=pltpu.VMEM)
ANYWHERE = pl.BlockSpec(memory_space=pl.ANY)
MIB = 1 << 20


def shape_of(shape, dtype):
    return jax.ShapeDtypeStruct(shape, dtype)


def call(kernel, number, ins, outs, out_specs, scratch, limit, operands, flops, moved):
    return pl.pallas_call(
        kernel,
        out_shape=outs,
        in_specs=ins,
        out_specs=out_specs,
        scratch_shapes=scratch,
        cost_estimate=pl.CostEstimate(
            flops=flops, bytes_accessed=moved, transcendentals=0
        ),
        compiler_params=pltpu.CompilerParams(
            collective_id=number, has_side_effects=True, vmem_limit_bytes=limit
        ),
    )(*operands)


def copies(count):
    return [pltpu.SemaphoreType.DMA((count,)), pltpu.SemaphoreType.DMA((count,))]


def forward_step(
    doc_lengths,
    layer_input,
    gains,
    out_grad,
    weights,
):
    tokens, width = layer_input.shape
    heads_width, key_width = weights[0].shape[1], weights[1].shape[1]
    units = weights[4].shape[1] // 4
    length, everyone = 4 * tokens, 16 * tokens
    exponents = -np.arange(0, HEAD_WIDTH, 2, dtype=np.float32) / HEAD_WIDTH
    frequency = np.tile((ROPE_BASE**exponents).astype(np.float32), 128 * 2 // HEAD_WIDTH)
    gain_attn, gain_ffn, gain_query, gain_key = gains
    v = pltpu.VMEM
    return call(
        forward_kernel,
        1,
        [pl.BlockSpec(memory_space=pltpu.SMEM)] + [IN_VMEM] * 6 + [ANYWHERE] * 8,
        [
            shape_of((length, width), BF16),
            shape_of((length, heads_width), BF16),
            shape_of((length, heads_width), BF16),
            shape_of((length, key_width), BF16),
            shape_of((length, key_width), BF16),
            shape_of((length, heads_width), F32),
            shape_of((length, key_width), F32),
            shape_of((length, 128), F32),
            shape_of((length, 128), F32),
            shape_of((length, 128), F32),
            shape_of((tokens, width), F32),
            shape_of((everyone, width), BF16),
            shape_of((everyone, width), BF16),
            shape_of((everyone, units), BF16),
            shape_of((everyone, 2 * units), BF16),
            shape_of((everyone, units), BF16),
        ],
        [ANYWHERE] + [IN_VMEM] * 10 + [ANYWHERE] * 2 + [IN_VMEM] * 3,
        [
            v((tokens, width), BF16),
            v((length, width), BF16),
            v((width, heads_width + 2 * key_width), BF16),
            v((heads_width, width), BF16),
            v((length, length), F32),
            v((length, width), BF16),
            v((2, tokens, width), BF16),
            v((tokens, width), BF16),
            v((tokens, width), BF16),
            v((everyone, width), BF16),
            v((everyone, width), BF16),
            v((width, units), BF16),
            v((width, units), BF16),
            v((units, width), BF16),
        ]
        + copies(64)
        + [pltpu.SemaphoreType.DMA((16,))],
        61 * MIB,
        (
            doc_lengths,
            layer_input,
            gain_attn[None, :],
            gain_ffn[None, :],
            jnp.tile(gain_query, heads_width // HEAD_WIDTH)[None, :],
            jnp.tile(gain_key, key_width // HEAD_WIDTH)[None, :],
            frequency[None, :],
            out_grad,
        )
        + weights,
        8 * everyone * width * units,
        200 * 10**6,
    )


def back_step(pair, w_gate, w_up, residual, gain_ffn, out_grad, hidden, ffn_all, grad_all):
    tokens, width = residual.shape
    units = pair.shape[1] // 2
    everyone = 16 * tokens
    return call(
        back_kernel,
        2,
        [IN_VMEM, ANYWHERE, ANYWHERE] + [IN_VMEM] * 4 + [ANYWHERE] * 2,
        [
            shape_of((tokens, width), F32),
            shape_of((1, width), F32),
            shape_of((4 * tokens, width), BF16),
            shape_of((4 * units, width // 8), BF16),
            shape_of((4, width // 8, 2 * units), BF16),
        ],
        [IN_VMEM, IN_VMEM, ANYWHERE, ANYWHERE, IN_VMEM],
        [
            pltpu.VMEM((width, 2 * units), BF16),
            pltpu.VMEM((4, units, width // 8), BF16),
            pltpu.VMEM((everyone, width // 2), BF16),
            pltpu.VMEM((everyone, width // 2), BF16),
            pltpu.VMEM((everyone, width), BF16),
            pltpu.VMEM((everyone // 2, width), BF16),
            pltpu.VMEM((everyone // 4, width), BF16),
            pltpu.VMEM((everyone // 8, width), BF16),
            pltpu.VMEM((everyone // 16, width), BF16),
            pltpu.VMEM((tokens, width), BF16),
        ]
        + copies(22)
        + [pltpu.SemaphoreType.DMA((5,))],
        58 * MIB,
        (pair, w_gate, w_up, residual, gain_ffn[None, :], out_grad, hidden, ffn_all, grad_all),
        8 * everyone * width * units,
        200 * 10**6,
    )


def finish_step(big, small, tokens, width, units, heads_width, key_width):
    length, everyone, block = 4 * tokens, 16 * tokens, width // 8
    qkv_width = heads_width + 2 * key_width
    gains = 2 * width + 128
    v = pltpu.VMEM
    return call(
        finish_kernel,
        3,
        [ANYWHERE] * len(big)
        + [IN_VMEM] * 9
        + [pl.BlockSpec(memory_space=pltpu.SMEM)]
        + [IN_VMEM] * (len(small) - 10),
        [
            shape_of((tokens, width), BF16),
            shape_of((tokens, width), BF16),
            shape_of((block, qkv_width), F32),
            shape_of((heads_width, block), F32),
            shape_of((block, 4 * units), F32),
            shape_of((block, 4 * units), F32),
            shape_of((4 * units, block), F32),
            shape_of((1, gains), F32),
        ],
        [IN_VMEM] * 8,
        [
            v((length, width), BF16),
            v((heads_width, width), BF16),
            v((width, qkv_width), BF16),
            v((length, width), BF16),
            v((everyone, 2 * units), BF16),
            v((everyone, units), BF16),
            v((everyone, width // 2), BF16),
            v((4 * units, block), BF16),
            v((length, length), F32),
            v((length, heads_width), BF16),
            v((length, qkv_width), BF16),
            v((length, qkv_width), BF16),
            v((length, width // 2), BF16),
            v((4, heads_width, block), BF16),
            v((4, heads_width, block), BF16),
            v((2, heads_width, block), BF16),
            v((heads_width, block), BF16),
            v((2, block, qkv_width), BF16),
            v((2, block, qkv_width), BF16),
            v((block, qkv_width), BF16),
            v((block, qkv_width), BF16),
            v((4, block, 2 * units), BF16),
            v((3, block, 2 * units), BF16),
            v((3, block, 2 * units), BF16),
            v((3, units, block), BF16),
            v((3, units, block), BF16),
            v((4, length, units), BF16),
            v((2, 2, tokens, width), BF16),
            v((2, tokens, width), BF16),
            v((2, tokens, width), BF16),
            v((6, 1, gains), F32),
            v((5, 1, gains), F32),
        ]
        + copies(40)
        + [pltpu.SemaphoreType.DMA((32,))],
        61 * MIB,
        big + small,
        8 * everyone * width * units,
        400 * 10**6,
    )


def per_device_sixteen(
    layer_input,
    doc_lengths,
    w_query,
    w_key,
    w_value,
    w_out,
    w_gate,
    w_up,
    w_down,
    gain_attn,
    gain_ffn,
    gain_query,
    gain_key,
    out_grad,
):
    outs = forward_step(
        doc_lengths,
        layer_input,
        (gain_attn, gain_ffn, gain_query, gain_key),
        out_grad,
        (w_query, w_key, w_value, w_out, w_gate, w_up, w_down),
    )
    attn_in, saved = outs[0], tuple(outs[1:10])
    residual, ffn_all, grad_all, hidden, pair, hidden_rows = outs[10:]
    residual_grad, gain_ffn_part, res_low, down_came, pair_sent = back_step(
        pair, w_gate, w_up, residual, gain_ffn, out_grad, hidden, ffn_all, grad_all
    )
    heads_width, key_width = w_query.shape[1], w_key.shape[1]
    layer_out, input_grad, grad_qkv, grad_out, grad_gate, grad_up, grad_down, gains = finish_step(
        (
            res_low,
            w_out,
            w_query,
            w_key,
            w_value,
            w_down,
            attn_in,
            pair,
            hidden,
            ffn_all,
            grad_all,
            hidden_rows,
            pair_sent,
            down_came,
        ),
        saved
        + (
            doc_lengths,
            jnp.tile(gain_query, heads_width // HEAD_WIDTH)[None, :],
            jnp.tile(gain_key, key_width // HEAD_WIDTH)[None, :],
            gain_attn[None, :],
            layer_input,
            residual_grad,
            gain_ffn_part,
            residual,
        ),
        layer_input.shape[0],
        layer_input.shape[1],
        hidden.shape[1],
        heads_width,
        key_width,
    )
    width = layer_input.shape[1]
    return (
        layer_out,
        input_grad,
        grad_qkv[:, :heads_width],
        grad_qkv[:, heads_width : heads_width + key_width],
        grad_qkv[:, heads_width + key_width :],
        grad_out,
        grad_gate,
        grad_up,
        grad_down,
        gains[0, :width],
        gains[0, width : 2 * width],
        gains[0, 2 * width : 2 * width + 64],
        gains[0, 2 * width + 64 :],
    )


def solution(mesh):
    in_specs = (
        P(("dp", "tensor"), None),
        P("dp", None),
        P(None, "tensor"),
        P(None, "tensor"),
        P(None, "tensor"),
        P("tensor", None),
        P(None, "tensor"),
        P(None, "tensor"),
        P("tensor", None),
        P(),
        P(),
        P(),
        P(),
        P(("dp", "tensor"), None),
    )
    out_specs = (
        P(("dp", "tensor"), None),
        P(("dp", "tensor"), None),
        P("dp", "tensor"),
        P("dp", "tensor"),
        P("dp", "tensor"),
        P("tensor", "dp"),
        P("dp", "tensor"),
        P("dp", "tensor"),
        P("tensor", "dp"),
        P(),
        P(),
        P(),
        P(),
    )
    sixteen = mesh.shape["dp"] == 8 and mesh.shape["tensor"] == 4
    return jax.shard_map(
        per_device_sixteen if sixteen else per_device, mesh=mesh, in_specs=in_specs, out_specs=out_specs, check_vma=False
    )
```

```python
import jax
import jax.numpy as jnp
import numpy as np
from jax import lax
from jax.experimental import pallas as pl
from jax.experimental.pallas import tpu as pltpu
from jax.sharding import PartitionSpec as P

HEADS = 32
KV = 8


EPSILON = 1e-06
ROPE_BASE = 10000.0
MASKED = -1e30


def norm_gain(row_block, gain_vec):
    factor = lax.rsqrt(jnp.mean(row_block * row_block, axis=-1, keepdims=True) + EPSILON)
    return row_block * factor * gain_vec


def rotate(vector, cosine, sine_table):
    half_width = vector.shape[-1] // 2
    first = vector[..., :half_width]
    second = vector[..., half_width:]
    return jnp.concatenate(
        [first * cosine - second * sine_table, second * cosine + first * sine_table], axis=-1
    )


def head_prep(raw_proj, gain_vec, cosine, sine_table):
    head_width = gain_vec.shape[0]
    per_head = raw_proj.reshape(raw_proj.shape[0], raw_proj.shape[1] // head_width, head_width)
    return rotate(norm_gain(per_head, gain_vec), cosine[:, None, :], sine_table[:, None, :])


def doc_layout(lengths, length):
    doc_ends = jnp.cumsum(lengths)
    places = jnp.arange(length, dtype=jnp.int32)
    passed_end = (places[:, None] >= doc_ends[None, :]).astype(jnp.int32)
    doc_ids = jnp.sum(passed_end, axis=1)
    starts = jnp.sum(passed_end * lengths[None, :], axis=1)
    return (doc_ids, places, places - starts)


def rope_tables(offsets, head_width):
    frequency = ROPE_BASE ** (-jnp.arange(0, head_width, 2, dtype=jnp.float32) / head_width)
    angles = offsets.astype(jnp.float32)[:, None] * frequency[None, :]
    return (jnp.cos(angles), jnp.sin(angles))


def swiglu(gate_proj, up_proj):
    return jax.nn.silu(gate_proj) * up_proj


def matmul_nt(left_mat, right_mat):
    return lax.dot_general(
        left_mat, right_mat, (((1,), (1,)), ((), ())), preferred_element_type=jnp.float32
    )


def matmul_tn(left_mat, right_mat):
    return lax.dot_general(
        left_mat, right_mat, (((0,), (0,)), ((), ())), preferred_element_type=jnp.float32
    )


def per_device(
    layer_input,
    doc_lengths,
    w_query,
    w_key,
    w_value,
    w_out,
    w_gate,
    w_up,
    w_down,
    gain_attn,
    gain_ffn,
    gain_query,
    gain_key,
    out_grad,
):
    tok_rows = layer_input.shape[0]
    head_width = gain_query.shape[0]
    tensor_count = lax.axis_size("tensor")
    length = tok_rows * tensor_count
    per_dev = w_query.shape[1] // head_width
    groups_dev = w_key.shape[1] // head_width
    input_f32 = layer_input.astype(jnp.float32)
    doc_ids, places, offsets = doc_layout(doc_lengths[0], length)
    cosine, sine_table = rope_tables(offsets, head_width)
    attn_in = lax.all_gather(
        norm_gain(input_f32, gain_attn).astype(jnp.bfloat16), "tensor", axis=0, tiled=True
    )
    query_raw = jnp.dot(attn_in, w_query, preferred_element_type=jnp.float32)
    key_raw = jnp.dot(attn_in, w_key, preferred_element_type=jnp.float32).astype(jnp.bfloat16)
    value_raw = jnp.dot(attn_in, w_value, preferred_element_type=jnp.float32).astype(jnp.bfloat16)
    key_f32 = key_raw.astype(jnp.float32)
    queries = head_prep(query_raw, gain_query, cosine, sine_table).astype(jnp.bfloat16)
    key_rot = head_prep(key_f32, gain_key, cosine, sine_table).astype(jnp.bfloat16)
    local_heads = jnp.arange(per_dev, dtype=jnp.int32)
    group_pick = (
        local_heads[:, None] // (HEADS // KV) == jnp.arange(groups_dev, dtype=jnp.int32)[None, :]
    ).astype(jnp.float32)
    pick_low = group_pick.astype(jnp.bfloat16)
    key_heads = jnp.einsum(
        "lgd,hg->lhd", key_rot, pick_low, preferred_element_type=jnp.float32
    ).astype(jnp.bfloat16)
    value_heads = jnp.einsum(
        "lgd,hg->lhd",
        value_raw.reshape(length, groups_dev, head_width),
        pick_low,
        preferred_element_type=jnp.float32,
    ).astype(jnp.bfloat16)
    block_rows = min(512, length)
    block_count = length // block_rows
    score_scale = head_width ** (-0.5)

    def block_scores(block_num):
        row_begin = block_num * block_rows
        query_block = lax.dynamic_slice_in_dim(queries, row_begin, block_rows, 0)
        ids_block = lax.dynamic_slice_in_dim(doc_ids, row_begin, block_rows, 0)
        places_block = lax.dynamic_slice_in_dim(places, row_begin, block_rows, 0)
        scores = (
            jnp.einsum("qhd,khd->hqk", query_block, key_heads, preferred_element_type=jnp.float32)
            * score_scale
        )
        allowed = (ids_block[:, None] == doc_ids[None, :]) & (
            places[None, :] <= places_block[:, None]
        )
        return (query_block, jnp.where(allowed[None], scores, MASKED))

    def forward_block(block_num):
        query_block, scores = block_scores(block_num)
        row_top = jnp.max(scores, axis=-1, keepdims=True)
        exponent = jnp.exp(scores - row_top)
        row_total = jnp.sum(exponent, axis=-1, keepdims=True)
        probabilities = (exponent / row_total).astype(jnp.bfloat16)
        mixed_block = jnp.einsum(
            "hqk,khd->qhd", probabilities, value_heads, preferred_element_type=jnp.float32
        )
        return (mixed_block, row_top + jnp.log(row_total))

    mixed_all, log_totals = lax.map(forward_block, jnp.arange(block_count, dtype=jnp.int32))
    attn_mixed = mixed_all.reshape(length, per_dev * head_width).astype(jnp.bfloat16)
    residual = input_f32 + lax.psum_scatter(
        jnp.dot(attn_mixed, w_out, preferred_element_type=jnp.float32).astype(jnp.bfloat16),
        "tensor",
        scatter_dimension=0,
        tiled=True,
    ).astype(jnp.float32)
    ffn_in = lax.all_gather(
        norm_gain(residual, gain_ffn).astype(jnp.bfloat16), "tensor", axis=0, tiled=True
    )
    gate_proj = jnp.dot(ffn_in, w_gate, preferred_element_type=jnp.float32)
    up_proj = jnp.dot(ffn_in, w_up, preferred_element_type=jnp.float32)
    hidden = swiglu(gate_proj, up_proj).astype(jnp.bfloat16)
    layer_out = (
        residual
        + lax.psum_scatter(
            jnp.dot(hidden, w_down, preferred_element_type=jnp.float32).astype(jnp.bfloat16),
            "tensor",
            scatter_dimension=0,
            tiled=True,
        ).astype(jnp.float32)
    ).astype(jnp.bfloat16)
    grad_rows = lax.all_gather(out_grad, "tensor", axis=0, tiled=True)
    hidden_grad = matmul_nt(grad_rows, w_down)
    grad_down = matmul_tn(hidden, grad_rows)
    unused_value, swiglu_back = jax.vjp(swiglu, gate_proj, up_proj)
    gate_grad, up_grad = swiglu_back(hidden_grad)
    gate_grad = gate_grad.astype(jnp.bfloat16)
    up_grad = up_grad.astype(jnp.bfloat16)
    grad_gate = matmul_tn(ffn_in, gate_grad)
    grad_up = matmul_tn(ffn_in, up_grad)
    ffn_in_grad = lax.psum_scatter(
        (matmul_nt(gate_grad, w_gate) + matmul_nt(up_grad, w_up)).astype(jnp.bfloat16),
        "tensor",
        scatter_dimension=0,
        tiled=True,
    ).astype(jnp.float32)
    unused_norm, ffn_norm_back = jax.vjp(norm_gain, residual, gain_ffn)
    residual_grad, gain_ffn_grad = ffn_norm_back(ffn_in_grad)
    residual_grad = residual_grad + out_grad.astype(jnp.float32)
    res_low = lax.all_gather(residual_grad.astype(jnp.bfloat16), "tensor", axis=0, tiled=True)
    mixed_grad = matmul_nt(res_low, w_out).astype(jnp.bfloat16).reshape(length, per_dev, head_width)
    grad_out = matmul_tn(attn_mixed, res_low)

    def backward_block(running, block_num):
        key_acc, value_acc = running
        query_block, scores = block_scores(block_num)
        probabilities = jnp.exp(scores - log_totals[block_num])
        grad_block = lax.dynamic_slice_in_dim(mixed_grad, block_num * block_rows, block_rows, 0)
        prob_grad = jnp.einsum(
            "qhd,khd->hqk", grad_block, value_heads, preferred_element_type=jnp.float32
        )
        value_acc = value_acc + jnp.einsum(
            "hqk,qhd->khd",
            probabilities.astype(jnp.bfloat16),
            grad_block,
            preferred_element_type=jnp.float32,
        )
        centre = jnp.sum(probabilities * prob_grad, axis=-1, keepdims=True)
        score_grad = (probabilities * (prob_grad - centre)).astype(jnp.bfloat16)
        query_part = (
            jnp.einsum("hqk,khd->qhd", score_grad, key_heads, preferred_element_type=jnp.float32)
            * score_scale
        )
        key_acc = (
            key_acc
            + jnp.einsum(
                "hqk,qhd->khd", score_grad, query_block, preferred_element_type=jnp.float32
            )
            * score_scale
        )
        return ((key_acc, value_acc), query_part)

    zeros_init = jnp.zeros((length, per_dev, head_width), jnp.float32)
    (key_acc, value_acc), query_parts = lax.scan(
        backward_block, (zeros_init, zeros_init), jnp.arange(block_count, dtype=jnp.int32)
    )
    query_rot_grad = query_parts.reshape(length, per_dev, head_width)
    unused_query, query_back = jax.vjp(
        lambda raw_proj, gain_vec: head_prep(raw_proj, gain_vec, cosine, sine_table),
        query_raw,
        gain_query,
    )
    query_raw_grad, gain_query_grad = query_back(query_rot_grad)
    query_low = query_raw_grad.astype(jnp.bfloat16)
    key_group_grad = jnp.einsum("lhd,hg->lgd", key_acc, group_pick, precision=lax.Precision.HIGHEST)
    value_group_grad = jnp.einsum(
        "lhd,hg->lgd", value_acc, group_pick, precision=lax.Precision.HIGHEST
    )
    unused_key, key_back = jax.vjp(
        lambda raw_proj, gain_vec: head_prep(raw_proj, gain_vec, cosine, sine_table),
        key_f32,
        gain_key,
    )
    key_raw_grad, gain_key_grad = key_back(key_group_grad)
    key_low = key_raw_grad.astype(jnp.bfloat16)
    value_low = value_group_grad.reshape(length, groups_dev * head_width).astype(jnp.bfloat16)
    grad_query = matmul_tn(attn_in, query_low)
    grad_key = matmul_tn(attn_in, key_low)
    grad_value = matmul_tn(attn_in, value_low)
    attn_in_grad = lax.psum_scatter(
        (
            matmul_nt(query_low, w_query)
            + matmul_nt(key_low, w_key)
            + matmul_nt(value_low, w_value)
        ).astype(jnp.bfloat16),
        "tensor",
        scatter_dimension=0,
        tiled=True,
    ).astype(jnp.float32)
    unused_attn, attn_norm_back = jax.vjp(norm_gain, input_f32, gain_attn)
    input_part, gain_attn_grad = attn_norm_back(attn_in_grad)
    input_grad = (input_part + residual_grad).astype(jnp.bfloat16)
    reduced = (
        lax.psum_scatter(
            grad_query.astype(jnp.bfloat16), "dp", scatter_dimension=0, tiled=True
        ).astype(jnp.float32),
        lax.psum_scatter(
            grad_key.astype(jnp.bfloat16), "dp", scatter_dimension=0, tiled=True
        ).astype(jnp.float32),
        lax.psum_scatter(
            grad_value.astype(jnp.bfloat16), "dp", scatter_dimension=0, tiled=True
        ).astype(jnp.float32),
        lax.psum_scatter(
            grad_out.astype(jnp.bfloat16), "dp", scatter_dimension=1, tiled=True
        ).astype(jnp.float32),
        lax.psum_scatter(
            grad_gate.astype(jnp.bfloat16), "dp", scatter_dimension=0, tiled=True
        ).astype(jnp.float32),
        lax.psum_scatter(
            grad_up.astype(jnp.bfloat16), "dp", scatter_dimension=0, tiled=True
        ).astype(jnp.float32),
        lax.psum_scatter(
            grad_down.astype(jnp.bfloat16), "dp", scatter_dimension=1, tiled=True
        ).astype(jnp.float32),
    )
    gain_sums = lax.psum(
        (gain_attn_grad, gain_ffn_grad, gain_query_grad, gain_key_grad), ("dp", "tensor")
    )
    return (
        layer_out,
        input_grad,
        reduced[0],
        reduced[1],
        reduced[2],
        reduced[3],
        reduced[4],
        reduced[5],
        reduced[6],
        gain_sums[0],
        gain_sums[1],
        gain_sums[2],
        gain_sums[3],
    )


MESH_ID = pl.DeviceIdType.MESH
ORDERS = (("x", "y", "z"), ("y", "z", "x"), ("z", "x", "y"))
LINKS = ("x", "y", "z", "core")
GRAD_PATHS = (("x", "y", "z"), ("x", "z", "y"), ("y", "z", "x"))
HEAD_WIDTH = 64
QUARTERS = (("y", "z"), ("y",), ("z",), ())
F32 = jnp.float32
BF16 = jnp.bfloat16


class Place:
    def __init__(self):
        row, column = lax.axis_index("dp"), lax.axis_index("tensor")
        self.far = row // 4
        self.at = {
            "z": (row // 2) % 2,
            "y": row % 2,
            "x": column // 2,
            "core": column % 2,
        }

    def flipped(self, names):
        return {
            name: 1 - value if name in names else value for name, value in self.at.items()
        }

    def device(self, names):
        names = (names,) if isinstance(names, str) else names
        at = self.flipped(names)
        far = 1 - self.far if "far" in names else self.far
        return {
            "dp": far * 4 + at["z"] * 2 + at["y"],
            "tensor": at["x"] * 2 + at["core"],
        }

    def column(self, names=()):
        at = self.flipped(names)
        return at["x"] * 2 + at["core"]

    def quarter(self, names=()):
        at = self.flipped(names)
        return at["z"] * 2 + at["y"]


def enter(place, names):
    barrier = pltpu.get_barrier_semaphore()
    for name in names:
        pl.semaphore_signal(
            barrier, inc=1, device_id=place.device(name), device_id_type=MESH_ID
        )
    pl.semaphore_wait(barrier, len(names))


class Sender:
    def __init__(self, place, send_sems, recv_sems):
        self.place, self.send_sems, self.recv_sems, self.used = place, send_sems, recv_sems, 0

    def copy(self, source, target, name):
        slot = self.used
        self.used += 1
        return pltpu.make_async_remote_copy(
            src_ref=source,
            dst_ref=target,
            send_sem=self.send_sems.at[slot],
            recv_sem=self.recv_sems.at[slot],
            device_id=self.place.device(name),
            device_id_type=MESH_ID,
        )


def part_rows(tokens):
    unit = tokens // 16
    first = -(-unit // 3)
    second = -(-(unit - first) // 2)
    return (first * 16, second * 16, (unit - first - second) * 16)


def part_starts(tokens):
    rows = part_rows(tokens)
    return (0, rows[0], rows[0] + rows[1])


def spot(tokens, part, half, core, index):
    rows, start = part_rows(tokens)[part], part_starts(tokens)[part]
    return half * 8 * tokens + 8 * start + core * 4 * rows + index * rows


def gather4(tokens, buffer, own, sender, place):
    mine = pl.ds(pl.multiple_of(place.column() * tokens, tokens), tokens)
    theirs = pl.ds(pl.multiple_of(place.column(("x",)) * tokens, tokens), tokens)
    return (
        sender.copy(own, buffer.at[mine], "x"),
        sender.copy(own, buffer.at[mine], "core"),
        sender.copy(buffer.at[theirs], buffer.at[theirs], "core"),
    )


def normed(values, gain):
    factor = lax.rsqrt(jnp.mean(values * values, axis=-1, keepdims=True) + EPSILON)
    return values * factor * gain


def norm_back(values, gain, grad):
    factor = lax.rsqrt(jnp.mean(values * values, axis=-1, keepdims=True) + EPSILON)
    unit = values * factor
    scaled = gain * grad
    back = factor * (scaled - unit * jnp.mean(scaled * unit, axis=-1, keepdims=True))
    return back, jnp.sum(grad * unit, axis=0, keepdims=True)


def scatter4(partial, from_core, from_x, tokens, sender, place):
    copies = []
    for names in (("x", "core"), ("core",)):
        shard = pl.ds(pl.multiple_of(place.column(names) * tokens, tokens), tokens)
        copies.append(
            sender.copy(partial.at[shard], from_core.at[len(copies)], "core")
        )
    return copies


def sum4(partial, from_core, outgoing, from_x, tokens, sender, place):
    copies = scatter4(partial, from_core, from_x, tokens, sender, place)
    for copy in copies:
        copy.start()
    far = pl.ds(pl.multiple_of(place.column(("x",)) * tokens, tokens), tokens)
    mine = pl.ds(pl.multiple_of(place.column() * tokens, tokens), tokens)
    copies[0].wait_recv()
    outgoing[...] = (partial[far, :].astype(F32) + from_core[0].astype(F32)).astype(BF16)
    along = sender.copy(outgoing, from_x, "x")
    along.start()
    copies[1].wait_recv()
    near = partial[mine, :].astype(F32) + from_core[1].astype(F32)
    along.wait_recv()
    total = near + from_x[...].astype(F32)
    for copy in copies:
        copy.wait_send()
    along.wait_send()
    return total


def silu_parts(gate, up, hidden_grad):
    s = 1.0 / (1.0 + jnp.exp(-gate))
    silu = gate * s
    hidden = silu * up
    gate_grad = hidden_grad * up * s * (1.0 + gate * (1.0 - s))
    return hidden, gate_grad, hidden_grad * silu


def back_kernel(
    pair_ref,
    gate_w,
    up_w,
    residual_ref,
    gain_ref,
    grad_ref,
    hidden_ref,
    ffn_all,
    grad_all,
    back_ref,
    gain_back_ref,
    low_all,
    down_came,
    pair_sent,
    weights,
    down_sent,
    ffn_half,
    grad_half,
    products,
    from_core,
    third,
    second,
    first,
    own,
    send_sems,
    recv_sems,
    local_sems,
):
    tokens = residual_ref.shape[0]
    units = pair_ref.shape[1] // 2
    place = Place()
    columns = pl.ds(pl.multiple_of(place.quarter() * units, units), units)
    loads = [
        pltpu.make_async_copy(
            gate_w.at[:, columns], weights.at[:, pl.ds(0, units)], local_sems.at[0]
        ),
        pltpu.make_async_copy(
            up_w.at[:, columns], weights.at[:, pl.ds(units, units)], local_sems.at[1]
        ),
    ]
    width = residual_ref.shape[1]
    block_width = width // 8
    other = pl.ds(pl.multiple_of((1 - place.far) * (width // 2), width // 2), width // 2)
    halves = [
        pltpu.make_async_copy(grad_all.at[:, other], grad_half, local_sems.at[3]),
        pltpu.make_async_copy(ffn_all.at[:, other], ffn_half, local_sems.at[4]),
    ]
    enter(place, LINKS + ("far",))
    for copy in loads + halves:
        copy.start()
    sender = Sender(place, send_sems, recv_sems)
    part_list = [
        (part, part_rows(tokens)[part], part_starts(tokens)[part]) for part in range(3)
    ]

    def place_of(part, half, core, index, count):
        return pl.ds(spot(tokens, part, half, core, index), count)

    to_core = [
        [
            sender.copy(
                products.at[place_of(part, half, 1, 0, 4 * rows)],
                from_core.at[pl.ds(half * 4 * tokens + 4 * start, 4 * rows)],
                "core",
            )
            for part, rows, start in part_list
        ]
        for half in range(2)
    ]
    far = [
        sender.copy(
            products.at[place_of(part, 1, 0, 0, 4 * rows)],
            third.at[pl.ds(4 * start, 4 * rows)],
            ORDERS[part][2],
        )
        for part, rows, start in part_list
    ]
    middle = [
        sender.copy(
            products.at[place_of(part, 0, 0, 2, 2 * rows)],
            second.at[pl.ds(2 * start, 2 * rows)],
            ORDERS[part][1],
        )
        for part, rows, start in part_list
    ]
    close = [
        sender.copy(
            products.at[place_of(part, 0, 0, 1, rows)],
            first.at[pl.ds(start, rows)],
            ORDERS[part][0],
        )
        for part, rows, start in part_list
    ]
    bulk = [
        sender.copy(
            down_sent.at[turn], down_came.at[pl.ds(turn * units, units)], "far"
        )
        for turn in range(4)
    ]

    def columns_of(names):
        start = place.quarter(names) * block_width
        return pl.ds(pl.multiple_of(start, block_width), block_width)

    for copy in loads:
        copy.wait()
    block = 2 * tokens

    def compute(index):
        rows = pl.ds(pl.multiple_of(index * block, block), block)
        products[rows, :] = matmul_nt(pair_ref[rows, :], weights[...]).astype(BF16)

    def add_in(rows, arrived):
        products[rows, :] = (
            products[rows, :].astype(F32) + arrived.astype(F32)
        ).astype(BF16)

    pl.loop(4, 8)(compute)
    for copy in to_core[1]:
        copy.start()
    pl.loop(0, 2)(compute)
    for part, rows, start in part_list:
        to_core[1][part].wait_recv()
        add_in(
            place_of(part, 1, 0, 0, 4 * rows),
            from_core[pl.ds(4 * tokens + 4 * start, 4 * rows), :],
        )
        far[part].start()
    pl.loop(2, 4)(compute)
    for copy in to_core[0]:
        copy.start()
    halves[0].wait()
    for turn, names in enumerate(QUARTERS):
        down_sent[turn] = matmul_tn(
            hidden_ref[...], grad_half[:, columns_of(names)]
        ).astype(BF16)
        if turn < 2:
            bulk[turn].start()
    for part, rows, start in part_list:
        to_core[0][part].wait_recv()
        add_in(
            place_of(part, 0, 0, 0, 4 * rows), from_core[pl.ds(4 * start, 4 * rows), :]
        )
    halves[1].wait()
    for turn, names in enumerate(QUARTERS):
        pair_sent[turn] = matmul_tn(
            ffn_half[:, columns_of(names)], pair_ref[...]
        ).astype(BF16)
    for part, rows, start in part_list:
        far[part].wait_recv()
        add_in(
            place_of(part, 0, 0, 2, 2 * rows),
            third[pl.ds(4 * start + 2 * rows, 2 * rows), :],
        )
        middle[part].start()
        add_in(place_of(part, 0, 0, 0, 2 * rows), third[pl.ds(4 * start, 2 * rows), :])
    bulk[2].start()
    for part, rows, start in part_list:
        middle[part].wait_recv()
        add_in(place_of(part, 0, 0, 1, rows), second[pl.ds(2 * start + rows, rows), :])
        close[part].start()
        add_in(place_of(part, 0, 0, 0, rows), second[pl.ds(2 * start, rows), :])
    bulk[3].start()
    gain_total = jnp.zeros(gain_ref.shape, F32)
    for part, rows, start in part_list:
        close[part].wait_recv()
        mine = pl.ds(start, rows)
        ffn_in_grad = products[place_of(part, 0, 0, 0, rows), :].astype(F32) + first[
            mine, :
        ].astype(F32)
        back, gain_part = norm_back(residual_ref[mine, :], gain_ref[...], ffn_in_grad)
        back = back + grad_ref[mine, :].astype(F32)
        back_ref[mine, :] = back
        own[mine, :] = back.astype(BF16)
        gain_total = gain_total + gain_part
    gain_back_ref[...] = gain_total
    row_copies = gather4(tokens, low_all, own, sender, place)
    row_copies[0].start()
    row_copies[1].start()
    mine = pl.ds(pl.multiple_of(place.column() * tokens, tokens), tokens)
    own_copy = pltpu.make_async_copy(own, low_all.at[mine], local_sems.at[2])
    own_copy.start()
    row_copies[0].wait_recv()
    row_copies[2].start()
    own_copy.wait()
    row_copies[1].wait_recv()
    row_copies[2].wait_recv()
    for copy in to_core[0] + to_core[1] + far + middle + close + list(row_copies):
        copy.wait_send()
    for copy in bulk:
        copy.wait()


def runs16(order, path, step):
    place_of = {
        name: position for position, name in enumerate(order)
    }
    known = [set(chosen) for chosen in subsets(path[:step])]
    moves = []
    for flips in known:
        spots = []
        for names in (flips, flips | {path[step]}):
            bits = [int(name in names) for name in order]
            spots.append((bits[2], bits[0] + 2 * bits[1]))
        moves.append(spots)
    moves.sort()
    runs = []
    for (half, index), (to_half, to_index) in moves:
        if runs:
            last = runs[-1]
            if (
                last[0] == half
                and last[2] == to_half
                and last[1] + last[4] == index
                and last[3] + last[4] == to_index
            ):
                last[4] += 1
                continue
        runs.append([half, index, to_half, to_index, 1])
    return runs


def subsets(names):
    result = [()]
    for name in names:
        result = result + [chosen + (name,) for chosen in result]
    return result


def gather16(tokens, buffer, own, sender, paths):
    links, cores = [], []
    for part, order in enumerate(ORDERS):
        rows, start = part_rows(tokens)[part], part_starts(tokens)[part]

        def region(half, index, count, core=0):
            return buffer.at[pl.ds(spot(tokens, part, half, core, index), count * rows)]

        mine = region(0, 0, 1) if own is None else own.at[pl.ds(start, rows)]
        part_links = []
        part_cores = [[sender.copy(mine, region(0, 0, 1, 1), "core")]]
        for step in range(3):
            step_links, step_cores = [], []
            for half, index, to_half, to_index, count in runs16(order, paths[part], step):
                source = mine if step == 0 else region(half, index, count)
                step_links.append(
                    sender.copy(source, region(to_half, to_index, count), paths[part][step])
                )
                step_cores.append(
                    sender.copy(
                        region(to_half, to_index, count),
                        region(to_half, to_index, count, 1),
                        "core",
                    )
                )
            part_links.append(step_links)
            part_cores.append(step_cores)
        links.append(part_links)
        cores.append(part_cores)
    return links, cores


def gather_begin(links, cores):
    for part in range(3):
        for copy in links[part][0] + cores[part][0]:
            copy.start()


def gather_go(links, cores, step, parts=(0, 1, 2)):
    for part in parts:
        for copy in links[part][step]:
            copy.wait_recv()
        if step < 2:
            for copy in links[part][step + 1]:
                copy.start()
        for copy in cores[part][step + 1]:
            copy.start()


def gather_sent(links, cores):
    for part in range(3):
        for copies in links[part] + cores[part]:
            for copy in copies:
                copy.wait_send()


def document_tables(lengths_ref, frequency, length):
    down = lax.broadcasted_iota(jnp.int32, (length, 128), 0)
    across_lanes = lax.broadcasted_iota(jnp.int32, (8, length), 1)
    ids_down = jnp.zeros((length, 128), jnp.int32)
    starts = jnp.zeros((length, 128), jnp.int32)
    ids_across = jnp.zeros((8, length), jnp.int32)
    end = jnp.int32(0)
    for document in range(lengths_ref.shape[1]):
        count = lengths_ref[0, document]
        end = end + count
        passed = down >= end
        ids_down = ids_down + jnp.where(passed, 1, 0)
        starts = starts + jnp.where(passed, count, 0)
        ids_across = ids_across + jnp.where(across_lanes >= end, 1, 0)
    angles = (down - starts).astype(F32) * frequency
    return ids_down[:, :1], ids_across[:1, :], angles


def document_bias(ids_down, ids_across, length):
    allowed = (ids_down == ids_across) & (
        lax.broadcasted_iota(jnp.int32, (length, length), 1)
        <= lax.broadcasted_iota(jnp.int32, (length, length), 0)
    )
    return jnp.where(allowed, 0.0, MASKED)


def head_forward(raw, gain, cosine, sine, head_width):
    factor = lax.rsqrt(head_means(raw * raw, head_width) + EPSILON)
    values = raw * factor * gain
    width = raw.shape[1]
    return values * widen(cosine, width) + swap_halves(values, head_width) * widen(sine, width)


def forward_kernel(
    lengths_ref,
    input_ref,
    gain_attn,
    gain_ffn,
    gain_query,
    gain_key,
    frequency,
    out_grad,
    query_w,
    key_w,
    value_w,
    out_w,
    gate_w,
    up_w,
    down_w,
    attn_all,
    mixed_ref,
    query_ref,
    key_ref,
    value_ref,
    query_raw,
    key_raw,
    totals_ref,
    cosine_ref,
    sine_ref,
    residual_ref,
    ffn_all,
    grad_all,
    hidden_all,
    pair_all,
    rows_all,
    own,
    hidden_ref,
    pair_ref,
    attn_in,
    qkv_w,
    out_v,
    bias,
    partial,
    from_core,
    outgoing,
    from_x,
    ffn_buf,
    grad_buf,
    gate_v,
    up_v,
    down_v,
    send_sems,
    recv_sems,
    local_sems,
):
    tokens, width = input_ref.shape
    length = 4 * tokens
    units = gate_v.shape[1]
    heads_width, key_width = query_ref.shape[1], key_ref.shape[1]
    place = Place()
    columns = pl.ds(pl.multiple_of(place.quarter() * units, units), units)
    local_used = [0]

    def load(source, target):
        copy = pltpu.make_async_copy(source, target, local_sems.at[local_used[0]])
        local_used[0] += 1
        copy.start()
        return copy

    enter(place, LINKS)
    sender = Sender(place, send_sems, recv_sems)
    own[...] = normed(input_ref[...].astype(F32), gain_attn[...]).astype(BF16)
    row_copies = gather4(tokens, attn_in, own, sender, place)
    row_copies[0].start()
    row_copies[1].start()
    grad_links, grad_cores = gather16(tokens, grad_buf, out_grad, sender, GRAD_PATHS)
    gather_begin(grad_links, grad_cores)
    first_loads = [
        load(query_w, qkv_w.at[:, pl.ds(0, heads_width)]),
        load(key_w, qkv_w.at[:, pl.ds(heads_width, key_width)]),
        load(value_w, qkv_w.at[:, pl.ds(heads_width + key_width, key_width)]),
        load(out_w, out_v),
    ]
    mine = pl.ds(pl.multiple_of(place.column() * tokens, tokens), tokens)
    attn_in[mine, :] = own[...]
    grad_loads = []
    for part in range(3):
        rows, start = part_rows(tokens)[part], part_starts(tokens)[part]
        grad_loads.append(
            load(
                out_grad.at[pl.ds(start, rows)],
                grad_buf.at[pl.ds(spot(tokens, part, 0, 0, 0), rows)],
            )
        )
    later_loads = [
        load(gate_w.at[:, columns], gate_v),
        load(up_w.at[:, columns], up_v),
        load(down_w.at[columns, :], down_v),
    ]
    ids_down, ids_across, angles = document_tables(lengths_ref, frequency[...], length)
    lane = lax.broadcasted_iota(jnp.int32, (length, 128), 1)
    cosine_ref[...] = jnp.cos(angles)
    sine = jnp.sin(angles)
    sine_ref[...] = jnp.where(lane % HEAD_WIDTH < HEAD_WIDTH // 2, -sine, sine)
    bias[...] = document_bias(ids_down, ids_across, length)
    for copy in first_loads + grad_loads:
        copy.wait()
    gather_go(grad_links, grad_cores, 0, (2,))
    row_copies[0].wait_recv()
    row_copies[2].start()
    row_copies[1].wait_recv()
    row_copies[2].wait_recv()
    attn_store = load(attn_in, attn_all)
    gather_go(grad_links, grad_cores, 1, (2,))

    raw = jnp.dot(attn_in[...], qkv_w[...], preferred_element_type=F32)
    query_raw[...] = raw[:, :heads_width]
    key_raw[...] = raw[:, heads_width : heads_width + key_width].astype(BF16).astype(F32)
    value_ref[...] = raw[:, heads_width + key_width :].astype(BF16)
    query_ref[...] = head_forward(
        query_raw[...], gain_query[...], cosine_ref[...], sine_ref[...], HEAD_WIDTH
    ).astype(BF16)
    key_ref[...] = head_forward(
        key_raw[...], gain_key[...], cosine_ref[...], sine_ref[...], HEAD_WIDTH
    ).astype(BF16)
    gather_go(grad_links, grad_cores, 0, (0, 1))
    scale = HEAD_WIDTH ** (-0.5)
    group_heads = HEADS // KV
    mixed_parts = []
    head_total = heads_width // HEAD_WIDTH
    for head in range(head_total):
        group = head // group_heads
        group_lanes = slice(group * HEAD_WIDTH, (group + 1) * HEAD_WIDTH)
        scores = (
            matmul_nt(
                query_ref[:, head * HEAD_WIDTH : (head + 1) * HEAD_WIDTH],
                key_ref[:, group_lanes],
            )
            * scale
            + bias[...]
        )
        top = jnp.max(scores, axis=-1, keepdims=True)
        exponent = jnp.exp(scores - top)
        total = jnp.sum(exponent, axis=-1, keepdims=True)
        probs = (exponent * (1.0 / total)).astype(BF16)
        mixed_parts.append(
            jnp.dot(probs, value_ref[:, group_lanes], preferred_element_type=F32)
        )
        totals_ref[:, head : head + 1] = top + jnp.log(total)
        if head % 2 == 1:
            mixed_ref[:, (head - 1) * HEAD_WIDTH : (head + 1) * HEAD_WIDTH] = (
                jnp.concatenate(mixed_parts, axis=1).astype(BF16)
            )
            mixed_parts = []
        if head == head_total // 2 - 1:
            gather_go(grad_links, grad_cores, 1, (0, 1))
    partial[...] = jnp.dot(mixed_ref[...], out_v[...], preferred_element_type=F32).astype(BF16)

    residual = input_ref[...].astype(F32) + sum4(
        partial, from_core, outgoing, from_x, tokens, sender, place
    )
    residual_ref[...] = residual
    for copy in row_copies:
        copy.wait_send()
    own[...] = normed(residual, gain_ffn[...]).astype(BF16)
    for part in range(3):
        rows, start = part_rows(tokens)[part], part_starts(tokens)[part]
        ffn_buf[pl.ds(spot(tokens, part, 0, 0, 0), rows), :] = own[pl.ds(start, rows), :]
    links, cores = gather16(tokens, ffn_buf, None, sender, ORDERS)
    gather_begin(links, cores)
    gather_go(grad_links, grad_cores, 2)
    gather_go(links, cores, 0)
    for copy in later_loads:
        copy.wait()
    for part in range(3):
        for step_copies in grad_cores[part]:
            for copy in step_copies:
                copy.wait_recv()
    grad_store = load(grad_buf, grad_all)
    gather_go(links, cores, 1)
    for part in range(3):
        for step_copies in cores[part][:3]:
            for copy in step_copies:
                copy.wait_recv()

    block = 2 * tokens

    def compute(index):
        rows = pl.ds(pl.multiple_of(index * block, block), block)
        values = ffn_buf[rows, :]
        gate = jnp.dot(values, gate_v[...], preferred_element_type=F32)
        up = jnp.dot(values, up_v[...], preferred_element_type=F32)
        hidden_grad = matmul_nt(grad_buf[rows, :], down_v[...])
        hidden, gate_grad, up_grad = silu_parts(gate, up, hidden_grad)
        hidden_ref[rows, :] = hidden.astype(BF16)
        pair_ref[rows, :units] = gate_grad.astype(BF16)
        pair_ref[rows, units:] = up_grad.astype(BF16)

    half = 8 * tokens
    stores = [attn_store, grad_store]

    def store_half(which):
        rows = pl.ds(which * half, half)
        stores.append(load(hidden_ref.at[rows], hidden_all.at[rows]))
        stores.append(load(pair_ref.at[rows], pair_all.at[rows]))
        for part, order in enumerate(ORDERS):
            count, start = part_rows(tokens)[part], part_starts(tokens)[part]
            for core in range(2):
                for index in range(4):
                    bits = (index % 2, index // 2, which)
                    flips = tuple(name for name, bit in zip(order, bits) if bit)
                    row = ("z" in flips) * 2 + ("y" in flips)
                    names = tuple(n for n in flips if n == "x") + (("core",) if core else ())
                    target = row * 4 * tokens + place.column(names) * tokens + start
                    stores.append(
                        load(
                            hidden_ref.at[
                                pl.ds(spot(tokens, part, which, core, index), count)
                            ],
                            rows_all.at[pl.ds(pl.multiple_of(target, 16), count)],
                        )
                    )

    stores.append(load(ffn_buf.at[pl.ds(0, half)], ffn_all.at[pl.ds(0, half)]))
    pl.loop(0, 4)(compute)
    gather_go(links, cores, 2)
    store_half(0)
    for part in range(3):
        for copy in cores[part][3]:
            copy.wait_recv()
    stores.append(load(ffn_buf.at[pl.ds(half, half)], ffn_all.at[pl.ds(half, half)]))
    pl.loop(4, 8)(compute)
    store_half(1)
    for copy in stores:
        copy.wait()
    gather_sent(grad_links, grad_cores)
    gather_sent(links, cores)


GAIN_LINKS = ("core", "x", "y", "z", "far")


def swap_halves(values, head_width):
    width = values.shape[1]
    half = head_width // 2
    lane = lax.broadcasted_iota(jnp.int32, values.shape, 1)
    return jnp.where(
        lane % head_width < half,
        pltpu.roll(values, width - half, 1),
        pltpu.roll(values, half, 1),
    )


def head_means(values, head_width):
    width = values.shape[1]
    rows = lax.broadcasted_iota(jnp.int32, (width, width), 0) // head_width
    columns = lax.broadcasted_iota(jnp.int32, (width, width), 1) // head_width
    blocks = jnp.where(rows == columns, 1.0 / head_width, 0.0).astype(BF16)
    upper = values.astype(BF16)
    lower = (values - upper.astype(F32)).astype(BF16)
    return jnp.dot(upper, blocks, preferred_element_type=F32) + jnp.dot(
        lower, blocks, preferred_element_type=F32
    )


def widen(table, width):
    return jnp.concatenate([table] * (width // table.shape[1]), axis=1)


def head_back(grad, raw, gain, cosine, sine, head_width):
    width = grad.shape[1]
    back = grad * widen(cosine, width) - swap_halves(grad, head_width) * widen(sine, width)
    factor = lax.rsqrt(head_means(raw * raw, head_width) + EPSILON)
    unit = raw * factor
    scaled = gain * back
    result = factor * (scaled - unit * head_means(scaled * unit, head_width))
    return result, jnp.sum(back * unit, axis=0, keepdims=True)


def fold_heads(row, head_width):
    total = row[:, :128]
    for start in range(128, row.shape[1], 128):
        total = total + row[:, start : start + 128]
    return total + pltpu.roll(total, head_width, 1)


GAIN_LINKS = ("core", "x", "y", "z", "far")


class RowSum:
    def __init__(self, partial, from_core, outgoing, from_x, tokens, sender, place):
        self.partial, self.from_core = partial, from_core
        self.outgoing, self.from_x = outgoing, from_x
        self.far = pl.ds(pl.multiple_of(place.column(("x",)) * tokens, tokens), tokens)
        self.mine = pl.ds(pl.multiple_of(place.column() * tokens, tokens), tokens)
        self.copies = scatter4(partial, from_core, from_x, tokens, sender, place)
        self.along = sender.copy(outgoing, from_x, "x")

    def begin(self):
        for copy in self.copies:
            copy.start()

    def send_on(self):
        self.copies[0].wait_recv()
        self.outgoing[...] = (
            self.partial[self.far, :].astype(F32) + self.from_core[0].astype(F32)
        ).astype(BF16)
        self.along.start()

    def total(self):
        self.copies[1].wait_recv()
        near = self.partial[self.mine, :].astype(F32) + self.from_core[1].astype(F32)
        self.along.wait_recv()
        total = near + self.from_x[...].astype(F32)
        for copy in self.copies:
            copy.wait_send()
        self.along.wait_send()
        return total


def finish_kernel(
    low_all,
    out_w,
    query_w,
    key_w,
    value_w,
    down_w,
    attn_all,
    pair_all,
    hidden_all,
    ffn_all,
    grad_all,
    rows_all,
    pair_sent,
    down_came,
    mixed_ref,
    query_ref,
    key_ref,
    value_ref,
    query_raw,
    key_raw,
    totals_ref,
    cosine_ref,
    sine_ref,
    lengths_ref,
    gain_query,
    gain_key,
    gain_attn,
    input_ref,
    back_ref,
    ffn_gain_ref,
    residual_ref,
    layer_ref,
    input_grad_ref,
    query_out,
    key_out,
    value_out,
    out_out,
    gate_out,
    up_out,
    down_out,
    attn_gain_out,
    ffn_gain_out,
    head_gain_out,
    low,
    out_v,
    qkv_w,
    attn_in,
    pair,
    hidden,
    columns_v,
    down_blocks,
    bias,
    mixed_grad,
    mixed_peer,
    qkv_low,
    qkv_peer,
    attn_peer,
    low_peer,
    out_near,
    out_near_came,
    out_far,
    out_far_came,
    qkv_near,
    qkv_near_came,
    qkv_far,
    qkv_far_came,
    out_part,
    qkv_part,
    pair_blocks,
    pair_blocks_came,
    down_blocks_came,
    rows_came,
    from_core,
    outgoing,
    from_x,
    near_layer,
    near_layer_came,
    sums,
    came,
    send_sems,
    recv_sems,
    local_sems,
):
    tokens, width = input_ref.shape
    length = 4 * tokens
    units = hidden.shape[1]
    heads_width = query_ref.shape[1]
    key_width = key_ref.shape[1]
    head_width = HEAD_WIDTH
    group_heads = HEADS // KV
    groups = key_width // head_width
    block = width // 8
    place = Place()
    y, z, far = place.at["y"], place.at["z"], place.far
    sender = Sender(place, send_sems, recv_sems)
    local_used = [0]

    def load(source, target):
        copy = pltpu.make_async_copy(source, target, local_sems.at[local_used[0]])
        local_used[0] += 1
        copy.start()
        return copy

    def lanes(start, count):
        return pl.ds(pl.multiple_of(start, count), count)

    def quarter_lanes(names):
        return lanes(place.quarter(names) * block, block)

    def quarter_units(names):
        return lanes(place.quarter(names) * units, units)

    def own_half(source):
        return source.at[:, lanes(far * (width // 2), width // 2)]

    enter(place, GAIN_LINKS + (("y", "z"),))
    mine = lanes(place.column() * tokens, tokens)
    bulk = [sender.copy(pair_sent.at[turn], pair_blocks.at[turn], "far") for turn in range(4)]
    bulk[0].start()
    bulk[1].start()
    mixed_copy = sender.copy(mixed_ref, mixed_peer, "y")
    mixed_copy.start()

    def to_peer(source, target):
        return [
            sender.copy(
                source.at[mine, lanes((index * 2 + 1 - y) * block, block)],
                target.at[mine, pl.ds(index * block, block)],
                "y",
            )
            for index in range(4)
        ]

    low_peers = to_peer(low_all, low_peer)
    attn_peers = to_peer(attn_all, attn_peer)
    for copy in low_peers + attn_peers:
        copy.start()
    hidden_load = load(hidden_all, hidden)
    grad_load = load(own_half(grad_all), columns_v)
    down_load = load(down_came, down_blocks)
    low_load = load(low_all, low)
    out_load = load(out_w, out_v)
    attn_load = load(attn_all, attn_in)
    pair_load = load(pair_all, pair)
    qkv_loads = [
        load(query_w, qkv_w.at[:, pl.ds(0, heads_width)]),
        load(key_w, qkv_w.at[:, pl.ds(heads_width, key_width)]),
        load(value_w, qkv_w.at[:, pl.ds(heads_width + key_width, key_width)]),
    ]
    row_loads = [
        load(rows_all.at[pl.ds(0, length)], rows_came.at[0]),
        load(rows_all.at[pl.ds(2 * length, length)], rows_came.at[2]),
    ]
    row_copies = [
        sender.copy(rows_all.at[pl.ds(offset * length, length)], rows_came.at[offset], "y")
        for offset in (1, 3)
    ]

    hidden_load.wait()
    grad_load.wait()
    down_load.wait()
    down_copies = []
    for turn, names in enumerate(QUARTERS):
        rows = pl.ds(turn * units, units)
        total = matmul_tn(hidden[...], columns_v[:, quarter_lanes(names)]) + down_blocks[
            rows, :
        ].astype(F32)
        if names:
            down_blocks[rows, :] = total.astype(BF16)
            copy = sender.copy(down_blocks.at[rows], down_blocks_came.at[turn], names)
            copy.start()
            down_copies.append(copy)
        else:
            down_out[quarter_units(()), :] = total.astype(BF16)
    own_load = load(own_half(ffn_all), columns_v)
    bulk[2].start()
    bulk[3].start()

    low_load.wait()
    out_load.wait()
    mixed_grad[...] = matmul_nt(low[...], out_v[...]).astype(BF16)
    ids_down, ids_across, unused_angles = document_tables(
        lengths_ref, jnp.ones((1, 128), F32), length
    )
    bias[...] = document_bias(ids_down, ids_across, length)
    for copy in low_peers + attn_peers:
        copy.wait_recv()
    low_gather = gather4(tokens, low_peer, low_peer.at[mine], sender, place)
    attn_gather = gather4(tokens, attn_peer, attn_peer.at[mine], sender, place)
    for copies_of in (low_gather, attn_gather):
        copies_of[0].start()
        copies_of[1].start()
    for copy in row_copies:
        copy.start()

    scale = head_width ** (-0.5)
    key_parts, value_parts, query_gain = [], [], [None]
    peer_copies = []

    def attention_group(group):
        group_lanes = slice(group * head_width, (group + 1) * head_width)
        key, value = key_ref[:, group_lanes], value_ref[:, group_lanes]
        key_grad = jnp.zeros((length, head_width), F32)
        value_grad = jnp.zeros((length, head_width), F32)
        query_parts = []
        for head in range(group * group_heads, (group + 1) * group_heads):
            head_lanes = slice(head * head_width, (head + 1) * head_width)
            query, grad = query_ref[:, head_lanes], mixed_grad[:, head_lanes]
            scores = matmul_nt(query, key) * scale + bias[...]
            probs = jnp.exp(scores - totals_ref[:, head : head + 1])
            prob_grad = matmul_nt(grad, value)
            value_grad = value_grad + matmul_tn(probs.astype(BF16), grad)
            centre = jnp.sum(probs * prob_grad, axis=-1, keepdims=True)
            score_grad = (probs * (prob_grad - centre)).astype(BF16)
            query_parts.append(jnp.dot(score_grad, key, preferred_element_type=F32) * scale)
            key_grad = key_grad + matmul_tn(score_grad, query) * scale
        key_parts.append(key_grad)
        value_parts.append(value_grad)
        wide = slice(group * group_heads * head_width, (group + 1) * group_heads * head_width)
        query_grad, gain_part = head_back(
            jnp.concatenate(query_parts, axis=1),
            query_raw[:, wide],
            gain_query[:, wide],
            cosine_ref[...],
            sine_ref[...],
            head_width,
        )
        gain_part = fold_heads(gain_part, head_width)
        query_gain[0] = gain_part if query_gain[0] is None else query_gain[0] + gain_part
        qkv_low[:, wide] = query_grad.astype(BF16)
        copy = sender.copy(qkv_low.at[:, wide], qkv_peer.at[:, wide], "y")
        copy.start()
        peer_copies.append(copy)

    attention_group(0)

    for copies_of in (low_gather, attn_gather):
        copies_of[0].wait_recv()
        copies_of[2].start()
    for copies_of in (low_gather, attn_gather):
        copies_of[1].wait_recv()
        copies_of[2].wait_recv()
    mixed_copy.wait_recv()

    def out_total(index):
        return matmul_tn(
            mixed_ref[...], low[:, lanes((index * 2 + y) * block, block)]
        ) + matmul_tn(mixed_peer[...], low_peer[:, lanes(index * block, block)])

    near_copies = []
    for turn, half in enumerate((1 - far, far)):
        out_near[turn] = out_total(half * 2 + 1 - z).astype(BF16)
        copy = sender.copy(out_near.at[turn], out_near_came.at[turn], "z")
        copy.start()
        near_copies.append(copy)
    out_part[...] = out_total((1 - far) * 2 + z)
    out_out[...] = out_total(far * 2 + z)

    for group in range(1, groups):
        attention_group(group)
    key_back, key_gain = head_back(
        jnp.concatenate(key_parts, axis=1),
        key_raw[...],
        gain_key[...],
        cosine_ref[...],
        sine_ref[...],
        head_width,
    )
    key_gain = fold_heads(key_gain, head_width)
    qkv_low[:, heads_width : heads_width + key_width] = key_back.astype(BF16)
    qkv_low[:, heads_width + key_width :] = jnp.concatenate(value_parts, axis=1).astype(BF16)
    tail = slice(heads_width, heads_width + 2 * key_width)
    peer_copies.append(sender.copy(qkv_low.at[:, tail], qkv_peer.at[:, tail], "y"))
    peer_copies[-1].start()

    partial = out_v
    for copy in qkv_loads:
        copy.wait()

    def part_of(index):
        columns = lanes(index * 512, 512)
        partial[:, columns] = matmul_nt(qkv_low[...], qkv_w[columns, :]).astype(BF16)

    pl.loop(0, width // 512)(part_of)
    attn_sum = RowSum(partial, from_core.at[0], outgoing.at[0], from_x.at[0], tokens, sender, place)
    attn_sum.begin()

    own_load.wait()
    pair_load.wait()
    pair_copies = []

    def spread_pair(turn):
        names = QUARTERS[turn]
        bulk[turn].wait_recv()
        total = matmul_tn(columns_v[:, quarter_lanes(names)], pair[...]) + pair_blocks[
            turn
        ].astype(F32)
        if names:
            pair_blocks[turn] = total.astype(BF16)
            copy = sender.copy(pair_blocks.at[turn], pair_blocks_came.at[turn], names)
            copy.start()
            pair_copies.append(copy)
        else:
            gate_out[:, quarter_units(())] = total[:, :units].astype(BF16)
            up_out[:, quarter_units(())] = total[:, units:].astype(BF16)

    spread_pair(0)
    attn_sum.send_on()

    attn_load.wait()
    for copy in peer_copies:
        copy.wait_recv()

    def qkv_total(index):
        return matmul_tn(
            attn_in[:, lanes((index * 2 + y) * block, block)], qkv_low[...]
        ) + matmul_tn(attn_peer[:, lanes(index * block, block)], qkv_peer[...])

    for turn, half in enumerate((1 - far, far)):
        qkv_near[turn] = qkv_total(half * 2 + 1 - z).astype(BF16)
        copy = sender.copy(qkv_near.at[turn], qkv_near_came.at[turn], "z")
        copy.start()
        near_copies.append(copy)
    near_copies[0].wait_recv()
    out_far[...] = (out_part[...] + out_near_came[0].astype(F32)).astype(BF16)
    out_far_copy = sender.copy(out_far, out_far_came, "far")
    out_far_copy.start()
    qkv_part[...] = qkv_total((1 - far) * 2 + z)
    own_qkv = qkv_total(far * 2 + z)
    query_out[...] = own_qkv[:, :heads_width]
    key_out[...] = own_qkv[:, heads_width : heads_width + key_width]
    value_out[...] = own_qkv[:, heads_width + key_width :]

    attn_grad = attn_sum.total()
    back, attn_gain = norm_back(input_ref[...].astype(F32), gain_attn[...], attn_grad)
    input_grad_ref[...] = (back + back_ref[...]).astype(BF16)
    sums[0, :, :width] = attn_gain
    sums[0, :, width : 2 * width] = ffn_gain_ref[...]
    lane = lax.broadcasted_iota(jnp.int32, (1, 128), 1)
    sums[0, :, 2 * width :] = jnp.where(lane < head_width, query_gain[0], key_gain)
    gain_copies = []

    def gain_begin(step):
        if step:
            gain_copies[-1].wait()
            sums[step] = sums[step - 1] + came[step - 1]
        if step < len(GAIN_LINKS):
            copy = sender.copy(sums.at[step], came.at[step], GAIN_LINKS[step])
            copy.start()
            gain_copies.append(copy)

    gain_begin(0)

    layer_parts = (low, out_v)
    for copy in row_loads:
        copy.wait()
    for copy in row_copies:
        copy.wait_recv()

    def down_loads(chunk):
        return [
            load(
                down_w.at[quarter_units(names), pl.ds(chunk * 512, 512)],
                qkv_w.at[pl.ds((chunk % 2) * 2 * units + turn * units, units), pl.ds(0, 512)],
            )
            for turn, names in enumerate(((), ("y",)))
        ]

    chunks = width // 512
    pending = down_loads(0)
    for chunk in range(chunks):
        columns = pl.ds(chunk * 512, 512)
        for copy in pending:
            copy.wait()
        if chunk + 1 < chunks:
            pending = down_loads(chunk + 1)
        base = (chunk % 2) * 2 * units
        for target, first in ((layer_parts[0], 2), (layer_parts[1], 0)):
            target[:, columns] = (
                jnp.dot(
                    rows_came[first],
                    qkv_w[pl.ds(base, units), pl.ds(0, 512)],
                    preferred_element_type=F32,
                )
                + jnp.dot(
                    rows_came[first + 1],
                    qkv_w[pl.ds(base + units, units), pl.ds(0, 512)],
                    preferred_element_type=F32,
                )
            ).astype(BF16)
    gain_begin(1)
    layer_sums = [
        RowSum(
            layer_parts[turn],
            from_core.at[turn + 1],
            outgoing.at[turn + 1],
            from_x.at[turn + 1],
            tokens,
            sender,
            place,
        )
        for turn in range(2)
    ]
    layer_sums[0].begin()
    layer_sums[1].begin()
    spread_pair(1)
    layer_sums[0].send_on()
    layer_sums[1].send_on()
    gain_begin(2)
    near_copies[2].wait_recv()
    qkv_far[...] = (qkv_part[...] + qkv_near_came[0].astype(F32)).astype(BF16)
    qkv_far_copy = sender.copy(qkv_far, qkv_far_came, "far")
    qkv_far_copy.start()
    near_layer[...] = layer_sums[0].total().astype(BF16)
    layer_copy = sender.copy(near_layer, near_layer_came, "z")
    layer_copy.start()
    gain_begin(3)
    spread_pair(2)
    for turn, copy in enumerate(down_copies):
        copy.wait_recv()
        down_out[quarter_units(QUARTERS[turn]), :] = down_blocks_came[turn]
    near_copies[1].wait_recv()
    out_out[...] += out_near_came[1].astype(F32)
    near_copies[3].wait_recv()
    own_near = qkv_near_came[1].astype(F32)
    query_out[...] += own_near[:, :heads_width]
    key_out[...] += own_near[:, heads_width : heads_width + key_width]
    value_out[...] += own_near[:, heads_width + key_width :]
    gain_begin(4)
    spread_pair(3)
    layer_total = layer_sums[1].total()
    layer_copy.wait_recv()
    layer_ref[...] = (
        residual_ref[...] + (layer_total + near_layer_came[...].astype(F32))
    ).astype(BF16)
    for turn, copy in enumerate(pair_copies):
        copy.wait_recv()
        columns = quarter_units(QUARTERS[turn])
        gate_out[:, columns] = pair_blocks_came[turn, :, :units]
        up_out[:, columns] = pair_blocks_came[turn, :, units:]
    out_far_copy.wait_recv()
    out_out[...] += out_far_came[...].astype(F32)
    qkv_far_copy.wait_recv()
    own_far = qkv_far_came[...].astype(F32)
    query_out[...] += own_far[:, :heads_width]
    key_out[...] += own_far[:, heads_width : heads_width + key_width]
    value_out[...] += own_far[:, heads_width + key_width :]
    gain_begin(5)
    attn_gain_out[...] = sums[5, :, :width]
    ffn_gain_out[...] = sums[5, :, width : 2 * width]
    head_gain_out[...] = sums[5, :, 2 * width :]
    for copy in (
        bulk
        + row_copies
        + low_peers
        + attn_peers
        + list(low_gather)
        + list(attn_gather)
        + peer_copies
        + near_copies
        + down_copies
        + pair_copies
        + [mixed_copy, out_far_copy, qkv_far_copy, layer_copy]
    ):
        copy.wait_send()
IN_VMEM = pl.BlockSpec(memory_space=pltpu.VMEM)
ANYWHERE = pl.BlockSpec(memory_space=pl.ANY)
MIB = 1 << 20


def shape_of(shape, dtype):
    return jax.ShapeDtypeStruct(shape, dtype)


def call(kernel, number, ins, outs, out_specs, scratch, limit, operands, flops, moved):
    return pl.pallas_call(
        kernel,
        out_shape=outs,
        in_specs=ins,
        out_specs=out_specs,
        scratch_shapes=scratch,
        cost_estimate=pl.CostEstimate(
            flops=flops, bytes_accessed=moved, transcendentals=0
        ),
        compiler_params=pltpu.CompilerParams(
            collective_id=number, has_side_effects=True, vmem_limit_bytes=limit
        ),
    )(*operands)


def copies(count):
    return [pltpu.SemaphoreType.DMA((count,)), pltpu.SemaphoreType.DMA((count,))]


def forward_step(
    doc_lengths,
    layer_input,
    gains,
    out_grad,
    weights,
):
    tokens, width = layer_input.shape
    heads_width, key_width = weights[0].shape[1], weights[1].shape[1]
    units = weights[4].shape[1] // 4
    length, everyone = 4 * tokens, 16 * tokens
    exponents = -np.arange(0, HEAD_WIDTH, 2, dtype=np.float32) / HEAD_WIDTH
    frequency = np.tile((ROPE_BASE**exponents).astype(np.float32), 128 * 2 // HEAD_WIDTH)
    gain_attn, gain_ffn, gain_query, gain_key = gains
    v = pltpu.VMEM
    return call(
        forward_kernel,
        1,
        [pl.BlockSpec(memory_space=pltpu.SMEM)] + [IN_VMEM] * 6 + [ANYWHERE] * 8,
        [
            shape_of((length, width), BF16),
            shape_of((length, heads_width), BF16),
            shape_of((length, heads_width), BF16),
            shape_of((length, key_width), BF16),
            shape_of((length, key_width), BF16),
            shape_of((length, heads_width), F32),
            shape_of((length, key_width), F32),
            shape_of((length, 128), F32),
            shape_of((length, 128), F32),
            shape_of((length, 128), F32),
            shape_of((tokens, width), F32),
            shape_of((everyone, width), BF16),
            shape_of((everyone, width), BF16),
            shape_of((everyone, units), BF16),
            shape_of((everyone, 2 * units), BF16),
            shape_of((everyone, units), BF16),
        ],
        [ANYWHERE] + [IN_VMEM] * 10 + [ANYWHERE] * 5,
        [
            v((tokens, width), BF16),
            v((everyone, units), BF16),
            v((everyone, 2 * units), BF16),
            v((length, width), BF16),
            v((width, heads_width + 2 * key_width), BF16),
            v((heads_width, width), BF16),
            v((length, length), F32),
            v((length, width), BF16),
            v((2, tokens, width), BF16),
            v((tokens, width), BF16),
            v((tokens, width), BF16),
            v((everyone, width), BF16),
            v((everyone, width), BF16),
            v((width, units), BF16),
            v((width, units), BF16),
            v((units, width), BF16),
        ]
        + copies(64)
        + [pltpu.SemaphoreType.DMA((80,))],
        61 * MIB,
        (
            doc_lengths,
            layer_input,
            gain_attn[None, :],
            gain_ffn[None, :],
            jnp.tile(gain_query, heads_width // HEAD_WIDTH)[None, :],
            jnp.tile(gain_key, key_width // HEAD_WIDTH)[None, :],
            frequency[None, :],
            out_grad,
        )
        + weights,
        8 * everyone * width * units,
        200 * 10**6,
    )


def back_step(pair, w_gate, w_up, residual, gain_ffn, out_grad, hidden, ffn_all, grad_all):
    tokens, width = residual.shape
    units = pair.shape[1] // 2
    everyone = 16 * tokens
    return call(
        back_kernel,
        2,
        [IN_VMEM, ANYWHERE, ANYWHERE] + [IN_VMEM] * 4 + [ANYWHERE] * 2,
        [
            shape_of((tokens, width), F32),
            shape_of((1, width), F32),
            shape_of((4 * tokens, width), BF16),
            shape_of((4 * units, width // 8), BF16),
            shape_of((4, width // 8, 2 * units), BF16),
        ],
        [IN_VMEM, IN_VMEM, ANYWHERE, ANYWHERE, IN_VMEM],
        [
            pltpu.VMEM((width, 2 * units), BF16),
            pltpu.VMEM((4, units, width // 8), BF16),
            pltpu.VMEM((everyone, width // 2), BF16),
            pltpu.VMEM((everyone, width // 2), BF16),
            pltpu.VMEM((everyone, width), BF16),
            pltpu.VMEM((everyone // 2, width), BF16),
            pltpu.VMEM((everyone // 4, width), BF16),
            pltpu.VMEM((everyone // 8, width), BF16),
            pltpu.VMEM((everyone // 16, width), BF16),
            pltpu.VMEM((tokens, width), BF16),
        ]
        + copies(22)
        + [pltpu.SemaphoreType.DMA((5,))],
        58 * MIB,
        (pair, w_gate, w_up, residual, gain_ffn[None, :], out_grad, hidden, ffn_all, grad_all),
        8 * everyone * width * units,
        200 * 10**6,
    )


def finish_step(big, small, tokens, width, units, heads_width, key_width):
    length, everyone, block = 4 * tokens, 16 * tokens, width // 8
    qkv_width = heads_width + 2 * key_width
    gains = 2 * width + 128
    v = pltpu.VMEM
    return call(
        finish_kernel,
        3,
        [ANYWHERE] * len(big)
        + [IN_VMEM] * 9
        + [pl.BlockSpec(memory_space=pltpu.SMEM)]
        + [IN_VMEM] * (len(small) - 10),
        [
            shape_of((tokens, width), BF16),
            shape_of((tokens, width), BF16),
            shape_of((block, heads_width), F32),
            shape_of((block, key_width), F32),
            shape_of((block, key_width), F32),
            shape_of((heads_width, block), F32),
            shape_of((block, 4 * units), BF16),
            shape_of((block, 4 * units), BF16),
            shape_of((4 * units, block), BF16),
            shape_of((1, width), F32),
            shape_of((1, width), F32),
            shape_of((1, 128), F32),
        ],
        [IN_VMEM] * 12,
        [
            v((length, width), BF16),
            v((heads_width, width), BF16),
            v((width, qkv_width), BF16),
            v((length, width), BF16),
            v((everyone, 2 * units), BF16),
            v((everyone, units), BF16),
            v((everyone, width // 2), BF16),
            v((4 * units, block), BF16),
            v((length, length), F32),
            v((length, heads_width), BF16),
            v((length, heads_width), BF16),
            v((length, qkv_width), BF16),
            v((length, qkv_width), BF16),
            v((length, width // 2), BF16),
            v((length, width // 2), BF16),
            v((2, heads_width, block), BF16),
            v((2, heads_width, block), BF16),
            v((heads_width, block), BF16),
            v((heads_width, block), BF16),
            v((2, block, qkv_width), BF16),
            v((2, block, qkv_width), BF16),
            v((block, qkv_width), BF16),
            v((block, qkv_width), BF16),
            v((heads_width, block), F32),
            v((block, qkv_width), F32),
            v((4, block, 2 * units), BF16),
            v((3, block, 2 * units), BF16),
            v((3, units, block), BF16),
            v((4, length, units), BF16),
            v((3, 2, tokens, width), BF16),
            v((3, tokens, width), BF16),
            v((3, tokens, width), BF16),
            v((tokens, width), BF16),
            v((tokens, width), BF16),
            v((6, 1, gains), F32),
            v((5, 1, gains), F32),
        ]
        + copies(64)
        + [pltpu.SemaphoreType.DMA((32,))],
        62 * MIB,
        big + small,
        8 * everyone * width * units,
        400 * 10**6,
    )


def per_device_sixteen(
    layer_input,
    doc_lengths,
    w_query,
    w_key,
    w_value,
    w_out,
    w_gate,
    w_up,
    w_down,
    gain_attn,
    gain_ffn,
    gain_query,
    gain_key,
    out_grad,
):
    outs = forward_step(
        doc_lengths,
        layer_input,
        (gain_attn, gain_ffn, gain_query, gain_key),
        out_grad,
        (w_query, w_key, w_value, w_out, w_gate, w_up, w_down),
    )
    attn_in, saved = outs[0], tuple(outs[1:10])
    residual, ffn_all, grad_all, hidden, pair, hidden_rows = outs[10:]
    residual_grad, gain_ffn_part, res_low, down_came, pair_sent = back_step(
        pair, w_gate, w_up, residual, gain_ffn, out_grad, hidden, ffn_all, grad_all
    )
    heads_width, key_width = w_query.shape[1], w_key.shape[1]
    (
        layer_out,
        input_grad,
        grad_query,
        grad_key,
        grad_value,
        grad_out,
        grad_gate,
        grad_up,
        grad_down,
        attn_gain,
        ffn_gain,
        head_gain,
    ) = finish_step(
        (
            res_low,
            w_out,
            w_query,
            w_key,
            w_value,
            w_down,
            attn_in,
            pair,
            hidden,
            ffn_all,
            grad_all,
            hidden_rows,
            pair_sent,
            down_came,
        ),
        saved
        + (
            doc_lengths,
            jnp.tile(gain_query, heads_width // HEAD_WIDTH)[None, :],
            jnp.tile(gain_key, key_width // HEAD_WIDTH)[None, :],
            gain_attn[None, :],
            layer_input,
            residual_grad,
            gain_ffn_part,
            residual,
        ),
        layer_input.shape[0],
        layer_input.shape[1],
        hidden.shape[1],
        heads_width,
        key_width,
    )
    return (
        layer_out,
        input_grad,
        grad_query,
        grad_key,
        grad_value,
        grad_out,
        grad_gate.astype(F32),
        grad_up.astype(F32),
        grad_down.astype(F32),
        attn_gain[0],
        ffn_gain[0],
        head_gain[0, :HEAD_WIDTH],
        head_gain[0, HEAD_WIDTH:],
    )


def solution(mesh):
    in_specs = (
        P(("dp", "tensor"), None),
        P("dp", None),
        P(None, "tensor"),
        P(None, "tensor"),
        P(None, "tensor"),
        P("tensor", None),
        P(None, "tensor"),
        P(None, "tensor"),
        P("tensor", None),
        P(),
        P(),
        P(),
        P(),
        P(("dp", "tensor"), None),
    )
    out_specs = (
        P(("dp", "tensor"), None),
        P(("dp", "tensor"), None),
        P("dp", "tensor"),
        P("dp", "tensor"),
        P("dp", "tensor"),
        P("tensor", "dp"),
        P("dp", "tensor"),
        P("dp", "tensor"),
        P("tensor", "dp"),
        P(),
        P(),
        P(),
        P(),
    )
    sixteen = mesh.shape["dp"] == 8 and mesh.shape["tensor"] == 4
    return jax.shard_map(
        per_device_sixteen if sixteen else per_device, mesh=mesh, in_specs=in_specs, out_specs=out_specs, check_vma=False
    )
```

```python
import jax
import jax.numpy as jnp
import numpy as np
from jax import lax
from jax.experimental import pallas as pl
from jax.experimental.pallas import tpu as pltpu
from jax.sharding import PartitionSpec as P

HEADS = 32
KV = 8


EPSILON = 1e-06
ROPE_BASE = 10000.0
MASKED = -1e30


def norm_gain(row_block, gain_vec):
    factor = lax.rsqrt(jnp.mean(row_block * row_block, axis=-1, keepdims=True) + EPSILON)
    return row_block * factor * gain_vec


def rotate(vector, cosine, sine_table):
    half_width = vector.shape[-1] // 2
    first = vector[..., :half_width]
    second = vector[..., half_width:]
    return jnp.concatenate(
        [first * cosine - second * sine_table, second * cosine + first * sine_table], axis=-1
    )


def head_prep(raw_proj, gain_vec, cosine, sine_table):
    head_width = gain_vec.shape[0]
    per_head = raw_proj.reshape(raw_proj.shape[0], raw_proj.shape[1] // head_width, head_width)
    return rotate(norm_gain(per_head, gain_vec), cosine[:, None, :], sine_table[:, None, :])


def doc_layout(lengths, length):
    doc_ends = jnp.cumsum(lengths)
    places = jnp.arange(length, dtype=jnp.int32)
    passed_end = (places[:, None] >= doc_ends[None, :]).astype(jnp.int32)
    doc_ids = jnp.sum(passed_end, axis=1)
    starts = jnp.sum(passed_end * lengths[None, :], axis=1)
    return (doc_ids, places, places - starts)


def rope_tables(offsets, head_width):
    frequency = ROPE_BASE ** (-jnp.arange(0, head_width, 2, dtype=jnp.float32) / head_width)
    angles = offsets.astype(jnp.float32)[:, None] * frequency[None, :]
    return (jnp.cos(angles), jnp.sin(angles))


def swiglu(gate_proj, up_proj):
    return jax.nn.silu(gate_proj) * up_proj


def matmul_nt(left_mat, right_mat):
    return lax.dot_general(
        left_mat, right_mat, (((1,), (1,)), ((), ())), preferred_element_type=jnp.float32
    )


def matmul_tn(left_mat, right_mat):
    return lax.dot_general(
        left_mat, right_mat, (((0,), (0,)), ((), ())), preferred_element_type=jnp.float32
    )


def per_device(
    layer_input,
    doc_lengths,
    w_query,
    w_key,
    w_value,
    w_out,
    w_gate,
    w_up,
    w_down,
    gain_attn,
    gain_ffn,
    gain_query,
    gain_key,
    out_grad,
):
    tok_rows = layer_input.shape[0]
    head_width = gain_query.shape[0]
    tensor_count = lax.axis_size("tensor")
    length = tok_rows * tensor_count
    per_dev = w_query.shape[1] // head_width
    groups_dev = w_key.shape[1] // head_width
    input_f32 = layer_input.astype(jnp.float32)
    doc_ids, places, offsets = doc_layout(doc_lengths[0], length)
    cosine, sine_table = rope_tables(offsets, head_width)
    attn_in = lax.all_gather(
        norm_gain(input_f32, gain_attn).astype(jnp.bfloat16), "tensor", axis=0, tiled=True
    )
    query_raw = jnp.dot(attn_in, w_query, preferred_element_type=jnp.float32)
    key_raw = jnp.dot(attn_in, w_key, preferred_element_type=jnp.float32).astype(jnp.bfloat16)
    value_raw = jnp.dot(attn_in, w_value, preferred_element_type=jnp.float32).astype(jnp.bfloat16)
    key_f32 = key_raw.astype(jnp.float32)
    queries = head_prep(query_raw, gain_query, cosine, sine_table).astype(jnp.bfloat16)
    key_rot = head_prep(key_f32, gain_key, cosine, sine_table).astype(jnp.bfloat16)
    local_heads = jnp.arange(per_dev, dtype=jnp.int32)
    group_pick = (
        local_heads[:, None] // (HEADS // KV) == jnp.arange(groups_dev, dtype=jnp.int32)[None, :]
    ).astype(jnp.float32)
    pick_low = group_pick.astype(jnp.bfloat16)
    key_heads = jnp.einsum(
        "lgd,hg->lhd", key_rot, pick_low, preferred_element_type=jnp.float32
    ).astype(jnp.bfloat16)
    value_heads = jnp.einsum(
        "lgd,hg->lhd",
        value_raw.reshape(length, groups_dev, head_width),
        pick_low,
        preferred_element_type=jnp.float32,
    ).astype(jnp.bfloat16)
    block_rows = min(512, length)
    block_count = length // block_rows
    score_scale = head_width ** (-0.5)

    def block_scores(block_num):
        row_begin = block_num * block_rows
        query_block = lax.dynamic_slice_in_dim(queries, row_begin, block_rows, 0)
        ids_block = lax.dynamic_slice_in_dim(doc_ids, row_begin, block_rows, 0)
        places_block = lax.dynamic_slice_in_dim(places, row_begin, block_rows, 0)
        scores = (
            jnp.einsum("qhd,khd->hqk", query_block, key_heads, preferred_element_type=jnp.float32)
            * score_scale
        )
        allowed = (ids_block[:, None] == doc_ids[None, :]) & (
            places[None, :] <= places_block[:, None]
        )
        return (query_block, jnp.where(allowed[None], scores, MASKED))

    def forward_block(block_num):
        query_block, scores = block_scores(block_num)
        row_top = jnp.max(scores, axis=-1, keepdims=True)
        exponent = jnp.exp(scores - row_top)
        row_total = jnp.sum(exponent, axis=-1, keepdims=True)
        probabilities = (exponent / row_total).astype(jnp.bfloat16)
        mixed_block = jnp.einsum(
            "hqk,khd->qhd", probabilities, value_heads, preferred_element_type=jnp.float32
        )
        return (mixed_block, row_top + jnp.log(row_total))

    mixed_all, log_totals = lax.map(forward_block, jnp.arange(block_count, dtype=jnp.int32))
    attn_mixed = mixed_all.reshape(length, per_dev * head_width).astype(jnp.bfloat16)
    residual = input_f32 + lax.psum_scatter(
        jnp.dot(attn_mixed, w_out, preferred_element_type=jnp.float32).astype(jnp.bfloat16),
        "tensor",
        scatter_dimension=0,
        tiled=True,
    ).astype(jnp.float32)
    ffn_in = lax.all_gather(
        norm_gain(residual, gain_ffn).astype(jnp.bfloat16), "tensor", axis=0, tiled=True
    )
    gate_proj = jnp.dot(ffn_in, w_gate, preferred_element_type=jnp.float32)
    up_proj = jnp.dot(ffn_in, w_up, preferred_element_type=jnp.float32)
    hidden = swiglu(gate_proj, up_proj).astype(jnp.bfloat16)
    layer_out = (
        residual
        + lax.psum_scatter(
            jnp.dot(hidden, w_down, preferred_element_type=jnp.float32).astype(jnp.bfloat16),
            "tensor",
            scatter_dimension=0,
            tiled=True,
        ).astype(jnp.float32)
    ).astype(jnp.bfloat16)
    grad_rows = lax.all_gather(out_grad, "tensor", axis=0, tiled=True)
    hidden_grad = matmul_nt(grad_rows, w_down)
    grad_down = matmul_tn(hidden, grad_rows)
    unused_value, swiglu_back = jax.vjp(swiglu, gate_proj, up_proj)
    gate_grad, up_grad = swiglu_back(hidden_grad)
    gate_grad = gate_grad.astype(jnp.bfloat16)
    up_grad = up_grad.astype(jnp.bfloat16)
    grad_gate = matmul_tn(ffn_in, gate_grad)
    grad_up = matmul_tn(ffn_in, up_grad)
    ffn_in_grad = lax.psum_scatter(
        (matmul_nt(gate_grad, w_gate) + matmul_nt(up_grad, w_up)).astype(jnp.bfloat16),
        "tensor",
        scatter_dimension=0,
        tiled=True,
    ).astype(jnp.float32)
    unused_norm, ffn_norm_back = jax.vjp(norm_gain, residual, gain_ffn)
    residual_grad, gain_ffn_grad = ffn_norm_back(ffn_in_grad)
    residual_grad = residual_grad + out_grad.astype(jnp.float32)
    res_low = lax.all_gather(residual_grad.astype(jnp.bfloat16), "tensor", axis=0, tiled=True)
    mixed_grad = matmul_nt(res_low, w_out).astype(jnp.bfloat16).reshape(length, per_dev, head_width)
    grad_out = matmul_tn(attn_mixed, res_low)

    def backward_block(running, block_num):
        key_acc, value_acc = running
        query_block, scores = block_scores(block_num)
        probabilities = jnp.exp(scores - log_totals[block_num])
        grad_block = lax.dynamic_slice_in_dim(mixed_grad, block_num * block_rows, block_rows, 0)
        prob_grad = jnp.einsum(
            "qhd,khd->hqk", grad_block, value_heads, preferred_element_type=jnp.float32
        )
        value_acc = value_acc + jnp.einsum(
            "hqk,qhd->khd",
            probabilities.astype(jnp.bfloat16),
            grad_block,
            preferred_element_type=jnp.float32,
        )
        centre = jnp.sum(probabilities * prob_grad, axis=-1, keepdims=True)
        score_grad = (probabilities * (prob_grad - centre)).astype(jnp.bfloat16)
        query_part = (
            jnp.einsum("hqk,khd->qhd", score_grad, key_heads, preferred_element_type=jnp.float32)
            * score_scale
        )
        key_acc = (
            key_acc
            + jnp.einsum(
                "hqk,qhd->khd", score_grad, query_block, preferred_element_type=jnp.float32
            )
            * score_scale
        )
        return ((key_acc, value_acc), query_part)

    zeros_init = jnp.zeros((length, per_dev, head_width), jnp.float32)
    (key_acc, value_acc), query_parts = lax.scan(
        backward_block, (zeros_init, zeros_init), jnp.arange(block_count, dtype=jnp.int32)
    )
    query_rot_grad = query_parts.reshape(length, per_dev, head_width)
    unused_query, query_back = jax.vjp(
        lambda raw_proj, gain_vec: head_prep(raw_proj, gain_vec, cosine, sine_table),
        query_raw,
        gain_query,
    )
    query_raw_grad, gain_query_grad = query_back(query_rot_grad)
    query_low = query_raw_grad.astype(jnp.bfloat16)
    key_group_grad = jnp.einsum("lhd,hg->lgd", key_acc, group_pick, precision=lax.Precision.HIGHEST)
    value_group_grad = jnp.einsum(
        "lhd,hg->lgd", value_acc, group_pick, precision=lax.Precision.HIGHEST
    )
    unused_key, key_back = jax.vjp(
        lambda raw_proj, gain_vec: head_prep(raw_proj, gain_vec, cosine, sine_table),
        key_f32,
        gain_key,
    )
    key_raw_grad, gain_key_grad = key_back(key_group_grad)
    key_low = key_raw_grad.astype(jnp.bfloat16)
    value_low = value_group_grad.reshape(length, groups_dev * head_width).astype(jnp.bfloat16)
    grad_query = matmul_tn(attn_in, query_low)
    grad_key = matmul_tn(attn_in, key_low)
    grad_value = matmul_tn(attn_in, value_low)
    attn_in_grad = lax.psum_scatter(
        (
            matmul_nt(query_low, w_query)
            + matmul_nt(key_low, w_key)
            + matmul_nt(value_low, w_value)
        ).astype(jnp.bfloat16),
        "tensor",
        scatter_dimension=0,
        tiled=True,
    ).astype(jnp.float32)
    unused_attn, attn_norm_back = jax.vjp(norm_gain, input_f32, gain_attn)
    input_part, gain_attn_grad = attn_norm_back(attn_in_grad)
    input_grad = (input_part + residual_grad).astype(jnp.bfloat16)
    reduced = (
        lax.psum_scatter(
            grad_query.astype(jnp.bfloat16), "dp", scatter_dimension=0, tiled=True
        ).astype(jnp.float32),
        lax.psum_scatter(
            grad_key.astype(jnp.bfloat16), "dp", scatter_dimension=0, tiled=True
        ).astype(jnp.float32),
        lax.psum_scatter(
            grad_value.astype(jnp.bfloat16), "dp", scatter_dimension=0, tiled=True
        ).astype(jnp.float32),
        lax.psum_scatter(
            grad_out.astype(jnp.bfloat16), "dp", scatter_dimension=1, tiled=True
        ).astype(jnp.float32),
        lax.psum_scatter(
            grad_gate.astype(jnp.bfloat16), "dp", scatter_dimension=0, tiled=True
        ).astype(jnp.float32),
        lax.psum_scatter(
            grad_up.astype(jnp.bfloat16), "dp", scatter_dimension=0, tiled=True
        ).astype(jnp.float32),
        lax.psum_scatter(
            grad_down.astype(jnp.bfloat16), "dp", scatter_dimension=1, tiled=True
        ).astype(jnp.float32),
    )
    gain_sums = lax.psum(
        (gain_attn_grad, gain_ffn_grad, gain_query_grad, gain_key_grad), ("dp", "tensor")
    )
    return (
        layer_out,
        input_grad,
        reduced[0],
        reduced[1],
        reduced[2],
        reduced[3],
        reduced[4],
        reduced[5],
        reduced[6],
        gain_sums[0],
        gain_sums[1],
        gain_sums[2],
        gain_sums[3],
    )


MESH_ID = pl.DeviceIdType.MESH
ORDERS = (("x", "y", "z"), ("y", "z", "x"), ("z", "x", "y"))
LINKS = ("x", "y", "z", "core")
GRAD_PATHS = (("x", "y", "z"), ("x", "z", "y"), ("y", "z", "x"))
HEAD_WIDTH = 64
QUARTERS = (("y", "z"), ("y",), ("z",), ())
F32 = jnp.float32
BF16 = jnp.bfloat16


class Place:
    def __init__(self):
        row, column = lax.axis_index("dp"), lax.axis_index("tensor")
        self.far = row // 4
        self.at = {
            "z": (row // 2) % 2,
            "y": row % 2,
            "x": column // 2,
            "core": column % 2,
        }

    def flipped(self, names):
        return {
            name: 1 - value if name in names else value for name, value in self.at.items()
        }

    def device(self, names):
        names = (names,) if isinstance(names, str) else names
        at = self.flipped(names)
        far = 1 - self.far if "far" in names else self.far
        return {
            "dp": far * 4 + at["z"] * 2 + at["y"],
            "tensor": at["x"] * 2 + at["core"],
        }

    def column(self, names=()):
        at = self.flipped(names)
        return at["x"] * 2 + at["core"]

    def quarter(self, names=()):
        at = self.flipped(names)
        return at["z"] * 2 + at["y"]


def enter(place, names):
    barrier = pltpu.get_barrier_semaphore()
    for name in names:
        pl.semaphore_signal(
            barrier, inc=1, device_id=place.device(name), device_id_type=MESH_ID
        )
    pl.semaphore_wait(barrier, len(names))


class Sender:
    def __init__(self, place, send_sems, recv_sems):
        self.place, self.send_sems, self.recv_sems, self.used = place, send_sems, recv_sems, 0

    def copy(self, source, target, name):
        slot = self.used
        self.used += 1
        return pltpu.make_async_remote_copy(
            src_ref=source,
            dst_ref=target,
            send_sem=self.send_sems.at[slot],
            recv_sem=self.recv_sems.at[slot],
            device_id=self.place.device(name),
            device_id_type=MESH_ID,
        )


def part_rows(tokens):
    unit = tokens // 16
    first = -(-unit // 3)
    second = -(-(unit - first) // 2)
    return ((unit - first - second) * 16, first * 16, second * 16)


def part_starts(tokens):
    rows = part_rows(tokens)
    return (0, rows[0], rows[0] + rows[1])


def spot(tokens, part, half, core, index):
    rows, start = part_rows(tokens)[part], part_starts(tokens)[part]
    return half * 8 * tokens + 8 * start + core * 4 * rows + index * rows


def gather4(tokens, buffer, own, sender, place):
    mine = pl.ds(pl.multiple_of(place.column() * tokens, tokens), tokens)
    theirs = pl.ds(pl.multiple_of(place.column(("x",)) * tokens, tokens), tokens)
    return (
        sender.copy(own, buffer.at[mine], "x"),
        sender.copy(own, buffer.at[mine], "core"),
        sender.copy(buffer.at[theirs], buffer.at[theirs], "core"),
    )


def normed(values, gain):
    factor = lax.rsqrt(jnp.mean(values * values, axis=-1, keepdims=True) + EPSILON)
    return values * factor * gain


def norm_back(values, gain, grad):
    factor = lax.rsqrt(jnp.mean(values * values, axis=-1, keepdims=True) + EPSILON)
    unit = values * factor
    scaled = gain * grad
    back = factor * (scaled - unit * jnp.mean(scaled * unit, axis=-1, keepdims=True))
    return back, jnp.sum(grad * unit, axis=0, keepdims=True)


def scatter4(partial, from_core, from_x, tokens, sender, place):
    copies = []
    for names in (("x", "core"), ("core",)):
        shard = pl.ds(pl.multiple_of(place.column(names) * tokens, tokens), tokens)
        copies.append(
            sender.copy(partial.at[shard], from_core.at[len(copies)], "core")
        )
    return copies


def sum4(partial, from_core, outgoing, from_x, tokens, sender, place):
    copies = scatter4(partial, from_core, from_x, tokens, sender, place)
    for copy in copies:
        copy.start()
    far = pl.ds(pl.multiple_of(place.column(("x",)) * tokens, tokens), tokens)
    mine = pl.ds(pl.multiple_of(place.column() * tokens, tokens), tokens)
    copies[0].wait_recv()
    outgoing[...] = (partial[far, :].astype(F32) + from_core[0].astype(F32)).astype(BF16)
    along = sender.copy(outgoing, from_x, "x")
    along.start()
    copies[1].wait_recv()
    near = partial[mine, :].astype(F32) + from_core[1].astype(F32)
    along.wait_recv()
    total = near + from_x[...].astype(F32)
    for copy in copies:
        copy.wait_send()
    along.wait_send()
    return total


def silu_parts(gate, up, hidden_grad):
    s = 1.0 / (1.0 + jnp.exp(-gate))
    silu = gate * s
    hidden = silu * up
    gate_grad = hidden_grad * up * s * (1.0 + gate * (1.0 - s))
    return hidden, gate_grad, hidden_grad * silu


def start_where(condition, *copies_of):
    @pl.when(condition)
    def start():
        for copy in copies_of:
            copy.start()


def back_kernel(
    gain_ref,
    residual_ref,
    grad_ref,
    pair_all,
    hidden_all,
    gate_w,
    up_w,
    ffn_all,
    grad_all,
    back_ref,
    gain_back_ref,
    down_out,
    low_all,
    pair_sent_all,
    weights,
    pair,
    hidden,
    down_sent,
    down_came,
    down_blocks_came,
    pair_sent,
    ffn_half,
    grad_half,
    grad_own,
    products,
    from_core,
    third,
    second,
    first,
    own,
    send_sems,
    recv_sems,
    local_sems,
):
    tokens, width = residual_ref.shape
    units = hidden.shape[1]
    place = Place()
    columns = pl.ds(pl.multiple_of(place.quarter() * units, units), units)
    block_width = width // 8
    local_used = [0]

    def load(source, target):
        copy = pltpu.make_async_copy(source, target, local_sems.at[local_used[0]])
        local_used[0] += 1
        copy.start()
        return copy

    def half_lanes(which):
        return pl.ds(pl.multiple_of(which * (width // 2), width // 2), width // 2)

    def columns_of(names):
        start = place.quarter(names) * block_width
        return pl.ds(pl.multiple_of(start, block_width), block_width)

    half = 8 * tokens
    enter(place, LINKS + ("far", ("y", "z")))
    hidden_load = load(hidden_all, hidden)
    other_load = load(grad_all.at[:, half_lanes(1 - place.far)], grad_half)
    weight_loads = [
        load(gate_w.at[:, columns], weights.at[:, pl.ds(0, units)]),
        load(up_w.at[:, columns], weights.at[:, pl.ds(units, units)]),
        load(pair_all.at[pl.ds(half, half)], pair.at[pl.ds(half, half)]),
    ]
    pair_load = load(pair_all.at[pl.ds(0, half)], pair.at[pl.ds(0, half)])
    own_load = load(grad_all.at[:, half_lanes(place.far)], grad_own)
    ffn_load = load(ffn_all.at[:, half_lanes(1 - place.far)], ffn_half)
    sender = Sender(place, send_sems, recv_sems)
    part_list = [
        (part, part_rows(tokens)[part], part_starts(tokens)[part]) for part in range(3)
    ]

    def place_of(part, half_bit, core, index, count):
        return pl.ds(spot(tokens, part, half_bit, core, index), count)

    to_core = [
        [
            sender.copy(
                products.at[place_of(part, half_bit, 1, 0, 4 * rows)],
                from_core.at[pl.ds(half_bit * 4 * tokens + 4 * start, 4 * rows)],
                "core",
            )
            for part, rows, start in part_list
        ]
        for half_bit in range(2)
    ]
    far = [
        sender.copy(
            products.at[place_of(part, 1, 0, 0, 4 * rows)],
            third.at[pl.ds(4 * start, 4 * rows)],
            ORDERS[part][2],
        )
        for part, rows, start in part_list
    ]
    middle = [
        sender.copy(
            products.at[place_of(part, 0, 0, 2, 2 * rows)],
            second.at[pl.ds(2 * start, 2 * rows)],
            ORDERS[part][1],
        )
        for part, rows, start in part_list
    ]
    close = [
        sender.copy(
            products.at[place_of(part, 0, 0, 1, rows)],
            first.at[pl.ds(start, rows)],
            ORDERS[part][0],
        )
        for part, rows, start in part_list
    ]
    bulk = [sender.copy(down_sent.at[turn], down_came.at[turn], "far") for turn in range(4)]
    down_copies = [
        sender.copy(down_came.at[turn], down_blocks_came.at[turn], QUARTERS[turn])
        for turn in range(3)
    ]

    def down_product(turn):
        down_sent[turn] = matmul_tn(
            hidden[...], grad_half[:, columns_of(QUARTERS[turn])]
        ).astype(BF16)
        bulk[turn].start()

    def pair_product(turn):
        pair_sent[turn] = matmul_tn(
            ffn_half[:, columns_of(QUARTERS[turn])], pair[...]
        ).astype(BF16)

    def quarter_units(names):
        return pl.ds(pl.multiple_of(place.quarter(names) * units, units), units)

    def spread_down(turn):
        names = QUARTERS[turn]
        bulk[turn].wait_recv()
        total = matmul_tn(hidden[...], grad_own[:, columns_of(names)]) + down_came[
            turn
        ].astype(F32)
        if names:
            down_came[turn] = total.astype(BF16)
            down_copies[turn].start()
        else:
            down_out[quarter_units(()), :] = total.astype(BF16)

    def compute(part, half_bit):
        rows = part_rows(tokens)[part]
        span = place_of(part, half_bit, 0, 0, 8 * rows)
        products[span, :] = matmul_nt(pair[span, :], weights[...]).astype(BF16)
        to_core[half_bit][part].start()

    def add_in(rows, arrived):
        products[rows, :] = (
            products[rows, :].astype(F32) + arrived.astype(F32)
        ).astype(BF16)

    def add_core(part, half_bit):
        rows, start = part_rows(tokens)[part], part_starts(tokens)[part]
        to_core[half_bit][part].wait_recv()
        add_in(
            place_of(part, half_bit, 0, 0, 4 * rows),
            from_core[pl.ds(half_bit * 4 * tokens + 4 * start, 4 * rows), :],
        )

    hidden_load.wait()
    other_load.wait()
    down_product(0)
    for copy in weight_loads:
        copy.wait()
    compute(0, 1)
    compute(1, 1)
    add_core(0, 1)
    far[0].start()
    compute(2, 1)
    add_core(1, 1)
    far[1].start()
    pair_load.wait()
    compute(0, 0)
    add_core(2, 1)
    far[2].start()
    down_product(1)
    compute(1, 0)
    compute(2, 0)
    for part in range(3):
        add_core(part, 0)
    ffn_load.wait()
    own_load.wait()
    pair_product(0)
    pair_product(1)
    pair_product(2)
    order = (0, 1, 2)
    for part in order:
        rows, start = part_rows(tokens)[part], part_starts(tokens)[part]
        far[part].wait_recv()
        add_in(
            place_of(part, 0, 0, 2, 2 * rows),
            third[pl.ds(4 * start + 2 * rows, 2 * rows), :],
        )
        middle[part].start()
        add_in(place_of(part, 0, 0, 0, 2 * rows), third[pl.ds(4 * start, 2 * rows), :])
    down_product(2)
    spread_down(0)
    pair_product(3)
    pair_stores = [load(pair_sent.at[turn], pair_sent_all.at[turn]) for turn in range(4)]
    for part in order:
        rows, start = part_rows(tokens)[part], part_starts(tokens)[part]
        middle[part].wait_recv()
        add_in(place_of(part, 0, 0, 1, rows), second[pl.ds(2 * start + rows, rows), :])
        close[part].start()
        add_in(place_of(part, 0, 0, 0, rows), second[pl.ds(2 * start, rows), :])
    down_product(3)
    spread_down(1)
    gain_total = jnp.zeros(gain_ref.shape, F32)
    mine = pl.multiple_of(place.column() * tokens, tokens)
    theirs = pl.multiple_of(place.column(("x",)) * tokens, tokens)
    row_copies = []
    own_stores = []
    for part in order:
        rows, start = part_rows(tokens)[part], part_starts(tokens)[part]
        close[part].wait_recv()
        span = pl.ds(start, rows)
        ffn_in_grad = products[place_of(part, 0, 0, 0, rows), :].astype(F32) + first[
            span, :
        ].astype(F32)
        back, gain_part = norm_back(residual_ref[span, :], gain_ref[...], ffn_in_grad)
        back = back + grad_ref[span, :].astype(F32)
        back_ref[span, :] = back
        own[span, :] = back.astype(BF16)
        gain_total = gain_total + gain_part
        target = low_all.at[pl.ds(mine + start, rows)]
        other = low_all.at[pl.ds(theirs + start, rows)]
        row_copies.append(
            (
                sender.copy(own.at[span], target, "x"),
                sender.copy(own.at[span], target, "core"),
                sender.copy(other, other, "core"),
            )
        )
        row_copies[-1][0].start()
        row_copies[-1][1].start()
        own_stores.append(load(own.at[span], target))
    gain_back_ref[...] = gain_total
    spread_down(2)
    for copies_of in row_copies:
        copies_of[0].wait_recv()
        copies_of[2].start()
    spread_down(3)
    for turn, copy in enumerate(down_copies):
        copy.wait_recv()
        down_out[quarter_units(QUARTERS[turn]), :] = down_blocks_came[turn]
    for copies_of in row_copies:
        copies_of[1].wait_recv()
        copies_of[2].wait_recv()
    for copy in own_stores + pair_stores:
        copy.wait()
    for copies_of in row_copies:
        for copy in copies_of:
            copy.wait_send()
    for copy in to_core[0] + to_core[1] + far + middle + close + bulk + down_copies:
        copy.wait_send()


def swap_halves(values, head_width):
    width = values.shape[1]
    half = head_width // 2
    lane = lax.broadcasted_iota(jnp.int32, values.shape, 1)
    return jnp.where(
        lane % head_width < half,
        pltpu.roll(values, width - half, 1),
        pltpu.roll(values, half, 1),
    )


def head_means(values, head_width):
    width = values.shape[1]
    rows = lax.broadcasted_iota(jnp.int32, (width, width), 0) // head_width
    columns = lax.broadcasted_iota(jnp.int32, (width, width), 1) // head_width
    blocks = jnp.where(rows == columns, 1.0 / head_width, 0.0).astype(BF16)
    upper = values.astype(BF16)
    lower = (values - upper.astype(F32)).astype(BF16)
    return jnp.dot(upper, blocks, preferred_element_type=F32) + jnp.dot(
        lower, blocks, preferred_element_type=F32
    )


def widen(table, width):
    return jnp.concatenate([table] * (width // table.shape[1]), axis=1)


def head_back(grad, raw, gain, cosine, sine, head_width):
    width = grad.shape[1]
    back = grad * widen(cosine, width) - swap_halves(grad, head_width) * widen(sine, width)
    factor = lax.rsqrt(head_means(raw * raw, head_width) + EPSILON)
    unit = raw * factor
    scaled = gain * back
    result = factor * (scaled - unit * head_means(scaled * unit, head_width))
    return result, jnp.sum(back * unit, axis=0, keepdims=True)


def fold_heads(row, head_width):
    total = row[:, :128]
    for start in range(128, row.shape[1], 128):
        total = total + row[:, start : start + 128]
    return total + pltpu.roll(total, head_width, 1)


def runs16(order, path, step):
    place_of = {
        name: position for position, name in enumerate(order)
    }
    known = [set(chosen) for chosen in subsets(path[:step])]
    moves = []
    for flips in known:
        spots = []
        for names in (flips, flips | {path[step]}):
            bits = [int(name in names) for name in order]
            spots.append((bits[2], bits[0] + 2 * bits[1]))
        moves.append(spots)
    moves.sort()
    runs = []
    for (half, index), (to_half, to_index) in moves:
        if runs:
            last = runs[-1]
            if (
                last[0] == half
                and last[2] == to_half
                and last[1] + last[4] == index
                and last[3] + last[4] == to_index
            ):
                last[4] += 1
                continue
        runs.append([half, index, to_half, to_index, 1])
    return runs


def subsets(names):
    result = [()]
    for name in names:
        result = result + [chosen + (name,) for chosen in result]
    return result


def gather16(tokens, buffer, own, sender, paths):
    links, cores = [], []
    for part, order in enumerate(ORDERS):
        rows, start = part_rows(tokens)[part], part_starts(tokens)[part]

        def region(half, index, count, core=0):
            return buffer.at[pl.ds(spot(tokens, part, half, core, index), count * rows)]

        mine = region(0, 0, 1) if own is None else own.at[pl.ds(start, rows)]
        part_links = []
        part_cores = [[sender.copy(mine, region(0, 0, 1, 1), "core")]]
        for step in range(3):
            step_links, step_cores = [], []
            for half, index, to_half, to_index, count in runs16(order, paths[part], step):
                source = mine if step == 0 else region(half, index, count)
                step_links.append(
                    sender.copy(source, region(to_half, to_index, count), paths[part][step])
                )
                step_cores.append(
                    sender.copy(
                        region(to_half, to_index, count),
                        region(to_half, to_index, count, 1),
                        "core",
                    )
                )
            part_links.append(step_links)
            part_cores.append(step_cores)
        links.append(part_links)
        cores.append(part_cores)
    return links, cores


def gather_begin(links, cores):
    for part in range(3):
        for copy in links[part][0] + cores[part][0]:
            copy.start()


def gather_go(links, cores, step, parts=(0, 1, 2)):
    for part in parts:
        for copy in links[part][step]:
            copy.wait_recv()
        if step < 2:
            for copy in links[part][step + 1]:
                copy.start()
        for copy in cores[part][step + 1]:
            copy.start()


def gather_sent(links, cores):
    for part in range(3):
        for copies in links[part] + cores[part]:
            for copy in copies:
                copy.wait_send()


def document_tables(lengths_ref, frequency, length):
    down = lax.broadcasted_iota(jnp.int32, (length, 128), 0)
    across_lanes = lax.broadcasted_iota(jnp.int32, (8, length), 1)
    ids_down = jnp.zeros((length, 128), jnp.int32)
    starts = jnp.zeros((length, 128), jnp.int32)
    ids_across = jnp.zeros((8, length), jnp.int32)
    end = jnp.int32(0)
    for document in range(lengths_ref.shape[1]):
        count = lengths_ref[0, document]
        end = end + count
        passed = down >= end
        ids_down = ids_down + jnp.where(passed, 1, 0)
        starts = starts + jnp.where(passed, count, 0)
        ids_across = ids_across + jnp.where(across_lanes >= end, 1, 0)
    angles = (down - starts).astype(F32) * frequency
    return ids_down[:, :1], ids_across[:1, :], angles


def document_bias(ids_down, ids_across, length):
    allowed = (ids_down == ids_across) & (
        lax.broadcasted_iota(jnp.int32, (length, length), 1)
        <= lax.broadcasted_iota(jnp.int32, (length, length), 0)
    )
    return jnp.where(allowed, 0.0, MASKED)


def head_forward(raw, gain, cosine, sine, head_width):
    factor = lax.rsqrt(head_means(raw * raw, head_width) + EPSILON)
    values = raw * factor * gain
    width = raw.shape[1]
    return values * widen(cosine, width) + swap_halves(values, head_width) * widen(sine, width)


def forward_kernel(
    lengths_ref,
    input_ref,
    gain_attn,
    gain_ffn,
    gain_query,
    gain_key,
    frequency,
    out_grad,
    query_w,
    key_w,
    value_w,
    out_w,
    gate_w,
    up_w,
    down_w,
    attn_all,
    mixed_ref,
    query_ref,
    key_ref,
    value_ref,
    query_raw,
    key_raw,
    totals_ref,
    cosine_ref,
    sine_ref,
    residual_ref,
    ffn_all,
    grad_all,
    hidden_all,
    pair_all,
    rows_all,
    own,
    hidden_ref,
    pair_ref,
    attn_in,
    qkv_w,
    out_v,
    bias,
    partial,
    from_core,
    outgoing,
    from_x,
    ffn_buf,
    grad_buf,
    gate_v,
    up_v,
    down_v,
    send_sems,
    recv_sems,
    local_sems,
):
    tokens, width = input_ref.shape
    length = 4 * tokens
    units = gate_v.shape[1]
    heads_width, key_width = query_ref.shape[1], key_ref.shape[1]
    place = Place()
    columns = pl.ds(pl.multiple_of(place.quarter() * units, units), units)
    local_used = [0]

    def load(source, target):
        copy = pltpu.make_async_copy(source, target, local_sems.at[local_used[0]])
        local_used[0] += 1
        copy.start()
        return copy

    enter(place, LINKS)
    sender = Sender(place, send_sems, recv_sems)
    own[...] = normed(input_ref[...].astype(F32), gain_attn[...]).astype(BF16)
    row_copies = gather4(tokens, attn_in, own, sender, place)
    row_copies[0].start()
    row_copies[1].start()
    grad_links, grad_cores = gather16(tokens, grad_buf, out_grad, sender, GRAD_PATHS)
    gather_begin(grad_links, grad_cores)
    first_loads = [
        load(query_w, qkv_w.at[:, pl.ds(0, heads_width)]),
        load(key_w, qkv_w.at[:, pl.ds(heads_width, key_width)]),
        load(value_w, qkv_w.at[:, pl.ds(heads_width + key_width, key_width)]),
        load(out_w, out_v),
    ]
    mine = pl.ds(pl.multiple_of(place.column() * tokens, tokens), tokens)
    attn_in[mine, :] = own[...]
    grad_loads = []
    for part in range(3):
        rows, start = part_rows(tokens)[part], part_starts(tokens)[part]
        grad_loads.append(
            load(
                out_grad.at[pl.ds(start, rows)],
                grad_buf.at[pl.ds(spot(tokens, part, 0, 0, 0), rows)],
            )
        )
    later_loads = [
        load(gate_w.at[:, columns], gate_v),
        load(up_w.at[:, columns], up_v),
        load(down_w.at[columns, :], down_v),
    ]
    ids_down, ids_across, angles = document_tables(lengths_ref, frequency[...], length)
    lane = lax.broadcasted_iota(jnp.int32, (length, 128), 1)
    cosine_ref[...] = jnp.cos(angles)
    sine = jnp.sin(angles)
    sine_ref[...] = jnp.where(lane % HEAD_WIDTH < HEAD_WIDTH // 2, -sine, sine)
    bias[...] = document_bias(ids_down, ids_across, length)
    for copy in first_loads + grad_loads:
        copy.wait()
    gather_go(grad_links, grad_cores, 0, (2,))
    row_copies[0].wait_recv()
    row_copies[2].start()
    row_copies[1].wait_recv()
    row_copies[2].wait_recv()
    attn_store = load(attn_in, attn_all)
    gather_go(grad_links, grad_cores, 1, (2,))

    raw = jnp.dot(attn_in[...], qkv_w[...], preferred_element_type=F32)
    query_raw[...] = raw[:, :heads_width]
    key_raw[...] = raw[:, heads_width : heads_width + key_width].astype(BF16).astype(F32)
    value_ref[...] = raw[:, heads_width + key_width :].astype(BF16)
    query_ref[...] = head_forward(
        query_raw[...], widen(gain_query[...], heads_width), cosine_ref[...], sine_ref[...], HEAD_WIDTH
    ).astype(BF16)
    key_ref[...] = head_forward(
        key_raw[...], widen(gain_key[...], key_width), cosine_ref[...], sine_ref[...], HEAD_WIDTH
    ).astype(BF16)
    gather_go(grad_links, grad_cores, 0, (0, 1))
    scale = HEAD_WIDTH ** (-0.5)
    group_heads = HEADS // KV
    mixed_parts = []
    head_total = heads_width // HEAD_WIDTH
    for head in range(head_total):
        group = head // group_heads
        group_lanes = slice(group * HEAD_WIDTH, (group + 1) * HEAD_WIDTH)
        scores = (
            matmul_nt(
                query_ref[:, head * HEAD_WIDTH : (head + 1) * HEAD_WIDTH],
                key_ref[:, group_lanes],
            )
            * scale
            + bias[...]
        )
        top = jnp.max(scores, axis=-1, keepdims=True)
        exponent = jnp.exp(scores - top)
        total = jnp.sum(exponent, axis=-1, keepdims=True)
        probs = (exponent * (1.0 / total)).astype(BF16)
        mixed_parts.append(
            jnp.dot(probs, value_ref[:, group_lanes], preferred_element_type=F32)
        )
        totals_ref[:, head : head + 1] = top + jnp.log(total)
        if head % 2 == 1:
            mixed_ref[:, (head - 1) * HEAD_WIDTH : (head + 1) * HEAD_WIDTH] = (
                jnp.concatenate(mixed_parts, axis=1).astype(BF16)
            )
            mixed_parts = []
        if head == head_total - 2:
            gather_go(grad_links, grad_cores, 1, (0, 1))
    partial[...] = jnp.dot(mixed_ref[...], out_v[...], preferred_element_type=F32).astype(BF16)

    residual = input_ref[...].astype(F32) + sum4(
        partial, from_core, outgoing, from_x, tokens, sender, place
    )
    residual_ref[...] = residual
    for copy in row_copies:
        copy.wait_send()
    own[...] = normed(residual, gain_ffn[...]).astype(BF16)
    for part in range(3):
        rows, start = part_rows(tokens)[part], part_starts(tokens)[part]
        ffn_buf[pl.ds(spot(tokens, part, 0, 0, 0), rows), :] = own[pl.ds(start, rows), :]
    links, cores = gather16(tokens, ffn_buf, None, sender, ORDERS)
    gather_begin(links, cores)
    gather_go(grad_links, grad_cores, 2)
    gather_go(links, cores, 0)
    for copy in later_loads:
        copy.wait()
    for part in range(3):
        for step_copies in grad_cores[part]:
            for copy in step_copies:
                copy.wait_recv()
    grad_store = load(grad_buf, grad_all)
    gather_go(links, cores, 1)
    for part in range(3):
        for step_copies in cores[part][:3]:
            for copy in step_copies:
                copy.wait_recv()

    block = 2 * tokens

    def compute(index):
        rows = pl.ds(pl.multiple_of(index * block, block), block)
        values = ffn_buf[rows, :]
        gate = jnp.dot(values, gate_v[...], preferred_element_type=F32)
        up = jnp.dot(values, up_v[...], preferred_element_type=F32)
        hidden_grad = matmul_nt(grad_buf[rows, :], down_v[...])
        hidden, gate_grad, up_grad = silu_parts(gate, up, hidden_grad)
        hidden_ref[rows, :] = hidden.astype(BF16)
        pair_ref[rows, :units] = gate_grad.astype(BF16)
        pair_ref[rows, units:] = up_grad.astype(BF16)

    half = 8 * tokens
    stores = [attn_store, grad_store]

    def store_half(which):
        rows = pl.ds(which * half, half)
        stores.append(load(hidden_ref.at[rows], hidden_all.at[rows]))
        stores.append(load(pair_ref.at[rows], pair_all.at[rows]))
        for part, order in enumerate(ORDERS):
            count, start = part_rows(tokens)[part], part_starts(tokens)[part]
            for core in range(2):
                for index in range(4):
                    bits = (index % 2, index // 2, which)
                    flips = tuple(name for name, bit in zip(order, bits) if bit)
                    row = ("z" in flips) * 2 + ("y" in flips)
                    names = tuple(n for n in flips if n == "x") + (("core",) if core else ())
                    target = row * 4 * tokens + place.column(names) * tokens + start
                    stores.append(
                        load(
                            hidden_ref.at[
                                pl.ds(spot(tokens, part, which, core, index), count)
                            ],
                            rows_all.at[pl.ds(pl.multiple_of(target, 16), count)],
                        )
                    )

    stores.append(load(ffn_buf.at[pl.ds(0, half)], ffn_all.at[pl.ds(0, half)]))
    pl.loop(0, 4)(compute)
    gather_go(links, cores, 2)
    store_half(0)
    for part in range(3):
        for copy in cores[part][3]:
            copy.wait_recv()
    stores.append(load(ffn_buf.at[pl.ds(half, half)], ffn_all.at[pl.ds(half, half)]))
    pl.loop(4, 8)(compute)
    store_half(1)
    for copy in stores:
        copy.wait()
    gather_sent(grad_links, grad_cores)
    gather_sent(links, cores)


GAIN_LINKS = ("core", "x", "y", "z", "far")


class RowSum:
    def __init__(self, partial, from_core, outgoing, from_x, tokens, sender, place):
        self.partial, self.from_core = partial, from_core
        self.outgoing, self.from_x = outgoing, from_x
        self.far = pl.ds(pl.multiple_of(place.column(("x",)) * tokens, tokens), tokens)
        self.mine = pl.ds(pl.multiple_of(place.column() * tokens, tokens), tokens)
        self.copies = scatter4(partial, from_core, from_x, tokens, sender, place)
        self.along = sender.copy(outgoing, from_x, "x")

    def begin(self):
        for copy in self.copies:
            copy.start()

    def send_on(self):
        self.copies[0].wait_recv()
        self.outgoing[...] = (
            self.partial[self.far, :].astype(F32) + self.from_core[0].astype(F32)
        ).astype(BF16)
        self.along.start()

    def total(self):
        self.copies[1].wait_recv()
        near = self.partial[self.mine, :].astype(F32) + self.from_core[1].astype(F32)
        self.along.wait_recv()
        total = near + self.from_x[...].astype(F32)
        for copy in self.copies:
            copy.wait_send()
        self.along.wait_send()
        return total


def finish_kernel(
    low_all,
    out_w,
    query_w,
    key_w,
    value_w,
    down_w,
    attn_all,
    pair_all,
    ffn_all,
    rows_all,
    pair_sent,
    mixed_ref,
    query_ref,
    key_ref,
    value_ref,
    query_raw,
    key_raw,
    totals_ref,
    cosine_ref,
    sine_ref,
    lengths_ref,
    gain_query,
    gain_key,
    gain_attn,
    input_ref,
    back_ref,
    ffn_gain_ref,
    residual_ref,
    layer_ref,
    input_grad_ref,
    query_out,
    key_out,
    value_out,
    out_out,
    gate_out,
    up_out,
    attn_gain_out,
    ffn_gain_out,
    head_gain_out,
    low,
    out_v,
    qkv_w,
    attn_in,
    pair,
    columns_v,
    bias,
    mixed_grad,
    mixed_peer,
    qkv_low,
    qkv_peer,
    attn_peer,
    low_peer,
    out_near,
    out_near_came,
    out_far,
    out_far_came,
    qkv_near,
    qkv_near_came,
    qkv_far,
    qkv_far_came,
    out_part,
    qkv_part,
    pair_blocks,
    pair_blocks_came,
    rows_came,
    from_core,
    outgoing,
    from_x,
    near_layer,
    near_layer_came,
    sums,
    came,
    send_sems,
    recv_sems,
    local_sems,
):
    tokens, width = input_ref.shape
    length = 4 * tokens
    units = pair.shape[1] // 2
    heads_width = query_ref.shape[1]
    key_width = key_ref.shape[1]
    head_width = HEAD_WIDTH
    group_heads = HEADS // KV
    groups = key_width // head_width
    block = width // 8
    place = Place()
    y, z, far = place.at["y"], place.at["z"], place.far
    sender = Sender(place, send_sems, recv_sems)
    local_used = [0]

    def load(source, target):
        copy = pltpu.make_async_copy(source, target, local_sems.at[local_used[0]])
        local_used[0] += 1
        copy.start()
        return copy

    def lanes(start, count):
        return pl.ds(pl.multiple_of(start, count), count)

    def quarter_lanes(names):
        return lanes(place.quarter(names) * block, block)

    def quarter_units(names):
        return lanes(place.quarter(names) * units, units)

    def own_half(source):
        return source.at[:, lanes(far * (width // 2), width // 2)]

    enter(place, GAIN_LINKS + (("y", "z"),))
    mine = lanes(place.column() * tokens, tokens)
    bulk = [sender.copy(pair_sent.at[turn], pair_blocks.at[turn], "far") for turn in range(4)]
    inner, outer = far != z, far == z
    start_where(outer, bulk[0])
    start_where(inner, bulk[0], bulk[1], bulk[2], bulk[3])
    mixed_copy = sender.copy(mixed_ref, mixed_peer, "y")

    def to_peer(source, target):
        return [
            sender.copy(
                source.at[mine, lanes((index * 2 + 1 - y) * block, block)],
                target.at[mine, pl.ds(index * block, block)],
                "y",
            )
            for index in range(4)
        ]

    low_peers = to_peer(low_all, low_peer)
    attn_peers = to_peer(attn_all, attn_peer)
    for copy in low_peers + attn_peers:
        copy.start()
    mixed_copy.start()
    low_load = load(low_all, low)
    out_load = load(out_w, out_v)
    attn_load = load(attn_all, attn_in)
    own_load = load(own_half(ffn_all), columns_v)
    pair_load = load(pair_all, pair)
    qkv_loads = [
        load(query_w, qkv_w.at[:, pl.ds(0, heads_width)]),
        load(key_w, qkv_w.at[:, pl.ds(heads_width, key_width)]),
        load(value_w, qkv_w.at[:, pl.ds(heads_width + key_width, key_width)]),
    ]
    row_loads = [
        load(rows_all.at[pl.ds(0, length)], rows_came.at[0]),
        load(rows_all.at[pl.ds(2 * length, length)], rows_came.at[2]),
    ]
    row_copies = [
        sender.copy(rows_all.at[pl.ds(offset * length, length)], rows_came.at[offset], "y")
        for offset in (1, 3)
    ]

    low_load.wait()
    out_load.wait()
    mixed_grad[...] = matmul_nt(low[...], out_v[...]).astype(BF16)
    ids_down, ids_across, unused_angles = document_tables(
        lengths_ref, jnp.ones((1, 128), F32), length
    )
    bias[...] = document_bias(ids_down, ids_across, length)
    low_gather = gather4(tokens, low_peer, low_peer.at[mine], sender, place)
    attn_gather = gather4(tokens, attn_peer, attn_peer.at[mine], sender, place)

    def peers_arrived():
        for copy in low_peers + attn_peers:
            copy.wait_recv()
        for copies_of in (low_gather, attn_gather):
            copies_of[0].start()
            copies_of[1].start()

    def peers_go_on():
        low_gather[0].wait_recv()
        low_gather[2].start()

    scale = head_width ** (-0.5)
    key_parts, value_parts, query_gain = [], [], [None]
    peer_copies = []

    def attention_group(group, between=None):
        group_lanes = slice(group * head_width, (group + 1) * head_width)
        key, value = key_ref[:, group_lanes], value_ref[:, group_lanes]
        key_grad = jnp.zeros((length, head_width), F32)
        value_grad = jnp.zeros((length, head_width), F32)
        query_parts = []
        for head in range(group * group_heads, (group + 1) * group_heads):
            head_lanes = slice(head * head_width, (head + 1) * head_width)
            query, grad = query_ref[:, head_lanes], mixed_grad[:, head_lanes]
            scores = matmul_nt(query, key) * scale + bias[...]
            probs = jnp.exp(scores - totals_ref[:, head : head + 1])
            prob_grad = matmul_nt(grad, value)
            value_grad = value_grad + matmul_tn(probs.astype(BF16), grad)
            centre = jnp.sum(probs * prob_grad, axis=-1, keepdims=True)
            score_grad = (probs * (prob_grad - centre)).astype(BF16)
            query_parts.append(jnp.dot(score_grad, key, preferred_element_type=F32) * scale)
            key_grad = key_grad + matmul_tn(score_grad, query) * scale
            if between and between[head - group * group_heads]:
                between[head - group * group_heads]()
        key_parts.append(key_grad)
        value_parts.append(value_grad)
        wide = slice(group * group_heads * head_width, (group + 1) * group_heads * head_width)
        query_grad, gain_part = head_back(
            jnp.concatenate(query_parts, axis=1),
            query_raw[:, wide],
            widen(gain_query[...], group_heads * head_width),
            cosine_ref[...],
            sine_ref[...],
            head_width,
        )
        gain_part = fold_heads(gain_part, head_width)
        query_gain[0] = gain_part if query_gain[0] is None else query_gain[0] + gain_part
        qkv_low[:, wide] = query_grad.astype(BF16)
        copy = sender.copy(qkv_low.at[:, wide], qkv_peer.at[:, wide], "y")
        copy.start()
        peer_copies.append(copy)

    attention_group(0, (None, peers_arrived, None, peers_go_on))
    row_copies[0].start()

    attn_gather[0].wait_recv()
    attn_gather[2].start()
    low_gather[1].wait_recv()
    low_gather[2].wait_recv()
    mixed_copy.wait_recv()

    def out_total(index):
        return matmul_tn(
            mixed_ref[...], low[:, lanes((index * 2 + y) * block, block)]
        ) + matmul_tn(mixed_peer[...], low_peer[:, lanes(index * block, block)])

    near_copies = []
    for turn, half in enumerate((1 - far, far)):
        out_near[turn] = out_total(half * 2 + 1 - z).astype(BF16)
        copy = sender.copy(out_near.at[turn], out_near_came.at[turn], "z")
        copy.start()
        near_copies.append(copy)
    start_where(outer, bulk[1])
    out_part[...] = out_total((1 - far) * 2 + z)
    out_out[...] = out_total(far * 2 + z)

    for group in range(1, groups):
        attention_group(group)
    key_back, key_gain = head_back(
        jnp.concatenate(key_parts, axis=1),
        key_raw[...],
        widen(gain_key[...], key_width),
        cosine_ref[...],
        sine_ref[...],
        head_width,
    )
    key_gain = fold_heads(key_gain, head_width)
    qkv_low[:, heads_width : heads_width + key_width] = key_back.astype(BF16)
    qkv_low[:, heads_width + key_width :] = jnp.concatenate(value_parts, axis=1).astype(BF16)
    tail = slice(heads_width, heads_width + 2 * key_width)
    peer_copies.append(sender.copy(qkv_low.at[:, tail], qkv_peer.at[:, tail], "y"))
    peer_copies[-1].start()
    row_copies[1].start()

    partial = out_v
    for copy in qkv_loads:
        copy.wait()

    def part_of(index):
        columns = lanes(index * 512, 512)
        partial[:, columns] = matmul_nt(qkv_low[...], qkv_w[columns, :]).astype(BF16)

    pl.loop(0, width // 512)(part_of)
    attn_sum = RowSum(partial, from_core.at[0], outgoing.at[0], from_x.at[0], tokens, sender, place)
    attn_sum.begin()

    own_load.wait()
    pair_load.wait()
    pair_copies = []

    def spread_pair(turn):
        names = QUARTERS[turn]
        bulk[turn].wait_recv()
        total = matmul_tn(columns_v[:, quarter_lanes(names)], pair[...]) + pair_blocks[
            turn
        ].astype(F32)
        if names:
            pair_blocks[turn] = total.astype(BF16)
            copy = sender.copy(pair_blocks.at[turn], pair_blocks_came.at[turn], names)
            copy.start()
            pair_copies.append(copy)
        else:
            gate_out[:, quarter_units(())] = total[:, :units].astype(BF16)
            up_out[:, quarter_units(())] = total[:, units:].astype(BF16)

    spread_pair(0)
    start_where(outer, bulk[2])
    attn_sum.send_on()

    attn_load.wait()
    for copy in peer_copies + list(attn_gather[1:]):
        copy.wait_recv()

    def qkv_total(index):
        return matmul_tn(
            attn_in[:, lanes((index * 2 + y) * block, block)], qkv_low[...]
        ) + matmul_tn(attn_peer[:, lanes(index * block, block)], qkv_peer[...])

    for turn, half in enumerate((1 - far, far)):
        qkv_near[turn] = qkv_total(half * 2 + 1 - z).astype(BF16)
        copy = sender.copy(qkv_near.at[turn], qkv_near_came.at[turn], "z")
        copy.start()
        near_copies.append(copy)
    near_copies[0].wait_recv()
    out_far[...] = (out_part[...] + out_near_came[0].astype(F32)).astype(BF16)
    out_far_copy = sender.copy(out_far, out_far_came, "far")
    out_far_copy.start()
    start_where(outer, bulk[3])
    qkv_part[...] = qkv_total((1 - far) * 2 + z)
    own_qkv = qkv_total(far * 2 + z)
    query_out[...] = own_qkv[:, :heads_width]
    key_out[...] = own_qkv[:, heads_width : heads_width + key_width]
    value_out[...] = own_qkv[:, heads_width + key_width :]

    attn_grad = attn_sum.total()
    back, attn_gain = norm_back(input_ref[...].astype(F32), gain_attn[...], attn_grad)
    input_grad_ref[...] = (back + back_ref[...]).astype(BF16)
    sums[0, :, :width] = attn_gain
    sums[0, :, width : 2 * width] = ffn_gain_ref[...]
    lane = lax.broadcasted_iota(jnp.int32, (1, 128), 1)
    sums[0, :, 2 * width :] = jnp.where(lane < head_width, query_gain[0], key_gain)
    gain_copies = []

    def gain_begin(step):
        if step:
            gain_copies[-1].wait()
            sums[step] = sums[step - 1] + came[step - 1]
        if step < len(GAIN_LINKS):
            copy = sender.copy(sums.at[step], came.at[step], GAIN_LINKS[step])
            copy.start()
            gain_copies.append(copy)

    gain_begin(0)
    near_copies[2].wait_recv()
    qkv_far[...] = (qkv_part[...] + qkv_near_came[0].astype(F32)).astype(BF16)
    qkv_far_copy = sender.copy(qkv_far, qkv_far_came, "far")
    qkv_far_copy.start()
    spread_pair(1)

    layer_parts = (low, out_v)
    for copy in row_loads:
        copy.wait()
    for copy in row_copies:
        copy.wait_recv()

    def down_loads(chunk):
        return [
            load(
                down_w.at[quarter_units(names), pl.ds(chunk * 512, 512)],
                qkv_w.at[pl.ds((chunk % 2) * 2 * units + turn * units, units), pl.ds(0, 512)],
            )
            for turn, names in enumerate(((), ("y",)))
        ]

    chunks = width // 512
    pending = down_loads(0)
    for chunk in range(chunks):
        columns = pl.ds(chunk * 512, 512)
        for copy in pending:
            copy.wait()
        if chunk + 1 < chunks:
            pending = down_loads(chunk + 1)
        base = (chunk % 2) * 2 * units
        for target, first in ((layer_parts[0], 2), (layer_parts[1], 0)):
            target[:, columns] = (
                jnp.dot(
                    rows_came[first],
                    qkv_w[pl.ds(base, units), pl.ds(0, 512)],
                    preferred_element_type=F32,
                )
                + jnp.dot(
                    rows_came[first + 1],
                    qkv_w[pl.ds(base + units, units), pl.ds(0, 512)],
                    preferred_element_type=F32,
                )
            ).astype(BF16)
    gain_begin(1)
    layer_sums = [
        RowSum(
            layer_parts[turn],
            from_core.at[turn + 1],
            outgoing.at[turn + 1],
            from_x.at[turn + 1],
            tokens,
            sender,
            place,
        )
        for turn in range(2)
    ]
    layer_sums[0].begin()
    layer_sums[1].begin()
    layer_sums[0].send_on()
    layer_sums[1].send_on()
    gain_begin(2)
    spread_pair(2)
    near_layer[...] = layer_sums[0].total().astype(BF16)
    layer_copy = sender.copy(near_layer, near_layer_came, "z")
    layer_copy.start()
    gain_begin(3)
    near_copies[1].wait_recv()
    out_out[...] += out_near_came[1].astype(F32)
    near_copies[3].wait_recv()
    own_near = qkv_near_came[1].astype(F32)
    query_out[...] += own_near[:, :heads_width]
    key_out[...] += own_near[:, heads_width : heads_width + key_width]
    value_out[...] += own_near[:, heads_width + key_width :]
    gain_begin(4)
    spread_pair(3)
    layer_total = layer_sums[1].total()
    layer_copy.wait_recv()
    layer_ref[...] = (
        residual_ref[...] + (layer_total + near_layer_came[...].astype(F32))
    ).astype(BF16)
    for turn, copy in enumerate(pair_copies):
        copy.wait_recv()
        columns = quarter_units(QUARTERS[turn])
        gate_out[:, columns] = pair_blocks_came[turn, :, :units]
        up_out[:, columns] = pair_blocks_came[turn, :, units:]
    out_far_copy.wait_recv()
    out_out[...] += out_far_came[...].astype(F32)
    qkv_far_copy.wait_recv()
    own_far = qkv_far_came[...].astype(F32)
    query_out[...] += own_far[:, :heads_width]
    key_out[...] += own_far[:, heads_width : heads_width + key_width]
    value_out[...] += own_far[:, heads_width + key_width :]
    gain_begin(5)
    attn_gain_out[...] = sums[5, :, :width]
    ffn_gain_out[...] = sums[5, :, width : 2 * width]
    head_gain_out[...] = sums[5, :, 2 * width :]
    for copy in (
        bulk
        + row_copies
        + low_peers
        + attn_peers
        + list(low_gather)
        + list(attn_gather)
        + peer_copies
        + near_copies
        + pair_copies
        + [mixed_copy, out_far_copy, qkv_far_copy, layer_copy]
    ):
        copy.wait_send()


IN_VMEM = pl.BlockSpec(memory_space=pltpu.VMEM)
ANYWHERE = pl.BlockSpec(memory_space=pl.ANY)
MIB = 1 << 20


def shape_of(shape, dtype):
    return jax.ShapeDtypeStruct(shape, dtype)


def call(kernel, number, ins, outs, out_specs, scratch, limit, operands, flops, moved):
    return pl.pallas_call(
        kernel,
        out_shape=outs,
        in_specs=ins,
        out_specs=out_specs,
        scratch_shapes=scratch,
        cost_estimate=pl.CostEstimate(
            flops=flops, bytes_accessed=moved, transcendentals=0
        ),
        compiler_params=pltpu.CompilerParams(
            collective_id=number, has_side_effects=True, vmem_limit_bytes=limit
        ),
    )(*operands)


def copies(count):
    return [pltpu.SemaphoreType.DMA((count,)), pltpu.SemaphoreType.DMA((count,))]


def forward_step(
    doc_lengths,
    layer_input,
    gains,
    out_grad,
    weights,
):
    tokens, width = layer_input.shape
    heads_width, key_width = weights[0].shape[1], weights[1].shape[1]
    units = weights[4].shape[1] // 4
    length, everyone = 4 * tokens, 16 * tokens
    exponents = -np.arange(0, HEAD_WIDTH, 2, dtype=np.float32) / HEAD_WIDTH
    frequency = np.tile((ROPE_BASE**exponents).astype(np.float32), 128 * 2 // HEAD_WIDTH)
    gain_attn, gain_ffn, gain_query, gain_key = gains
    v = pltpu.VMEM
    return call(
        forward_kernel,
        1,
        [pl.BlockSpec(memory_space=pltpu.SMEM)] + [IN_VMEM] * 6 + [ANYWHERE] * 8,
        [
            shape_of((length, width), BF16),
            shape_of((length, heads_width), BF16),
            shape_of((length, heads_width), BF16),
            shape_of((length, key_width), BF16),
            shape_of((length, key_width), BF16),
            shape_of((length, heads_width), F32),
            shape_of((length, key_width), F32),
            shape_of((length, 128), F32),
            shape_of((length, 128), F32),
            shape_of((length, 128), F32),
            shape_of((tokens, width), F32),
            shape_of((everyone, width), BF16),
            shape_of((everyone, width), BF16),
            shape_of((everyone, units), BF16),
            shape_of((everyone, 2 * units), BF16),
            shape_of((everyone, units), BF16),
        ],
        [ANYWHERE] + [IN_VMEM] * 10 + [ANYWHERE] * 5,
        [
            v((tokens, width), BF16),
            v((everyone, units), BF16),
            v((everyone, 2 * units), BF16),
            v((length, width), BF16),
            v((width, heads_width + 2 * key_width), BF16),
            v((heads_width, width), BF16),
            v((length, length), F32),
            v((length, width), BF16),
            v((2, tokens, width), BF16),
            v((tokens, width), BF16),
            v((tokens, width), BF16),
            v((everyone, width), BF16),
            v((everyone, width), BF16),
            v((width, units), BF16),
            v((width, units), BF16),
            v((units, width), BF16),
        ]
        + copies(64)
        + [pltpu.SemaphoreType.DMA((80,))],
        61 * MIB,
        (
            doc_lengths,
            layer_input,
            gain_attn[None, :],
            gain_ffn[None, :],
            gain_query[None, :],
            gain_key[None, :],
            frequency[None, :],
            out_grad,
        )
        + weights,
        8 * everyone * width * units,
        200 * 10**6,
    )


def back_step(pair, w_gate, w_up, residual, gain_ffn, out_grad, hidden, ffn_all, grad_all):
    tokens, width = residual.shape
    units = hidden.shape[1]
    everyone, block = 16 * tokens, width // 8
    v = pltpu.VMEM
    return call(
        back_kernel,
        2,
        [IN_VMEM] * 3 + [ANYWHERE] * 6,
        [
            shape_of((tokens, width), F32),
            shape_of((1, width), F32),
            shape_of((4 * units, block), BF16),
            shape_of((4 * tokens, width), BF16),
            shape_of((4, block, 2 * units), BF16),
        ],
        [IN_VMEM] * 3 + [ANYWHERE] * 2,
        [
            v((width, 2 * units), BF16),
            v((everyone, 2 * units), BF16),
            v((everyone, units), BF16),
            v((4, units, block), BF16),
            v((4, units, block), BF16),
            v((3, units, block), BF16),
            v((4, block, 2 * units), BF16),
            v((everyone, width // 2), BF16),
            v((everyone, width // 2), BF16),
            v((everyone, width // 2), BF16),
            v((everyone, width), BF16),
            v((everyone // 2, width), BF16),
            v((everyone // 4, width), BF16),
            v((everyone // 8, width), BF16),
            v((everyone // 16, width), BF16),
            v((tokens, width), BF16),
        ]
        + copies(32)
        + [pltpu.SemaphoreType.DMA((16,))],
        60 * MIB,
        (
            gain_ffn[None, :],
            residual,
            out_grad,
            pair,
            hidden,
            w_gate,
            w_up,
            ffn_all,
            grad_all,
        ),
        8 * everyone * width * units,
        200 * 10**6,
    )


def finish_step(big, small, tokens, width, units, heads_width, key_width):
    length, everyone, block = 4 * tokens, 16 * tokens, width // 8
    qkv_width = heads_width + 2 * key_width
    gains = 2 * width + 128
    v = pltpu.VMEM
    return call(
        finish_kernel,
        3,
        [ANYWHERE] * len(big)
        + [IN_VMEM] * 9
        + [pl.BlockSpec(memory_space=pltpu.SMEM)]
        + [IN_VMEM] * (len(small) - 10),
        [
            shape_of((tokens, width), BF16),
            shape_of((tokens, width), BF16),
            shape_of((block, heads_width), F32),
            shape_of((block, key_width), F32),
            shape_of((block, key_width), F32),
            shape_of((heads_width, block), F32),
            shape_of((block, 4 * units), BF16),
            shape_of((block, 4 * units), BF16),
            shape_of((1, width), F32),
            shape_of((1, width), F32),
            shape_of((1, 128), F32),
        ],
        [IN_VMEM] * 11,
        [
            v((length, width), BF16),
            v((heads_width, width), BF16),
            v((width, qkv_width), BF16),
            v((length, width), BF16),
            v((everyone, 2 * units), BF16),
            v((everyone, width // 2), BF16),
            v((length, length), F32),
            v((length, heads_width), BF16),
            v((length, heads_width), BF16),
            v((length, qkv_width), BF16),
            v((length, qkv_width), BF16),
            v((length, width // 2), BF16),
            v((length, width // 2), BF16),
            v((2, heads_width, block), BF16),
            v((2, heads_width, block), BF16),
            v((heads_width, block), BF16),
            v((heads_width, block), BF16),
            v((2, block, qkv_width), BF16),
            v((2, block, qkv_width), BF16),
            v((block, qkv_width), BF16),
            v((block, qkv_width), BF16),
            v((heads_width, block), F32),
            v((block, qkv_width), F32),
            v((4, block, 2 * units), BF16),
            v((3, block, 2 * units), BF16),
            v((4, length, units), BF16),
            v((3, 2, tokens, width), BF16),
            v((3, tokens, width), BF16),
            v((3, tokens, width), BF16),
            v((tokens, width), BF16),
            v((tokens, width), BF16),
            v((6, 1, gains), F32),
            v((5, 1, gains), F32),
        ]
        + copies(64)
        + [pltpu.SemaphoreType.DMA((32,))],
        62 * MIB,
        big + small,
        8 * everyone * width * units,
        400 * 10**6,
    )


def per_device_sixteen(
    layer_input,
    doc_lengths,
    w_query,
    w_key,
    w_value,
    w_out,
    w_gate,
    w_up,
    w_down,
    gain_attn,
    gain_ffn,
    gain_query,
    gain_key,
    out_grad,
):
    outs = forward_step(
        doc_lengths,
        layer_input,
        (gain_attn, gain_ffn, gain_query, gain_key),
        out_grad,
        (w_query, w_key, w_value, w_out, w_gate, w_up, w_down),
    )
    attn_in, saved = outs[0], tuple(outs[1:10])
    residual, ffn_all, grad_all, hidden, pair, hidden_rows = outs[10:]
    residual_grad, gain_ffn_part, grad_down, res_low, pair_sent = back_step(
        pair, w_gate, w_up, residual, gain_ffn, out_grad, hidden, ffn_all, grad_all
    )
    heads_width, key_width = w_query.shape[1], w_key.shape[1]
    (
        layer_out,
        input_grad,
        grad_query,
        grad_key,
        grad_value,
        grad_out,
        grad_gate,
        grad_up,
        attn_gain,
        ffn_gain,
        head_gain,
    ) = finish_step(
        (
            res_low,
            w_out,
            w_query,
            w_key,
            w_value,
            w_down,
            attn_in,
            pair,
            ffn_all,
            hidden_rows,
            pair_sent,
        ),
        saved
        + (
            doc_lengths,
            gain_query[None, :],
            gain_key[None, :],
            gain_attn[None, :],
            layer_input,
            residual_grad,
            gain_ffn_part,
            residual,
        ),
        layer_input.shape[0],
        layer_input.shape[1],
        hidden.shape[1],
        heads_width,
        key_width,
    )
    return (
        layer_out,
        input_grad,
        grad_query,
        grad_key,
        grad_value,
        grad_out,
        grad_gate.astype(F32),
        grad_up.astype(F32),
        grad_down.astype(F32),
        attn_gain[0],
        ffn_gain[0],
        head_gain[0, :HEAD_WIDTH],
        head_gain[0, HEAD_WIDTH:],
    )


def solution(mesh):
    in_specs = (
        P(("dp", "tensor"), None),
        P("dp", None),
        P(None, "tensor"),
        P(None, "tensor"),
        P(None, "tensor"),
        P("tensor", None),
        P(None, "tensor"),
        P(None, "tensor"),
        P("tensor", None),
        P(),
        P(),
        P(),
        P(),
        P(("dp", "tensor"), None),
    )
    out_specs = (
        P(("dp", "tensor"), None),
        P(("dp", "tensor"), None),
        P("dp", "tensor"),
        P("dp", "tensor"),
        P("dp", "tensor"),
        P("tensor", "dp"),
        P("dp", "tensor"),
        P("dp", "tensor"),
        P("tensor", "dp"),
        P(),
        P(),
        P(),
        P(),
    )
    sixteen = mesh.shape["dp"] == 8 and mesh.shape["tensor"] == 4
    return jax.shard_map(
        per_device_sixteen if sixteen else per_device, mesh=mesh, in_specs=in_specs, out_specs=out_specs, check_vma=False
    )
```

```python
import jax
import jax.numpy as jnp
import numpy as np
from jax import lax
from jax.experimental import pallas as pl
from jax.experimental.pallas import tpu as pltpu
from jax.sharding import PartitionSpec as P

HEADS = 32
KV = 8


EPSILON = 1e-06
ROPE_BASE = 10000.0
MASKED = -1e30


def norm_gain(row_block, gain_vec):
    factor = lax.rsqrt(jnp.mean(row_block * row_block, axis=-1, keepdims=True) + EPSILON)
    return row_block * factor * gain_vec


def rotate(vector, cosine, sine_table):
    half_width = vector.shape[-1] // 2
    first = vector[..., :half_width]
    second = vector[..., half_width:]
    return jnp.concatenate(
        [first * cosine - second * sine_table, second * cosine + first * sine_table], axis=-1
    )


def head_prep(raw_proj, gain_vec, cosine, sine_table):
    head_width = gain_vec.shape[0]
    per_head = raw_proj.reshape(raw_proj.shape[0], raw_proj.shape[1] // head_width, head_width)
    return rotate(norm_gain(per_head, gain_vec), cosine[:, None, :], sine_table[:, None, :])


def doc_layout(lengths, length):
    doc_ends = jnp.cumsum(lengths)
    places = jnp.arange(length, dtype=jnp.int32)
    passed_end = (places[:, None] >= doc_ends[None, :]).astype(jnp.int32)
    doc_ids = jnp.sum(passed_end, axis=1)
    starts = jnp.sum(passed_end * lengths[None, :], axis=1)
    return (doc_ids, places, places - starts)


def rope_tables(offsets, head_width):
    frequency = ROPE_BASE ** (-jnp.arange(0, head_width, 2, dtype=jnp.float32) / head_width)
    angles = offsets.astype(jnp.float32)[:, None] * frequency[None, :]
    return (jnp.cos(angles), jnp.sin(angles))


def swiglu(gate_proj, up_proj):
    return jax.nn.silu(gate_proj) * up_proj


def matmul_nt(left_mat, right_mat):
    return lax.dot_general(
        left_mat, right_mat, (((1,), (1,)), ((), ())), preferred_element_type=jnp.float32
    )


def matmul_tn(left_mat, right_mat):
    return lax.dot_general(
        left_mat, right_mat, (((0,), (0,)), ((), ())), preferred_element_type=jnp.float32
    )


def per_device(
    layer_input,
    doc_lengths,
    w_query,
    w_key,
    w_value,
    w_out,
    w_gate,
    w_up,
    w_down,
    gain_attn,
    gain_ffn,
    gain_query,
    gain_key,
    out_grad,
):
    tok_rows = layer_input.shape[0]
    head_width = gain_query.shape[0]
    tensor_count = lax.axis_size("tensor")
    length = tok_rows * tensor_count
    per_dev = w_query.shape[1] // head_width
    groups_dev = w_key.shape[1] // head_width
    input_f32 = layer_input.astype(jnp.float32)
    doc_ids, places, offsets = doc_layout(doc_lengths[0], length)
    cosine, sine_table = rope_tables(offsets, head_width)
    attn_in = lax.all_gather(
        norm_gain(input_f32, gain_attn).astype(jnp.bfloat16), "tensor", axis=0, tiled=True
    )
    query_raw = jnp.dot(attn_in, w_query, preferred_element_type=jnp.float32)
    key_raw = jnp.dot(attn_in, w_key, preferred_element_type=jnp.float32).astype(jnp.bfloat16)
    value_raw = jnp.dot(attn_in, w_value, preferred_element_type=jnp.float32).astype(jnp.bfloat16)
    key_f32 = key_raw.astype(jnp.float32)
    queries = head_prep(query_raw, gain_query, cosine, sine_table).astype(jnp.bfloat16)
    key_rot = head_prep(key_f32, gain_key, cosine, sine_table).astype(jnp.bfloat16)
    local_heads = jnp.arange(per_dev, dtype=jnp.int32)
    group_pick = (
        local_heads[:, None] // (HEADS // KV) == jnp.arange(groups_dev, dtype=jnp.int32)[None, :]
    ).astype(jnp.float32)
    pick_low = group_pick.astype(jnp.bfloat16)
    key_heads = jnp.einsum(
        "lgd,hg->lhd", key_rot, pick_low, preferred_element_type=jnp.float32
    ).astype(jnp.bfloat16)
    value_heads = jnp.einsum(
        "lgd,hg->lhd",
        value_raw.reshape(length, groups_dev, head_width),
        pick_low,
        preferred_element_type=jnp.float32,
    ).astype(jnp.bfloat16)
    block_rows = min(512, length)
    block_count = length // block_rows
    score_scale = head_width ** (-0.5)

    def block_scores(block_num):
        row_begin = block_num * block_rows
        query_block = lax.dynamic_slice_in_dim(queries, row_begin, block_rows, 0)
        ids_block = lax.dynamic_slice_in_dim(doc_ids, row_begin, block_rows, 0)
        places_block = lax.dynamic_slice_in_dim(places, row_begin, block_rows, 0)
        scores = (
            jnp.einsum("qhd,khd->hqk", query_block, key_heads, preferred_element_type=jnp.float32)
            * score_scale
        )
        allowed = (ids_block[:, None] == doc_ids[None, :]) & (
            places[None, :] <= places_block[:, None]
        )
        return (query_block, jnp.where(allowed[None], scores, MASKED))

    def forward_block(block_num):
        query_block, scores = block_scores(block_num)
        row_top = jnp.max(scores, axis=-1, keepdims=True)
        exponent = jnp.exp(scores - row_top)
        row_total = jnp.sum(exponent, axis=-1, keepdims=True)
        probabilities = (exponent / row_total).astype(jnp.bfloat16)
        mixed_block = jnp.einsum(
            "hqk,khd->qhd", probabilities, value_heads, preferred_element_type=jnp.float32
        )
        return (mixed_block, row_top + jnp.log(row_total))

    mixed_all, log_totals = lax.map(forward_block, jnp.arange(block_count, dtype=jnp.int32))
    attn_mixed = mixed_all.reshape(length, per_dev * head_width).astype(jnp.bfloat16)
    residual = input_f32 + lax.psum_scatter(
        jnp.dot(attn_mixed, w_out, preferred_element_type=jnp.float32).astype(jnp.bfloat16),
        "tensor",
        scatter_dimension=0,
        tiled=True,
    ).astype(jnp.float32)
    ffn_in = lax.all_gather(
        norm_gain(residual, gain_ffn).astype(jnp.bfloat16), "tensor", axis=0, tiled=True
    )
    gate_proj = jnp.dot(ffn_in, w_gate, preferred_element_type=jnp.float32)
    up_proj = jnp.dot(ffn_in, w_up, preferred_element_type=jnp.float32)
    hidden = swiglu(gate_proj, up_proj).astype(jnp.bfloat16)
    layer_out = (
        residual
        + lax.psum_scatter(
            jnp.dot(hidden, w_down, preferred_element_type=jnp.float32).astype(jnp.bfloat16),
            "tensor",
            scatter_dimension=0,
            tiled=True,
        ).astype(jnp.float32)
    ).astype(jnp.bfloat16)
    grad_rows = lax.all_gather(out_grad, "tensor", axis=0, tiled=True)
    hidden_grad = matmul_nt(grad_rows, w_down)
    grad_down = matmul_tn(hidden, grad_rows)
    unused_value, swiglu_back = jax.vjp(swiglu, gate_proj, up_proj)
    gate_grad, up_grad = swiglu_back(hidden_grad)
    gate_grad = gate_grad.astype(jnp.bfloat16)
    up_grad = up_grad.astype(jnp.bfloat16)
    grad_gate = matmul_tn(ffn_in, gate_grad)
    grad_up = matmul_tn(ffn_in, up_grad)
    ffn_in_grad = lax.psum_scatter(
        (matmul_nt(gate_grad, w_gate) + matmul_nt(up_grad, w_up)).astype(jnp.bfloat16),
        "tensor",
        scatter_dimension=0,
        tiled=True,
    ).astype(jnp.float32)
    unused_norm, ffn_norm_back = jax.vjp(norm_gain, residual, gain_ffn)
    residual_grad, gain_ffn_grad = ffn_norm_back(ffn_in_grad)
    residual_grad = residual_grad + out_grad.astype(jnp.float32)
    res_low = lax.all_gather(residual_grad.astype(jnp.bfloat16), "tensor", axis=0, tiled=True)
    mixed_grad = matmul_nt(res_low, w_out).astype(jnp.bfloat16).reshape(length, per_dev, head_width)
    grad_out = matmul_tn(attn_mixed, res_low)

    def backward_block(running, block_num):
        key_acc, value_acc = running
        query_block, scores = block_scores(block_num)
        probabilities = jnp.exp(scores - log_totals[block_num])
        grad_block = lax.dynamic_slice_in_dim(mixed_grad, block_num * block_rows, block_rows, 0)
        prob_grad = jnp.einsum(
            "qhd,khd->hqk", grad_block, value_heads, preferred_element_type=jnp.float32
        )
        value_acc = value_acc + jnp.einsum(
            "hqk,qhd->khd",
            probabilities.astype(jnp.bfloat16),
            grad_block,
            preferred_element_type=jnp.float32,
        )
        centre = jnp.sum(probabilities * prob_grad, axis=-1, keepdims=True)
        score_grad = (probabilities * (prob_grad - centre)).astype(jnp.bfloat16)
        query_part = (
            jnp.einsum("hqk,khd->qhd", score_grad, key_heads, preferred_element_type=jnp.float32)
            * score_scale
        )
        key_acc = (
            key_acc
            + jnp.einsum(
                "hqk,qhd->khd", score_grad, query_block, preferred_element_type=jnp.float32
            )
            * score_scale
        )
        return ((key_acc, value_acc), query_part)

    zeros_init = jnp.zeros((length, per_dev, head_width), jnp.float32)
    (key_acc, value_acc), query_parts = lax.scan(
        backward_block, (zeros_init, zeros_init), jnp.arange(block_count, dtype=jnp.int32)
    )
    query_rot_grad = query_parts.reshape(length, per_dev, head_width)
    unused_query, query_back = jax.vjp(
        lambda raw_proj, gain_vec: head_prep(raw_proj, gain_vec, cosine, sine_table),
        query_raw,
        gain_query,
    )
    query_raw_grad, gain_query_grad = query_back(query_rot_grad)
    query_low = query_raw_grad.astype(jnp.bfloat16)
    key_group_grad = jnp.einsum("lhd,hg->lgd", key_acc, group_pick, precision=lax.Precision.HIGHEST)
    value_group_grad = jnp.einsum(
        "lhd,hg->lgd", value_acc, group_pick, precision=lax.Precision.HIGHEST
    )
    unused_key, key_back = jax.vjp(
        lambda raw_proj, gain_vec: head_prep(raw_proj, gain_vec, cosine, sine_table),
        key_f32,
        gain_key,
    )
    key_raw_grad, gain_key_grad = key_back(key_group_grad)
    key_low = key_raw_grad.astype(jnp.bfloat16)
    value_low = value_group_grad.reshape(length, groups_dev * head_width).astype(jnp.bfloat16)
    grad_query = matmul_tn(attn_in, query_low)
    grad_key = matmul_tn(attn_in, key_low)
    grad_value = matmul_tn(attn_in, value_low)
    attn_in_grad = lax.psum_scatter(
        (
            matmul_nt(query_low, w_query)
            + matmul_nt(key_low, w_key)
            + matmul_nt(value_low, w_value)
        ).astype(jnp.bfloat16),
        "tensor",
        scatter_dimension=0,
        tiled=True,
    ).astype(jnp.float32)
    unused_attn, attn_norm_back = jax.vjp(norm_gain, input_f32, gain_attn)
    input_part, gain_attn_grad = attn_norm_back(attn_in_grad)
    input_grad = (input_part + residual_grad).astype(jnp.bfloat16)
    reduced = (
        lax.psum_scatter(
            grad_query.astype(jnp.bfloat16), "dp", scatter_dimension=0, tiled=True
        ).astype(jnp.float32),
        lax.psum_scatter(
            grad_key.astype(jnp.bfloat16), "dp", scatter_dimension=0, tiled=True
        ).astype(jnp.float32),
        lax.psum_scatter(
            grad_value.astype(jnp.bfloat16), "dp", scatter_dimension=0, tiled=True
        ).astype(jnp.float32),
        lax.psum_scatter(
            grad_out.astype(jnp.bfloat16), "dp", scatter_dimension=1, tiled=True
        ).astype(jnp.float32),
        lax.psum_scatter(
            grad_gate.astype(jnp.bfloat16), "dp", scatter_dimension=0, tiled=True
        ).astype(jnp.float32),
        lax.psum_scatter(
            grad_up.astype(jnp.bfloat16), "dp", scatter_dimension=0, tiled=True
        ).astype(jnp.float32),
        lax.psum_scatter(
            grad_down.astype(jnp.bfloat16), "dp", scatter_dimension=1, tiled=True
        ).astype(jnp.float32),
    )
    gain_sums = lax.psum(
        (gain_attn_grad, gain_ffn_grad, gain_query_grad, gain_key_grad), ("dp", "tensor")
    )
    return (
        layer_out,
        input_grad,
        reduced[0],
        reduced[1],
        reduced[2],
        reduced[3],
        reduced[4],
        reduced[5],
        reduced[6],
        gain_sums[0],
        gain_sums[1],
        gain_sums[2],
        gain_sums[3],
    )


MESH_ID = pl.DeviceIdType.MESH
ORDERS = (("x", "y", "z"), ("y", "z", "x"), ("z", "x", "y"))
LINKS = ("x", "y", "z", "core")
GRAD_PATHS = (("x", "y", "z"), ("x", "z", "y"), ("y", "z", "x"))
HEAD_WIDTH = 64
QUARTERS = (("y", "z"), ("y",), ("z",), ())
F32 = jnp.float32
BF16 = jnp.bfloat16


class Place:
    def __init__(self):
        row, column = lax.axis_index("dp"), lax.axis_index("tensor")
        self.far = row // 4
        self.at = {
            "z": (row // 2) % 2,
            "y": row % 2,
            "x": column // 2,
            "core": column % 2,
        }

    def flipped(self, names):
        return {
            name: 1 - value if name in names else value for name, value in self.at.items()
        }

    def device(self, names):
        names = (names,) if isinstance(names, str) else names
        at = self.flipped(names)
        far = 1 - self.far if "far" in names else self.far
        return {
            "dp": far * 4 + at["z"] * 2 + at["y"],
            "tensor": at["x"] * 2 + at["core"],
        }

    def column(self, names=()):
        at = self.flipped(names)
        return at["x"] * 2 + at["core"]

    def quarter(self, names=()):
        at = self.flipped(names)
        return at["z"] * 2 + at["y"]


def enter(place, names):
    barrier = pltpu.get_barrier_semaphore()
    for name in names:
        pl.semaphore_signal(
            barrier, inc=1, device_id=place.device(name), device_id_type=MESH_ID
        )
    pl.semaphore_wait(barrier, len(names))


class Sender:
    def __init__(self, place, send_sems, recv_sems):
        self.place, self.send_sems, self.recv_sems, self.used = place, send_sems, recv_sems, 0

    def copy(self, source, target, name):
        slot = self.used
        self.used += 1
        return pltpu.make_async_remote_copy(
            src_ref=source,
            dst_ref=target,
            send_sem=self.send_sems.at[slot],
            recv_sem=self.recv_sems.at[slot],
            device_id=self.place.device(name),
            device_id_type=MESH_ID,
        )


def part_rows(tokens):
    unit = tokens // 16
    first = -(-unit // 3)
    second = -(-(unit - first) // 2)
    return ((unit - first - second) * 16, first * 16, second * 16)


def part_starts(tokens):
    rows = part_rows(tokens)
    return (0, rows[0], rows[0] + rows[1])


def spot(tokens, part, half, core, index):
    rows, start = part_rows(tokens)[part], part_starts(tokens)[part]
    return half * 8 * tokens + 8 * start + core * 4 * rows + index * rows


def gather4(tokens, buffer, own, sender, place):
    mine = pl.ds(pl.multiple_of(place.column() * tokens, tokens), tokens)
    theirs = pl.ds(pl.multiple_of(place.column(("x",)) * tokens, tokens), tokens)
    return (
        sender.copy(own, buffer.at[mine], "x"),
        sender.copy(own, buffer.at[mine], "core"),
        sender.copy(buffer.at[theirs], buffer.at[theirs], "core"),
    )


def normed(values, gain):
    factor = lax.rsqrt(jnp.mean(values * values, axis=-1, keepdims=True) + EPSILON)
    return values * factor * gain


def norm_back(values, gain, grad):
    factor = lax.rsqrt(jnp.mean(values * values, axis=-1, keepdims=True) + EPSILON)
    unit = values * factor
    scaled = gain * grad
    back = factor * (scaled - unit * jnp.mean(scaled * unit, axis=-1, keepdims=True))
    return back, jnp.sum(grad * unit, axis=0, keepdims=True)


def scatter4(partial, from_core, from_x, tokens, sender, place):
    copies = []
    for names in (("x", "core"), ("core",)):
        shard = pl.ds(pl.multiple_of(place.column(names) * tokens, tokens), tokens)
        copies.append(
            sender.copy(partial.at[shard], from_core.at[len(copies)], "core")
        )
    return copies


def sum4(partial, from_core, outgoing, from_x, tokens, sender, place):
    copies = scatter4(partial, from_core, from_x, tokens, sender, place)
    for copy in copies:
        copy.start()
    far = pl.ds(pl.multiple_of(place.column(("x",)) * tokens, tokens), tokens)
    mine = pl.ds(pl.multiple_of(place.column() * tokens, tokens), tokens)
    copies[0].wait_recv()
    outgoing[...] = (partial[far, :].astype(F32) + from_core[0].astype(F32)).astype(BF16)
    along = sender.copy(outgoing, from_x, "x")
    along.start()
    copies[1].wait_recv()
    near = partial[mine, :].astype(F32) + from_core[1].astype(F32)
    along.wait_recv()
    total = near + from_x[...].astype(F32)
    for copy in copies:
        copy.wait_send()
    along.wait_send()
    return total


def silu_parts(gate, up, hidden_grad):
    s = 1.0 / (1.0 + jnp.exp(-gate))
    silu = gate * s
    hidden = silu * up
    gate_grad = hidden_grad * up * s * (1.0 + gate * (1.0 - s))
    return hidden, gate_grad, hidden_grad * silu


def start_where(condition, *copies_of):
    @pl.when(condition)
    def start():
        for copy in copies_of:
            copy.start()


def back_kernel(
    gain_ref,
    residual_ref,
    grad_ref,
    pair_all,
    hidden_all,
    gate_w,
    up_w,
    ffn_all,
    grad_all,
    back_ref,
    gain_back_ref,
    down_out,
    low_all,
    pair_sent_all,
    weights,
    pair,
    hidden,
    down_sent,
    down_came,
    down_blocks_came,
    pair_sent,
    ffn_half,
    grad_half,
    grad_own,
    products,
    from_core,
    third,
    second,
    first,
    own,
    send_sems,
    recv_sems,
    local_sems,
):
    tokens, width = residual_ref.shape
    units = hidden.shape[1]
    place = Place()
    columns = pl.ds(pl.multiple_of(place.quarter() * units, units), units)
    block_width = width // 8
    local_used = [0]

    def load(source, target):
        copy = pltpu.make_async_copy(source, target, local_sems.at[local_used[0]])
        local_used[0] += 1
        copy.start()
        return copy

    def half_lanes(which):
        return pl.ds(pl.multiple_of(which * (width // 2), width // 2), width // 2)

    def columns_of(names):
        start = place.quarter(names) * block_width
        return pl.ds(pl.multiple_of(start, block_width), block_width)

    half = 8 * tokens
    enter(place, LINKS + ("far", ("y", "z")))
    hidden_load = load(hidden_all, hidden)
    other_load = load(grad_all.at[:, half_lanes(1 - place.far)], grad_half)
    weight_loads = [
        load(gate_w.at[:, columns], weights.at[:, pl.ds(0, units)]),
        load(up_w.at[:, columns], weights.at[:, pl.ds(units, units)]),
        load(pair_all.at[pl.ds(half, half)], pair.at[pl.ds(half, half)]),
    ]
    pair_load = load(pair_all.at[pl.ds(0, half)], pair.at[pl.ds(0, half)])
    own_load = load(grad_all.at[:, half_lanes(place.far)], grad_own)
    ffn_load = load(ffn_all.at[:, half_lanes(1 - place.far)], ffn_half)
    sender = Sender(place, send_sems, recv_sems)
    part_list = [
        (part, part_rows(tokens)[part], part_starts(tokens)[part]) for part in range(3)
    ]

    def place_of(part, half_bit, core, index, count):
        return pl.ds(spot(tokens, part, half_bit, core, index), count)

    to_core = [
        [
            sender.copy(
                products.at[place_of(part, half_bit, 1, 0, 4 * rows)],
                from_core.at[pl.ds(half_bit * 4 * tokens + 4 * start, 4 * rows)],
                "core",
            )
            for part, rows, start in part_list
        ]
        for half_bit in range(2)
    ]
    far = [
        sender.copy(
            products.at[place_of(part, 1, 0, 0, 4 * rows)],
            third.at[pl.ds(4 * start, 4 * rows)],
            ORDERS[part][2],
        )
        for part, rows, start in part_list
    ]
    middle = [
        sender.copy(
            products.at[place_of(part, 0, 0, 2, 2 * rows)],
            second.at[pl.ds(2 * start, 2 * rows)],
            ORDERS[part][1],
        )
        for part, rows, start in part_list
    ]
    close = [
        sender.copy(
            products.at[place_of(part, 0, 0, 1, rows)],
            first.at[pl.ds(start, rows)],
            ORDERS[part][0],
        )
        for part, rows, start in part_list
    ]
    bulk = [sender.copy(down_sent.at[turn], down_came.at[turn], "far") for turn in range(4)]
    down_copies = [
        sender.copy(down_came.at[turn], down_blocks_came.at[turn], QUARTERS[turn])
        for turn in range(3)
    ]

    def down_product(turn):
        down_sent[turn] = matmul_tn(
            hidden[...], grad_half[:, columns_of(QUARTERS[turn])]
        ).astype(BF16)
        bulk[turn].start()

    def pair_product(turn):
        pair_sent[turn] = matmul_tn(
            ffn_half[:, columns_of(QUARTERS[turn])], pair[...]
        ).astype(BF16)

    def quarter_units(names):
        return pl.ds(pl.multiple_of(place.quarter(names) * units, units), units)

    def spread_down(turn):
        names = QUARTERS[turn]
        bulk[turn].wait_recv()
        total = matmul_tn(hidden[...], grad_own[:, columns_of(names)]) + down_came[
            turn
        ].astype(F32)
        if names:
            down_came[turn] = total.astype(BF16)
            down_copies[turn].start()
        else:
            down_out[quarter_units(()), :] = total.astype(BF16)

    def compute(part, half_bit):
        rows = part_rows(tokens)[part]
        span = place_of(part, half_bit, 0, 0, 8 * rows)
        products[span, :] = matmul_nt(pair[span, :], weights[...]).astype(BF16)
        to_core[half_bit][part].start()

    def add_in(rows, arrived):
        products[rows, :] = (
            products[rows, :].astype(F32) + arrived.astype(F32)
        ).astype(BF16)

    def add_core(part, half_bit):
        rows, start = part_rows(tokens)[part], part_starts(tokens)[part]
        to_core[half_bit][part].wait_recv()
        add_in(
            place_of(part, half_bit, 0, 0, 4 * rows),
            from_core[pl.ds(half_bit * 4 * tokens + 4 * start, 4 * rows), :],
        )

    hidden_load.wait()
    other_load.wait()
    down_product(0)
    for copy in weight_loads:
        copy.wait()
    compute(0, 1)
    compute(1, 1)
    add_core(0, 1)
    far[0].start()
    compute(2, 1)
    add_core(1, 1)
    far[1].start()
    pair_load.wait()
    compute(0, 0)
    add_core(2, 1)
    far[2].start()
    down_product(1)
    compute(1, 0)
    compute(2, 0)
    for part in range(3):
        add_core(part, 0)
    ffn_load.wait()
    own_load.wait()
    pair_product(0)
    pair_product(1)
    pair_product(2)
    order = (0, 1, 2)
    for part in order:
        rows, start = part_rows(tokens)[part], part_starts(tokens)[part]
        far[part].wait_recv()
        add_in(
            place_of(part, 0, 0, 2, 2 * rows),
            third[pl.ds(4 * start + 2 * rows, 2 * rows), :],
        )
        middle[part].start()
        add_in(place_of(part, 0, 0, 0, 2 * rows), third[pl.ds(4 * start, 2 * rows), :])
    down_product(2)
    spread_down(0)
    pair_product(3)
    pair_stores = [load(pair_sent.at[turn], pair_sent_all.at[turn]) for turn in range(4)]
    for part in order:
        rows, start = part_rows(tokens)[part], part_starts(tokens)[part]
        middle[part].wait_recv()
        add_in(place_of(part, 0, 0, 1, rows), second[pl.ds(2 * start + rows, rows), :])
        close[part].start()
        add_in(place_of(part, 0, 0, 0, rows), second[pl.ds(2 * start, rows), :])
    down_product(3)
    spread_down(1)
    gain_total = jnp.zeros(gain_ref.shape, F32)
    mine = pl.multiple_of(place.column() * tokens, tokens)
    theirs = pl.multiple_of(place.column(("x",)) * tokens, tokens)
    row_copies = []
    own_stores = []
    for part in order:
        rows, start = part_rows(tokens)[part], part_starts(tokens)[part]
        close[part].wait_recv()
        span = pl.ds(start, rows)
        ffn_in_grad = products[place_of(part, 0, 0, 0, rows), :].astype(F32) + first[
            span, :
        ].astype(F32)
        back, gain_part = norm_back(residual_ref[span, :], gain_ref[...], ffn_in_grad)
        back = back + grad_ref[span, :].astype(F32)
        back_ref[span, :] = back
        own[span, :] = back.astype(BF16)
        gain_total = gain_total + gain_part
        target = low_all.at[pl.ds(mine + start, rows)]
        other = low_all.at[pl.ds(theirs + start, rows)]
        row_copies.append(
            (
                sender.copy(own.at[span], target, "x"),
                sender.copy(own.at[span], target, "core"),
                sender.copy(other, other, "core"),
            )
        )
        row_copies[-1][0].start()
        row_copies[-1][1].start()
        own_stores.append(load(own.at[span], target))
    gain_back_ref[...] = gain_total
    spread_down(2)
    for copies_of in row_copies:
        copies_of[0].wait_recv()
        copies_of[2].start()
    spread_down(3)
    for turn, copy in enumerate(down_copies):
        copy.wait_recv()
        down_out[quarter_units(QUARTERS[turn]), :] = down_blocks_came[turn]
    for copies_of in row_copies:
        copies_of[1].wait_recv()
        copies_of[2].wait_recv()
    for copy in own_stores + pair_stores:
        copy.wait()
    for copies_of in row_copies:
        for copy in copies_of:
            copy.wait_send()
    for copy in to_core[0] + to_core[1] + far + middle + close + bulk + down_copies:
        copy.wait_send()


def swap_halves(values, head_width):
    width = values.shape[1]
    half = head_width // 2
    lane = lax.broadcasted_iota(jnp.int32, values.shape, 1)
    return jnp.where(
        lane % head_width < half,
        pltpu.roll(values, width - half, 1),
        pltpu.roll(values, half, 1),
    )


def head_means(values, head_width):
    width = values.shape[1]
    rows = lax.broadcasted_iota(jnp.int32, (width, width), 0) // head_width
    columns = lax.broadcasted_iota(jnp.int32, (width, width), 1) // head_width
    blocks = jnp.where(rows == columns, 1.0 / head_width, 0.0).astype(BF16)
    upper = values.astype(BF16)
    lower = (values - upper.astype(F32)).astype(BF16)
    return jnp.dot(upper, blocks, preferred_element_type=F32) + jnp.dot(
        lower, blocks, preferred_element_type=F32
    )


def widen(table, width):
    return jnp.concatenate([table] * (width // table.shape[1]), axis=1)


def head_back(grad, raw, gain, cosine, sine, head_width):
    width = grad.shape[1]
    back = grad * widen(cosine, width) - swap_halves(grad, head_width) * widen(sine, width)
    factor = lax.rsqrt(head_means(raw * raw, head_width) + EPSILON)
    unit = raw * factor
    scaled = gain * back
    result = factor * (scaled - unit * head_means(scaled * unit, head_width))
    return result, jnp.sum(back * unit, axis=0, keepdims=True)


def fold_heads(row, head_width):
    total = row[:, :128]
    for start in range(128, row.shape[1], 128):
        total = total + row[:, start : start + 128]
    return total + pltpu.roll(total, head_width, 1)


def runs16(order, path, step):
    place_of = {
        name: position for position, name in enumerate(order)
    }
    known = [set(chosen) for chosen in subsets(path[:step])]
    moves = []
    for flips in known:
        spots = []
        for names in (flips, flips | {path[step]}):
            bits = [int(name in names) for name in order]
            spots.append((bits[2], bits[0] + 2 * bits[1]))
        moves.append(spots)
    moves.sort()
    runs = []
    for (half, index), (to_half, to_index) in moves:
        if runs:
            last = runs[-1]
            if (
                last[0] == half
                and last[2] == to_half
                and last[1] + last[4] == index
                and last[3] + last[4] == to_index
            ):
                last[4] += 1
                continue
        runs.append([half, index, to_half, to_index, 1])
    return runs


def subsets(names):
    result = [()]
    for name in names:
        result = result + [chosen + (name,) for chosen in result]
    return result


def gather16(tokens, buffer, own, sender, paths):
    links, cores = [], []
    for part, order in enumerate(ORDERS):
        rows, start = part_rows(tokens)[part], part_starts(tokens)[part]

        def region(half, index, count, core=0):
            return buffer.at[pl.ds(spot(tokens, part, half, core, index), count * rows)]

        mine = region(0, 0, 1) if own is None else own.at[pl.ds(start, rows)]
        part_links = []
        part_cores = [[sender.copy(mine, region(0, 0, 1, 1), "core")]]
        for step in range(3):
            step_links, step_cores = [], []
            for half, index, to_half, to_index, count in runs16(order, paths[part], step):
                source = mine if step == 0 else region(half, index, count)
                step_links.append(
                    sender.copy(source, region(to_half, to_index, count), paths[part][step])
                )
                step_cores.append(
                    sender.copy(
                        region(to_half, to_index, count),
                        region(to_half, to_index, count, 1),
                        "core",
                    )
                )
            part_links.append(step_links)
            part_cores.append(step_cores)
        links.append(part_links)
        cores.append(part_cores)
    return links, cores


def gather_begin(links, cores):
    for part in range(3):
        for copy in links[part][0] + cores[part][0]:
            copy.start()


def gather_go(links, cores, step, parts=(0, 1, 2)):
    for part in parts:
        for copy in links[part][step]:
            copy.wait_recv()
        if step < 2:
            for copy in links[part][step + 1]:
                copy.start()
        for copy in cores[part][step + 1]:
            copy.start()


def gather_sent(links, cores):
    for part in range(3):
        for copies in links[part] + cores[part]:
            for copy in copies:
                copy.wait_send()


def document_tables(lengths_ref, frequency, length):
    down = lax.broadcasted_iota(jnp.int32, (length, 128), 0)
    across_lanes = lax.broadcasted_iota(jnp.int32, (8, length), 1)
    ids_down = jnp.zeros((length, 128), jnp.int32)
    starts = jnp.zeros((length, 128), jnp.int32)
    ids_across = jnp.zeros((8, length), jnp.int32)
    end = jnp.int32(0)
    for document in range(lengths_ref.shape[1]):
        count = lengths_ref[0, document]
        end = end + count
        passed = down >= end
        ids_down = ids_down + jnp.where(passed, 1, 0)
        starts = starts + jnp.where(passed, count, 0)
        ids_across = ids_across + jnp.where(across_lanes >= end, 1, 0)
    angles = (down - starts).astype(F32) * frequency
    return ids_down[:, :1], ids_across[:1, :], angles


def document_bias(ids_down, ids_across, length):
    allowed = (ids_down == ids_across) & (
        lax.broadcasted_iota(jnp.int32, (length, length), 1)
        <= lax.broadcasted_iota(jnp.int32, (length, length), 0)
    )
    return jnp.where(allowed, 0.0, MASKED)


def head_forward(raw, gain, cosine, sine, head_width):
    factor = lax.rsqrt(head_means(raw * raw, head_width) + EPSILON)
    values = raw * factor * gain
    width = raw.shape[1]
    return values * widen(cosine, width) + swap_halves(values, head_width) * widen(sine, width)


def forward_kernel(
    lengths_ref,
    input_ref,
    gain_attn,
    gain_ffn,
    gain_query,
    gain_key,
    frequency,
    out_grad,
    query_w,
    key_w,
    value_w,
    out_w,
    gate_w,
    up_w,
    down_w,
    attn_all,
    mixed_ref,
    query_ref,
    key_ref,
    value_ref,
    query_raw,
    key_raw,
    totals_ref,
    cosine_ref,
    sine_ref,
    residual_ref,
    ffn_all,
    grad_all,
    hidden_all,
    pair_all,
    rows_all,
    own,
    hidden_ref,
    pair_ref,
    attn_in,
    qkv_w,
    out_v,
    bias,
    partial,
    from_core,
    outgoing,
    from_x,
    ffn_buf,
    grad_buf,
    gate_v,
    up_v,
    down_v,
    send_sems,
    recv_sems,
    local_sems,
):
    tokens, width = input_ref.shape
    length = 4 * tokens
    units = gate_v.shape[1]
    heads_width, key_width = query_ref.shape[1], key_ref.shape[1]
    place = Place()
    columns = pl.ds(pl.multiple_of(place.quarter() * units, units), units)
    local_used = [0]

    def load(source, target):
        copy = pltpu.make_async_copy(source, target, local_sems.at[local_used[0]])
        local_used[0] += 1
        copy.start()
        return copy

    enter(place, LINKS)
    sender = Sender(place, send_sems, recv_sems)
    own[...] = normed(input_ref[...].astype(F32), gain_attn[...]).astype(BF16)
    row_copies = gather4(tokens, attn_in, own, sender, place)
    row_copies[0].start()
    row_copies[1].start()
    grad_links, grad_cores = gather16(tokens, grad_buf, out_grad, sender, GRAD_PATHS)
    gather_begin(grad_links, grad_cores)
    first_loads = [
        load(query_w, qkv_w.at[:, pl.ds(0, heads_width)]),
        load(key_w, qkv_w.at[:, pl.ds(heads_width, key_width)]),
        load(value_w, qkv_w.at[:, pl.ds(heads_width + key_width, key_width)]),
        load(out_w, out_v),
    ]
    mine = pl.ds(pl.multiple_of(place.column() * tokens, tokens), tokens)
    attn_in[mine, :] = own[...]
    grad_loads = []
    for part in range(3):
        rows, start = part_rows(tokens)[part], part_starts(tokens)[part]
        grad_loads.append(
            load(
                out_grad.at[pl.ds(start, rows)],
                grad_buf.at[pl.ds(spot(tokens, part, 0, 0, 0), rows)],
            )
        )
    later_loads = [
        load(gate_w.at[:, columns], gate_v),
        load(up_w.at[:, columns], up_v),
        load(down_w.at[columns, :], down_v),
    ]
    ids_down, ids_across, angles = document_tables(lengths_ref, frequency[...], length)
    lane = lax.broadcasted_iota(jnp.int32, (length, 128), 1)
    cosine_ref[...] = jnp.cos(angles)
    sine = jnp.sin(angles)
    sine_ref[...] = jnp.where(lane % HEAD_WIDTH < HEAD_WIDTH // 2, -sine, sine)
    bias[...] = document_bias(ids_down, ids_across, length)
    for copy in first_loads + grad_loads:
        copy.wait()
    gather_go(grad_links, grad_cores, 0, (2,))
    row_copies[0].wait_recv()
    row_copies[2].start()
    row_copies[1].wait_recv()
    row_copies[2].wait_recv()
    attn_store = load(attn_in, attn_all)
    gather_go(grad_links, grad_cores, 1, (2,))

    raw = jnp.dot(attn_in[...], qkv_w[...], preferred_element_type=F32)
    query_raw[...] = raw[:, :heads_width]
    key_raw[...] = raw[:, heads_width : heads_width + key_width].astype(BF16).astype(F32)
    value_ref[...] = raw[:, heads_width + key_width :].astype(BF16)
    query_ref[...] = head_forward(
        query_raw[...], widen(gain_query[...], heads_width), cosine_ref[...], sine_ref[...], HEAD_WIDTH
    ).astype(BF16)
    key_ref[...] = head_forward(
        key_raw[...], widen(gain_key[...], key_width), cosine_ref[...], sine_ref[...], HEAD_WIDTH
    ).astype(BF16)
    gather_go(grad_links, grad_cores, 0, (0, 1))
    scale = HEAD_WIDTH ** (-0.5)
    group_heads = HEADS // KV
    mixed_parts = []
    head_total = heads_width // HEAD_WIDTH
    for head in range(head_total):
        group = head // group_heads
        group_lanes = slice(group * HEAD_WIDTH, (group + 1) * HEAD_WIDTH)
        scores = (
            matmul_nt(
                query_ref[:, head * HEAD_WIDTH : (head + 1) * HEAD_WIDTH],
                key_ref[:, group_lanes],
            )
            * scale
            + bias[...]
        )
        top = jnp.max(scores, axis=-1, keepdims=True)
        exponent = jnp.exp(scores - top)
        total = jnp.sum(exponent, axis=-1, keepdims=True)
        probs = (exponent * (1.0 / total)).astype(BF16)
        mixed_parts.append(
            jnp.dot(probs, value_ref[:, group_lanes], preferred_element_type=F32)
        )
        totals_ref[:, head : head + 1] = top + jnp.log(total)
        if head % 2 == 1:
            mixed_ref[:, (head - 1) * HEAD_WIDTH : (head + 1) * HEAD_WIDTH] = (
                jnp.concatenate(mixed_parts, axis=1).astype(BF16)
            )
            mixed_parts = []
        if head == head_total - 2:
            gather_go(grad_links, grad_cores, 1, (0, 1))
    partial[...] = jnp.dot(mixed_ref[...], out_v[...], preferred_element_type=F32).astype(BF16)

    residual = input_ref[...].astype(F32) + sum4(
        partial, from_core, outgoing, from_x, tokens, sender, place
    )
    residual_ref[...] = residual
    for copy in row_copies:
        copy.wait_send()
    own[...] = normed(residual, gain_ffn[...]).astype(BF16)
    for part in range(3):
        rows, start = part_rows(tokens)[part], part_starts(tokens)[part]
        ffn_buf[pl.ds(spot(tokens, part, 0, 0, 0), rows), :] = own[pl.ds(start, rows), :]
    links, cores = gather16(tokens, ffn_buf, None, sender, ORDERS)
    gather_begin(links, cores)
    gather_go(grad_links, grad_cores, 2)
    gather_go(links, cores, 0)
    for copy in later_loads:
        copy.wait()
    for part in range(3):
        for step_copies in grad_cores[part]:
            for copy in step_copies:
                copy.wait_recv()
    grad_store = load(grad_buf, grad_all)
    gather_go(links, cores, 1)
    for part in range(3):
        for step_copies in cores[part][:3]:
            for copy in step_copies:
                copy.wait_recv()

    block = 2 * tokens

    def compute(index):
        rows = pl.ds(pl.multiple_of(index * block, block), block)
        values = ffn_buf[rows, :]
        gate = jnp.dot(values, gate_v[...], preferred_element_type=F32)
        up = jnp.dot(values, up_v[...], preferred_element_type=F32)
        hidden_grad = matmul_nt(grad_buf[rows, :], down_v[...])
        hidden, gate_grad, up_grad = silu_parts(gate, up, hidden_grad)
        hidden_ref[rows, :] = hidden.astype(BF16)
        pair_ref[rows, :units] = gate_grad.astype(BF16)
        pair_ref[rows, units:] = up_grad.astype(BF16)

    half = 8 * tokens
    stores = [attn_store, grad_store]

    def store_half(which):
        rows = pl.ds(which * half, half)
        stores.append(load(hidden_ref.at[rows], hidden_all.at[rows]))
        stores.append(load(pair_ref.at[rows], pair_all.at[rows]))
        for part, order in enumerate(ORDERS):
            count, start = part_rows(tokens)[part], part_starts(tokens)[part]
            for core in range(2):
                for index in range(4):
                    bits = (index % 2, index // 2, which)
                    flips = tuple(name for name, bit in zip(order, bits) if bit)
                    row = ("z" in flips) * 2 + ("y" in flips)
                    names = tuple(n for n in flips if n == "x") + (("core",) if core else ())
                    target = row * 4 * tokens + place.column(names) * tokens + start
                    stores.append(
                        load(
                            hidden_ref.at[
                                pl.ds(spot(tokens, part, which, core, index), count)
                            ],
                            rows_all.at[pl.ds(pl.multiple_of(target, 16), count)],
                        )
                    )

    stores.append(load(ffn_buf.at[pl.ds(0, half)], ffn_all.at[pl.ds(0, half)]))
    pl.loop(0, 4)(compute)
    gather_go(links, cores, 2)
    store_half(0)
    for part in range(3):
        for copy in cores[part][3]:
            copy.wait_recv()
    stores.append(load(ffn_buf.at[pl.ds(half, half)], ffn_all.at[pl.ds(half, half)]))
    pl.loop(4, 8)(compute)
    store_half(1)
    for copy in stores:
        copy.wait()
    gather_sent(grad_links, grad_cores)
    gather_sent(links, cores)


GAIN_LINKS = ("core", "x", "y", "z", "far")


class RowSum:
    def __init__(self, partial, from_core, outgoing, from_x, tokens, sender, place):
        self.partial, self.from_core = partial, from_core
        self.outgoing, self.from_x = outgoing, from_x
        self.far = pl.ds(pl.multiple_of(place.column(("x",)) * tokens, tokens), tokens)
        self.mine = pl.ds(pl.multiple_of(place.column() * tokens, tokens), tokens)
        self.copies = scatter4(partial, from_core, from_x, tokens, sender, place)
        self.along = sender.copy(outgoing, from_x, "x")

    def begin(self):
        for copy in self.copies:
            copy.start()

    def send_on(self):
        self.copies[0].wait_recv()
        self.outgoing[...] = (
            self.partial[self.far, :].astype(F32) + self.from_core[0].astype(F32)
        ).astype(BF16)
        self.along.start()

    def total(self):
        self.copies[1].wait_recv()
        near = self.partial[self.mine, :].astype(F32) + self.from_core[1].astype(F32)
        self.along.wait_recv()
        total = near + self.from_x[...].astype(F32)
        for copy in self.copies:
            copy.wait_send()
        self.along.wait_send()
        return total


def finish_kernel(
    low_all,
    out_w,
    query_w,
    key_w,
    value_w,
    down_w,
    attn_all,
    pair_all,
    ffn_all,
    rows_all,
    pair_sent,
    mixed_ref,
    query_ref,
    key_ref,
    value_ref,
    query_raw,
    key_raw,
    totals_ref,
    cosine_ref,
    sine_ref,
    lengths_ref,
    gain_query,
    gain_key,
    gain_attn,
    input_ref,
    back_ref,
    ffn_gain_ref,
    residual_ref,
    layer_ref,
    input_grad_ref,
    query_out,
    key_out,
    value_out,
    out_out,
    gate_out,
    up_out,
    attn_gain_out,
    ffn_gain_out,
    head_gain_out,
    low,
    out_v,
    qkv_w,
    attn_in,
    pair,
    columns_v,
    bias,
    mixed_grad,
    mixed_peer,
    qkv_low,
    qkv_peer,
    attn_peer,
    low_peer,
    out_near,
    out_near_came,
    out_far,
    out_far_came,
    qkv_near,
    qkv_near_came,
    qkv_far,
    qkv_far_came,
    out_part,
    qkv_part,
    pair_blocks,
    pair_blocks_came,
    rows_came,
    from_core,
    outgoing,
    from_x,
    near_layer,
    near_layer_came,
    sums,
    came,
    send_sems,
    recv_sems,
    local_sems,
):
    tokens, width = input_ref.shape
    length = 4 * tokens
    units = pair.shape[1] // 2
    heads_width = query_ref.shape[1]
    key_width = key_ref.shape[1]
    head_width = HEAD_WIDTH
    group_heads = HEADS // KV
    groups = key_width // head_width
    block = width // 8
    place = Place()
    y, z, far = place.at["y"], place.at["z"], place.far
    sender = Sender(place, send_sems, recv_sems)
    local_used = [0]

    def load(source, target):
        copy = pltpu.make_async_copy(source, target, local_sems.at[local_used[0]])
        local_used[0] += 1
        copy.start()
        return copy

    def lanes(start, count):
        return pl.ds(pl.multiple_of(start, count), count)

    def quarter_lanes(names):
        return lanes(place.quarter(names) * block, block)

    def quarter_units(names):
        return lanes(place.quarter(names) * units, units)

    def own_half(source):
        return source.at[:, lanes(far * (width // 2), width // 2)]

    enter(place, GAIN_LINKS + (("y", "z"),))
    mine = lanes(place.column() * tokens, tokens)
    bulk = [sender.copy(pair_sent.at[turn], pair_blocks.at[turn], "far") for turn in range(4)]
    inner, outer = far != z, far == z
    start_where(outer, bulk[0])
    start_where(inner, bulk[0], bulk[1], bulk[2], bulk[3])
    mixed_copy = sender.copy(mixed_ref, mixed_peer, "y")

    def to_peer(source, target):
        return [
            sender.copy(
                source.at[mine, lanes((index * 2 + 1 - y) * block, block)],
                target.at[mine, pl.ds(index * block, block)],
                "y",
            )
            for index in range(4)
        ]

    low_peers = to_peer(low_all, low_peer)
    attn_peers = to_peer(attn_all, attn_peer)
    for copy in low_peers + attn_peers:
        copy.start()
    mixed_copy.start()
    low_load = load(low_all, low)
    out_load = load(out_w, out_v)
    attn_load = load(attn_all, attn_in)
    own_load = load(own_half(ffn_all), columns_v)
    pair_load = load(pair_all, pair)
    qkv_loads = [
        load(query_w, qkv_w.at[:, pl.ds(0, heads_width)]),
        load(key_w, qkv_w.at[:, pl.ds(heads_width, key_width)]),
        load(value_w, qkv_w.at[:, pl.ds(heads_width + key_width, key_width)]),
    ]
    row_loads = [
        load(rows_all.at[pl.ds(0, length)], rows_came.at[0]),
        load(rows_all.at[pl.ds(2 * length, length)], rows_came.at[2]),
    ]
    row_copies = [
        sender.copy(rows_all.at[pl.ds(offset * length, length)], rows_came.at[offset], "y")
        for offset in (1, 3)
    ]

    low_load.wait()
    out_load.wait()
    mixed_grad[...] = matmul_nt(low[...], out_v[...]).astype(BF16)
    ids_down, ids_across, unused_angles = document_tables(
        lengths_ref, jnp.ones((1, 128), F32), length
    )
    bias[...] = document_bias(ids_down, ids_across, length)
    low_gather = gather4(tokens, low_peer, low_peer.at[mine], sender, place)
    attn_gather = gather4(tokens, attn_peer, attn_peer.at[mine], sender, place)

    def peers_arrived():
        for copy in low_peers + attn_peers:
            copy.wait_recv()
        for copies_of in (low_gather, attn_gather):
            copies_of[0].start()
            copies_of[1].start()

    def peers_go_on():
        low_gather[0].wait_recv()
        low_gather[2].start()

    scale = head_width ** (-0.5)
    key_parts, value_parts, query_gain = [], [], [None]
    peer_copies = []

    def attention_group(group, between=None):
        group_lanes = slice(group * head_width, (group + 1) * head_width)
        key, value = key_ref[:, group_lanes], value_ref[:, group_lanes]
        key_grad = jnp.zeros((length, head_width), F32)
        value_grad = jnp.zeros((length, head_width), F32)
        query_parts = []
        for head in range(group * group_heads, (group + 1) * group_heads):
            head_lanes = slice(head * head_width, (head + 1) * head_width)
            query, grad = query_ref[:, head_lanes], mixed_grad[:, head_lanes]
            scores = matmul_nt(query, key) * scale + bias[...]
            probs = jnp.exp(scores - totals_ref[:, head : head + 1])
            prob_grad = matmul_nt(grad, value)
            value_grad = value_grad + matmul_tn(probs.astype(BF16), grad)
            centre = jnp.sum(probs * prob_grad, axis=-1, keepdims=True)
            score_grad = (probs * (prob_grad - centre)).astype(BF16)
            query_parts.append(jnp.dot(score_grad, key, preferred_element_type=F32) * scale)
            key_grad = key_grad + matmul_tn(score_grad, query) * scale
            if between and between[head - group * group_heads]:
                between[head - group * group_heads]()
        key_parts.append(key_grad)
        value_parts.append(value_grad)
        wide = slice(group * group_heads * head_width, (group + 1) * group_heads * head_width)
        query_grad, gain_part = head_back(
            jnp.concatenate(query_parts, axis=1),
            query_raw[:, wide],
            widen(gain_query[...], group_heads * head_width),
            cosine_ref[...],
            sine_ref[...],
            head_width,
        )
        gain_part = fold_heads(gain_part, head_width)
        query_gain[0] = gain_part if query_gain[0] is None else query_gain[0] + gain_part
        qkv_low[:, wide] = query_grad.astype(BF16)
        copy = sender.copy(qkv_low.at[:, wide], qkv_peer.at[:, wide], "y")
        copy.start()
        peer_copies.append(copy)

    attention_group(0, (None, peers_arrived, None, peers_go_on))
    row_copies[0].start()

    attn_gather[0].wait_recv()
    attn_gather[2].start()
    low_gather[1].wait_recv()
    low_gather[2].wait_recv()
    mixed_copy.wait_recv()

    def out_total(index):
        return matmul_tn(
            mixed_ref[...], low[:, lanes((index * 2 + y) * block, block)]
        ) + matmul_tn(mixed_peer[...], low_peer[:, lanes(index * block, block)])

    near_copies = []
    for turn, half in enumerate((1 - far, far)):
        out_near[turn] = out_total(half * 2 + 1 - z).astype(BF16)
        copy = sender.copy(out_near.at[turn], out_near_came.at[turn], "z")
        copy.start()
        near_copies.append(copy)
    start_where(outer, bulk[1])
    out_part[...] = out_total((1 - far) * 2 + z)
    out_out[...] = out_total(far * 2 + z)

    for group in range(1, groups):
        attention_group(group)
    key_back, key_gain = head_back(
        jnp.concatenate(key_parts, axis=1),
        key_raw[...],
        widen(gain_key[...], key_width),
        cosine_ref[...],
        sine_ref[...],
        head_width,
    )
    key_gain = fold_heads(key_gain, head_width)
    qkv_low[:, heads_width : heads_width + key_width] = key_back.astype(BF16)
    qkv_low[:, heads_width + key_width :] = jnp.concatenate(value_parts, axis=1).astype(BF16)
    tail = slice(heads_width, heads_width + 2 * key_width)
    peer_copies.append(sender.copy(qkv_low.at[:, tail], qkv_peer.at[:, tail], "y"))
    peer_copies[-1].start()
    row_copies[1].start()

    partial = out_v
    for copy in qkv_loads:
        copy.wait()

    def part_of(index):
        columns = lanes(index * 512, 512)
        partial[:, columns] = matmul_nt(qkv_low[...], qkv_w[columns, :]).astype(BF16)

    pl.loop(0, width // 512)(part_of)
    attn_sum = RowSum(partial, from_core.at[0], outgoing.at[0], from_x.at[0], tokens, sender, place)
    attn_sum.begin()

    own_load.wait()
    pair_load.wait()
    pair_copies = []

    def spread_pair(turn):
        names = QUARTERS[turn]
        bulk[turn].wait_recv()
        total = matmul_tn(columns_v[:, quarter_lanes(names)], pair[...]) + pair_blocks[
            turn
        ].astype(F32)
        if names:
            pair_blocks[turn] = total.astype(BF16)
            copy = sender.copy(pair_blocks.at[turn], pair_blocks_came.at[turn], names)
            copy.start()
            pair_copies.append(copy)
        else:
            gate_out[:, quarter_units(())] = total[:, :units].astype(BF16)
            up_out[:, quarter_units(())] = total[:, units:].astype(BF16)

    spread_pair(0)
    start_where(outer, bulk[2])
    attn_sum.send_on()

    attn_load.wait()
    for copy in peer_copies + list(attn_gather[1:]):
        copy.wait_recv()

    def qkv_total(index):
        return matmul_tn(
            attn_in[:, lanes((index * 2 + y) * block, block)], qkv_low[...]
        ) + matmul_tn(attn_peer[:, lanes(index * block, block)], qkv_peer[...])

    for turn, half in enumerate((1 - far, far)):
        qkv_near[turn] = qkv_total(half * 2 + 1 - z).astype(BF16)
        copy = sender.copy(qkv_near.at[turn], qkv_near_came.at[turn], "z")
        copy.start()
        near_copies.append(copy)
    near_copies[0].wait_recv()
    out_far[...] = (out_part[...] + out_near_came[0].astype(F32)).astype(BF16)
    out_far_copy = sender.copy(out_far, out_far_came, "far")
    out_far_copy.start()
    start_where(outer, bulk[3])
    qkv_part[...] = qkv_total((1 - far) * 2 + z)
    own_qkv = qkv_total(far * 2 + z)
    query_out[...] = own_qkv[:, :heads_width]
    key_out[...] = own_qkv[:, heads_width : heads_width + key_width]
    value_out[...] = own_qkv[:, heads_width + key_width :]

    attn_grad = attn_sum.total()
    back, attn_gain = norm_back(input_ref[...].astype(F32), gain_attn[...], attn_grad)
    input_grad_ref[...] = (back + back_ref[...]).astype(BF16)
    sums[0, :, :width] = attn_gain
    sums[0, :, width : 2 * width] = ffn_gain_ref[...]
    lane = lax.broadcasted_iota(jnp.int32, (1, 128), 1)
    sums[0, :, 2 * width :] = jnp.where(lane < head_width, query_gain[0], key_gain)
    gain_copies = []

    def gain_begin(step):
        if step:
            gain_copies[-1].wait()
            sums[step] = sums[step - 1] + came[step - 1]
        if step < len(GAIN_LINKS):
            copy = sender.copy(sums.at[step], came.at[step], GAIN_LINKS[step])
            copy.start()
            gain_copies.append(copy)

    gain_begin(0)
    near_copies[2].wait_recv()
    qkv_far[...] = (qkv_part[...] + qkv_near_came[0].astype(F32)).astype(BF16)
    qkv_far_copy = sender.copy(qkv_far, qkv_far_came, "far")
    qkv_far_copy.start()
    spread_pair(1)
    gain_begin(1)

    layer_parts = (low, out_v)
    for copy in row_loads:
        copy.wait()
    for copy in row_copies:
        copy.wait_recv()

    def down_loads(chunk):
        return [
            load(
                down_w.at[quarter_units(names), pl.ds(chunk * 512, 512)],
                qkv_w.at[pl.ds((chunk % 2) * 2 * units + turn * units, units), pl.ds(0, 512)],
            )
            for turn, names in enumerate(((), ("y",)))
        ]

    chunks = width // 512
    pending = down_loads(0)
    for chunk in range(chunks):
        columns = pl.ds(chunk * 512, 512)
        for copy in pending:
            copy.wait()
        if chunk + 1 < chunks:
            pending = down_loads(chunk + 1)
        base = (chunk % 2) * 2 * units
        for target, first in ((layer_parts[0], 2), (layer_parts[1], 0)):
            target[:, columns] = (
                jnp.dot(
                    rows_came[first],
                    qkv_w[pl.ds(base, units), pl.ds(0, 512)],
                    preferred_element_type=F32,
                )
                + jnp.dot(
                    rows_came[first + 1],
                    qkv_w[pl.ds(base + units, units), pl.ds(0, 512)],
                    preferred_element_type=F32,
                )
            ).astype(BF16)
    gain_begin(2)
    layer_sums = [
        RowSum(
            layer_parts[turn],
            from_core.at[turn + 1],
            outgoing.at[turn + 1],
            from_x.at[turn + 1],
            tokens,
            sender,
            place,
        )
        for turn in range(2)
    ]
    layer_sums[0].begin()
    layer_sums[1].begin()
    layer_sums[0].send_on()
    layer_sums[1].send_on()
    spread_pair(2)
    gain_begin(3)
    near_layer[...] = layer_sums[0].total().astype(BF16)
    layer_copy = sender.copy(near_layer, near_layer_came, "z")
    layer_copy.start()
    near_copies[1].wait_recv()
    out_out[...] += out_near_came[1].astype(F32)
    near_copies[3].wait_recv()
    own_near = qkv_near_came[1].astype(F32)
    query_out[...] += own_near[:, :heads_width]
    key_out[...] += own_near[:, heads_width : heads_width + key_width]
    value_out[...] += own_near[:, heads_width + key_width :]
    gain_begin(4)
    spread_pair(3)
    layer_total = layer_sums[1].total()
    layer_copy.wait_recv()
    layer_ref[...] = (
        residual_ref[...] + (layer_total + near_layer_came[...].astype(F32))
    ).astype(BF16)
    for turn, copy in enumerate(pair_copies):
        copy.wait_recv()
        columns = quarter_units(QUARTERS[turn])
        gate_out[:, columns] = pair_blocks_came[turn, :, :units]
        up_out[:, columns] = pair_blocks_came[turn, :, units:]
    out_far_copy.wait_recv()
    out_out[...] += out_far_came[...].astype(F32)
    qkv_far_copy.wait_recv()
    own_far = qkv_far_came[...].astype(F32)
    query_out[...] += own_far[:, :heads_width]
    key_out[...] += own_far[:, heads_width : heads_width + key_width]
    value_out[...] += own_far[:, heads_width + key_width :]
    gain_begin(5)
    attn_gain_out[...] = sums[5, :, :width]
    ffn_gain_out[...] = sums[5, :, width : 2 * width]
    head_gain_out[...] = sums[5, :, 2 * width :]
    for copy in (
        bulk
        + row_copies
        + low_peers
        + attn_peers
        + list(low_gather)
        + list(attn_gather)
        + peer_copies
        + near_copies
        + pair_copies
        + [mixed_copy, out_far_copy, qkv_far_copy, layer_copy]
    ):
        copy.wait_send()


IN_VMEM = pl.BlockSpec(memory_space=pltpu.VMEM)
ANYWHERE = pl.BlockSpec(memory_space=pl.ANY)
MIB = 1 << 20


def shape_of(shape, dtype):
    return jax.ShapeDtypeStruct(shape, dtype)


def call(kernel, number, ins, outs, out_specs, scratch, limit, operands, flops, moved):
    return pl.pallas_call(
        kernel,
        out_shape=outs,
        in_specs=ins,
        out_specs=out_specs,
        scratch_shapes=scratch,
        cost_estimate=pl.CostEstimate(
            flops=flops, bytes_accessed=moved, transcendentals=0
        ),
        compiler_params=pltpu.CompilerParams(
            collective_id=number, has_side_effects=True, vmem_limit_bytes=limit
        ),
    )(*operands)


def copies(count):
    return [pltpu.SemaphoreType.DMA((count,)), pltpu.SemaphoreType.DMA((count,))]


def forward_step(
    doc_lengths,
    layer_input,
    gains,
    out_grad,
    weights,
):
    tokens, width = layer_input.shape
    heads_width, key_width = weights[0].shape[1], weights[1].shape[1]
    units = weights[4].shape[1] // 4
    length, everyone = 4 * tokens, 16 * tokens
    exponents = -np.arange(0, HEAD_WIDTH, 2, dtype=np.float32) / HEAD_WIDTH
    frequency = np.tile((ROPE_BASE**exponents).astype(np.float32), 128 * 2 // HEAD_WIDTH)
    gain_attn, gain_ffn, gain_query, gain_key = gains
    v = pltpu.VMEM
    return call(
        forward_kernel,
        1,
        [pl.BlockSpec(memory_space=pltpu.SMEM)] + [IN_VMEM] * 6 + [ANYWHERE] * 8,
        [
            shape_of((length, width), BF16),
            shape_of((length, heads_width), BF16),
            shape_of((length, heads_width), BF16),
            shape_of((length, key_width), BF16),
            shape_of((length, key_width), BF16),
            shape_of((length, heads_width), F32),
            shape_of((length, key_width), F32),
            shape_of((length, 128), F32),
            shape_of((length, 128), F32),
            shape_of((length, 128), F32),
            shape_of((tokens, width), F32),
            shape_of((everyone, width), BF16),
            shape_of((everyone, width), BF16),
            shape_of((everyone, units), BF16),
            shape_of((everyone, 2 * units), BF16),
            shape_of((everyone, units), BF16),
        ],
        [ANYWHERE] + [IN_VMEM] * 10 + [ANYWHERE] * 5,
        [
            v((tokens, width), BF16),
            v((everyone, units), BF16),
            v((everyone, 2 * units), BF16),
            v((length, width), BF16),
            v((width, heads_width + 2 * key_width), BF16),
            v((heads_width, width), BF16),
            v((length, length), F32),
            v((length, width), BF16),
            v((2, tokens, width), BF16),
            v((tokens, width), BF16),
            v((tokens, width), BF16),
            v((everyone, width), BF16),
            v((everyone, width), BF16),
            v((width, units), BF16),
            v((width, units), BF16),
            v((units, width), BF16),
        ]
        + copies(64)
        + [pltpu.SemaphoreType.DMA((80,))],
        61 * MIB,
        (
            doc_lengths,
            layer_input,
            gain_attn[None, :],
            gain_ffn[None, :],
            gain_query[None, :],
            gain_key[None, :],
            frequency[None, :],
            out_grad,
        )
        + weights,
        8 * everyone * width * units,
        200 * 10**6,
    )


def back_step(pair, w_gate, w_up, residual, gain_ffn, out_grad, hidden, ffn_all, grad_all):
    tokens, width = residual.shape
    units = hidden.shape[1]
    everyone, block = 16 * tokens, width // 8
    v = pltpu.VMEM
    return call(
        back_kernel,
        2,
        [IN_VMEM] * 3 + [ANYWHERE] * 6,
        [
            shape_of((tokens, width), F32),
            shape_of((1, width), F32),
            shape_of((4 * units, block), BF16),
            shape_of((4 * tokens, width), BF16),
            shape_of((4, block, 2 * units), BF16),
        ],
        [IN_VMEM] * 3 + [ANYWHERE] * 2,
        [
            v((width, 2 * units), BF16),
            v((everyone, 2 * units), BF16),
            v((everyone, units), BF16),
            v((4, units, block), BF16),
            v((4, units, block), BF16),
            v((3, units, block), BF16),
            v((4, block, 2 * units), BF16),
            v((everyone, width // 2), BF16),
            v((everyone, width // 2), BF16),
            v((everyone, width // 2), BF16),
            v((everyone, width), BF16),
            v((everyone // 2, width), BF16),
            v((everyone // 4, width), BF16),
            v((everyone // 8, width), BF16),
            v((everyone // 16, width), BF16),
            v((tokens, width), BF16),
        ]
        + copies(32)
        + [pltpu.SemaphoreType.DMA((16,))],
        60 * MIB,
        (
            gain_ffn[None, :],
            residual,
            out_grad,
            pair,
            hidden,
            w_gate,
            w_up,
            ffn_all,
            grad_all,
        ),
        8 * everyone * width * units,
        200 * 10**6,
    )


def finish_step(big, small, tokens, width, units, heads_width, key_width):
    length, everyone, block = 4 * tokens, 16 * tokens, width // 8
    qkv_width = heads_width + 2 * key_width
    gains = 2 * width + 128
    v = pltpu.VMEM
    return call(
        finish_kernel,
        3,
        [ANYWHERE] * len(big)
        + [IN_VMEM] * 9
        + [pl.BlockSpec(memory_space=pltpu.SMEM)]
        + [IN_VMEM] * (len(small) - 10),
        [
            shape_of((tokens, width), BF16),
            shape_of((tokens, width), BF16),
            shape_of((block, heads_width), F32),
            shape_of((block, key_width), F32),
            shape_of((block, key_width), F32),
            shape_of((heads_width, block), F32),
            shape_of((block, 4 * units), BF16),
            shape_of((block, 4 * units), BF16),
            shape_of((1, width), F32),
            shape_of((1, width), F32),
            shape_of((1, 128), F32),
        ],
        [IN_VMEM] * 11,
        [
            v((length, width), BF16),
            v((heads_width, width), BF16),
            v((width, qkv_width), BF16),
            v((length, width), BF16),
            v((everyone, 2 * units), BF16),
            v((everyone, width // 2), BF16),
            v((length, length), F32),
            v((length, heads_width), BF16),
            v((length, heads_width), BF16),
            v((length, qkv_width), BF16),
            v((length, qkv_width), BF16),
            v((length, width // 2), BF16),
            v((length, width // 2), BF16),
            v((2, heads_width, block), BF16),
            v((2, heads_width, block), BF16),
            v((heads_width, block), BF16),
            v((heads_width, block), BF16),
            v((2, block, qkv_width), BF16),
            v((2, block, qkv_width), BF16),
            v((block, qkv_width), BF16),
            v((block, qkv_width), BF16),
            v((heads_width, block), F32),
            v((block, qkv_width), F32),
            v((4, block, 2 * units), BF16),
            v((3, block, 2 * units), BF16),
            v((4, length, units), BF16),
            v((3, 2, tokens, width), BF16),
            v((3, tokens, width), BF16),
            v((3, tokens, width), BF16),
            v((tokens, width), BF16),
            v((tokens, width), BF16),
            v((6, 1, gains), F32),
            v((5, 1, gains), F32),
        ]
        + copies(64)
        + [pltpu.SemaphoreType.DMA((32,))],
        62 * MIB,
        big + small,
        8 * everyone * width * units,
        400 * 10**6,
    )


def per_device_sixteen(
    layer_input,
    doc_lengths,
    w_query,
    w_key,
    w_value,
    w_out,
    w_gate,
    w_up,
    w_down,
    gain_attn,
    gain_ffn,
    gain_query,
    gain_key,
    out_grad,
):
    outs = forward_step(
        doc_lengths,
        layer_input,
        (gain_attn, gain_ffn, gain_query, gain_key),
        out_grad,
        (w_query, w_key, w_value, w_out, w_gate, w_up, w_down),
    )
    attn_in, saved = outs[0], tuple(outs[1:10])
    residual, ffn_all, grad_all, hidden, pair, hidden_rows = outs[10:]
    residual_grad, gain_ffn_part, grad_down, res_low, pair_sent = back_step(
        pair, w_gate, w_up, residual, gain_ffn, out_grad, hidden, ffn_all, grad_all
    )
    heads_width, key_width = w_query.shape[1], w_key.shape[1]
    (
        layer_out,
        input_grad,
        grad_query,
        grad_key,
        grad_value,
        grad_out,
        grad_gate,
        grad_up,
        attn_gain,
        ffn_gain,
        head_gain,
    ) = finish_step(
        (
            res_low,
            w_out,
            w_query,
            w_key,
            w_value,
            w_down,
            attn_in,
            pair,
            ffn_all,
            hidden_rows,
            pair_sent,
        ),
        saved
        + (
            doc_lengths,
            gain_query[None, :],
            gain_key[None, :],
            gain_attn[None, :],
            layer_input,
            residual_grad,
            gain_ffn_part,
            residual,
        ),
        layer_input.shape[0],
        layer_input.shape[1],
        hidden.shape[1],
        heads_width,
        key_width,
    )
    return (
        layer_out,
        input_grad,
        grad_query,
        grad_key,
        grad_value,
        grad_out,
        grad_gate.astype(F32),
        grad_up.astype(F32),
        grad_down.astype(F32),
        attn_gain[0],
        ffn_gain[0],
        head_gain[0, :HEAD_WIDTH],
        head_gain[0, HEAD_WIDTH:],
    )


def solution(mesh):
    in_specs = (
        P(("dp", "tensor"), None),
        P("dp", None),
        P(None, "tensor"),
        P(None, "tensor"),
        P(None, "tensor"),
        P("tensor", None),
        P(None, "tensor"),
        P(None, "tensor"),
        P("tensor", None),
        P(),
        P(),
        P(),
        P(),
        P(("dp", "tensor"), None),
    )
    out_specs = (
        P(("dp", "tensor"), None),
        P(("dp", "tensor"), None),
        P("dp", "tensor"),
        P("dp", "tensor"),
        P("dp", "tensor"),
        P("tensor", "dp"),
        P("dp", "tensor"),
        P("dp", "tensor"),
        P("tensor", "dp"),
        P(),
        P(),
        P(),
        P(),
    )
    sixteen = mesh.shape["dp"] == 8 and mesh.shape["tensor"] == 4
    return jax.shard_map(
        per_device_sixteen if sixteen else per_device, mesh=mesh, in_specs=in_specs, out_specs=out_specs, check_vma=False
    )
```
